32 devices in a mesh: dp: 32 (over z, y, x, core).
Axes of the slice: x: 2, y: 2, z: 4, core: 2. Of those that a mesh axis runs over, the one named last changes fastest.
Arguments:
- tokens: bfloat16 [32768, 576], P('dp'), may hold values from -6 to 6
- cotangent: bfloat16 [32768, 576], P('dp'), may hold values from -16 to 16, as said below
- w_query: bfloat16 [331776], P('dp'), may hold values from -0.25 to 0.25
- w_key: bfloat16 [110592], P('dp'), may hold values from -0.25 to 0.25
- w_value: bfloat16 [110592], P('dp'), may hold values from -0.25 to 0.25
- w_out: bfloat16 [331776], P('dp'), may hold values from -2 to 2
- w_gate: bfloat16 [884736], P('dp'), may hold values from -0.25 to 0.25
- w_up: bfloat16 [884736], P('dp'), may hold values from -0.25 to 0.25
- w_down: bfloat16 [884736], P('dp'), may hold values from -0.15625 to 0.15625
- norm_gains: bfloat16 [2, 576], replicated, may hold values from 0.5 to 1.5
Outputs:
- output: bfloat16 [32768, 576], P('dp')
- input_grad: bfloat16 [32768, 576], P('dp')
- query_grad: float32 [331776], P('dp')
- key_grad: float32 [110592], P('dp')
- value_grad: float32 [110592], P('dp')
- out_grad: float32 [331776], P('dp')
- gate_grad: float32 [884736], P('dp')
- up_grad: float32 [884736], P('dp')
- down_grad: float32 [884736], P('dp')
- gain_grad: float32 [2, 576], replicated
The draws below stay inside these ranges and needn't reach their ends.
Inputs may be any that keep to these rules, and one draw needn't show every extreme that they name: `cotangent`: rows of one sequence share a scale; scales vary over the sequences.
All inputs are finite; a program needn't handle non-finite values.
Results may differ from the reference program's by a relative error of at most 0.013.
Values may be sent and summed in bfloat16 or wider, within the bound.
No kernel may reach another device: no remote copies, remote signals or barrier semaphores. Data moves between devices by JAX's collectives and lax.ppermute only.
A program may use at most 128 MiB of HBM per device.

```python
import jax
import jax.numpy as jnp
from jax import lax

D = 576
HEADS = 9
KV_HEADS = 3
HEAD_DIM = 64
FF = 1536
LENGTH = 1024
SEQS = 32
TOKENS = 32768


def draw_cotangent(key, part):
    key = jax.random.fold_in(key, 11)
    seq_index = jnp.arange(TOKENS) // LENGTH
    ramp = 3.0 ** (seq_index.astype(jnp.float32) / max(SEQS - 1, 1))
    base = jnp.clip(jax.random.normal(key, (TOKENS, D), jnp.float32), -4.0, 4.0)
    return (base * ramp[:, None]).astype(jnp.bfloat16)


def block_scale(rng, shape, split, least, high):
    loudness = 1.0
    for axis_at, parts in split:
        steps = jax.random.uniform(jax.random.fold_in(jax.random.fold_in(rng, 6), axis_at), (parts,), jnp.float32, least / len(split), high / len(split))
        loudness = loudness * jnp.repeat(jnp.exp(steps), shape[axis_at] // parts).reshape((-1,) + (1,) * (len(shape) - 1 - axis_at))
    return loudness


def normal_values(own_key, shape, spread, limit, cuts=(), kind=jnp.bfloat16):
    values = spread * jax.random.normal(own_key, shape, jnp.float32)
    if cuts:
        values = values * block_scale(own_key, shape, cuts, -0.22, 0.18)
    return jnp.clip(values, -limit, limit).astype(kind)


def setup_inputs(seed: int = 0) -> dict:
    keys = jax.random.split(jax.random.key(seed), 11)
    tokens = normal_values(keys[0], (TOKENS, D), 1.0, 6.0, ((0, 32),))
    cotangent = draw_cotangent(jax.random.fold_in(keys[10], 71), 0)
    w_query = normal_values(keys[2], (D * D,), D ** -0.5, 0.25, ((0, 32),))
    w_key = normal_values(keys[3], (D * KV_HEADS * HEAD_DIM,), D ** -0.5, 0.25, ((0, 32),))
    w_value = normal_values(keys[4], (D * KV_HEADS * HEAD_DIM,), D ** -0.5, 0.25, ((0, 32),))
    w_out = normal_values(keys[5], (D * D,), (max(D // 64, 1)) ** -0.5, 2.0, ((0, 32),))
    w_gate = normal_values(keys[6], (D * FF,), D ** -0.5, 0.25, ((0, 32),))
    w_up = normal_values(keys[7], (D * FF,), D ** -0.5, 0.25, ((0, 32),))
    w_down = normal_values(keys[8], (FF * D,), FF ** -0.5, 0.15625, ((0, 32),))
    norm_gains = jnp.clip(1.0 + 0.1 * jax.random.normal(keys[9], (2, D), jnp.float32), 0.5, 1.5).astype(jnp.bfloat16)
    return {"tokens": tokens, "cotangent": cotangent, "w_query": w_query, "w_key": w_key, "w_value": w_value, "w_out": w_out, "w_gate": w_gate, "w_up": w_up, "w_down": w_down, "norm_gains": norm_gains}


EPS = 1e-05
THETA = 100000.0
NEG_BIG = -1e+30

@jax.custom_vjp
def low(v):
    return lax.optimization_barrier(v.astype(jnp.bfloat16)).astype(jnp.float32)

@jax.custom_vjp
def low_back(v):
    return v

def low_keep(v):
    return (low(v), None)

def low_pass(kept, grad):
    return (grad,)

def back_keep(v):
    return (v, None)

def back_low(kept, grad):
    return (low(grad),)
low.defvjp(low_keep, low_pass)
low_back.defvjp(back_keep, back_low)

def rotary_tables(length, head_dim):
    half_dim = head_dim // 2
    frequency = THETA ** (-(jnp.arange(half_dim, dtype=jnp.float32) * 2.0 / head_dim))
    angles = jnp.arange(length, dtype=jnp.float32)[:, None] * frequency[None, :]
    return (jnp.cos(angles), jnp.sin(angles))

def rotate_heads(field, cosine, sine):
    half_dim = field.shape[-1] // 2
    first_half = field[..., :half_dim]
    second_half = field[..., half_dim:]
    cosine = cosine[:, None, :]
    sine = sine[:, None, :]
    return jnp.concatenate([first_half * cosine - second_half * sine, second_half * cosine + first_half * sine], -1)

def rms_norm(hidden, gain):
    return hidden * lax.rsqrt(lax.optimization_barrier(jnp.mean(hidden * hidden, -1, keepdims=True)) + EPS) * gain

def matmul(left, right):
    return jnp.dot(left, right, precision=lax.Precision.HIGHEST)

def layer(sequence, w_query, w_key, w_value, w_out, w_gate, w_up, w_down, norm_gains):
    group_size = HEADS // KV_HEADS
    normed_one = low(rms_norm(sequence, norm_gains[0]))
    query_lin = low_back(matmul(normed_one, w_query)).reshape(LENGTH, HEADS, HEAD_DIM)
    key_lin = low_back(matmul(normed_one, w_key)).reshape(LENGTH, KV_HEADS, HEAD_DIM)
    values = low(low_back(matmul(normed_one, w_value))).reshape(LENGTH, KV_HEADS, HEAD_DIM)
    cosine, sine = rotary_tables(LENGTH, HEAD_DIM)
    query_rot = low(rotate_heads(query_lin, cosine, sine)).reshape(LENGTH, KV_HEADS, group_size, HEAD_DIM)
    key_rot = low(rotate_heads(key_lin, cosine, sine))
    scores = jnp.einsum('qkgd,tkd->kgqt', query_rot, key_rot, precision=lax.Precision.HIGHEST)
    scores = low_back(scores * HEAD_DIM ** (-0.5))
    row_index = jnp.arange(LENGTH)[:, None]
    col_index = jnp.arange(LENGTH)[None, :]
    scores = jnp.where(row_index >= col_index, scores, NEG_BIG)
    maxima = lax.optimization_barrier(jnp.max(scores, -1, keepdims=True))
    expo = jnp.exp(scores - maxima)
    probs = expo / lax.optimization_barrier(jnp.sum(expo, -1, keepdims=True))
    mixed = jnp.einsum('kgqt,tkd->qkgd', low(probs), values, precision=lax.Precision.HIGHEST)
    mixed = low(low_back(mixed.reshape(LENGTH, HEADS * HEAD_DIM)))
    attn_out = low_back(matmul(mixed, w_out))
    middle = sequence + attn_out
    normed_two = low(rms_norm(middle, norm_gains[1]))
    gate = low_back(matmul(normed_two, w_gate))
    upward = low_back(matmul(normed_two, w_up))
    hidden = low(jax.nn.silu(gate) * upward)
    return middle + low_back(matmul(hidden, w_down))

def reference(tokens, cotangent, w_query, w_key, w_value, w_out, w_gate, w_up, w_down, norm_gains):
    seq_count = tokens.shape[0] // LENGTH
    inputs_f = (tokens.astype(jnp.float32).reshape(seq_count, LENGTH, D), w_query.astype(jnp.float32).reshape(D, D), w_key.astype(jnp.float32).reshape(D, KV_HEADS * HEAD_DIM), w_value.astype(jnp.float32).reshape(D, KV_HEADS * HEAD_DIM), w_out.astype(jnp.float32).reshape(D, D), w_gate.astype(jnp.float32).reshape(D, FF), w_up.astype(jnp.float32).reshape(D, FF), w_down.astype(jnp.float32).reshape(FF, D), norm_gains.astype(jnp.float32))

    def forward(sequences, wq_mat, wk_mat, wv_mat, wo_mat, wg_mat, wu_mat, wd_mat, gain_mat):

        def per_seq(sequence):
            return jax.checkpoint(layer)(sequence, wq_mat, wk_mat, wv_mat, wo_mat, wg_mat, wu_mat, wd_mat, gain_mat)
        return lax.map(per_seq, sequences)
    result, pullback = jax.vjp(forward, *inputs_f)
    gradients = pullback(cotangent.astype(jnp.float32).reshape(seq_count, LENGTH, D))
    return (result.reshape(-1, D).astype(jnp.bfloat16), gradients[0].reshape(-1, D).astype(jnp.bfloat16), gradients[1].reshape(-1), gradients[2].reshape(-1), gradients[3].reshape(-1), gradients[4].reshape(-1), gradients[5].reshape(-1), gradients[6].reshape(-1), gradients[7].reshape(-1), gradients[8])
```

```python
import functools

import jax
import jax.numpy as jnp
from jax import lax
from jax.experimental import pallas as pl
from jax.experimental.pallas import tpu as pltpu
from jax.sharding import PartitionSpec as P

HEADS = 9
KV_HEADS = 3
HEAD_DIM = 64
LENGTH = 1024


EPS = 1e-05
THETA = 100000.0
NEG_BIG = -1e30
LANES = 128
VMEM_LIMIT = 56 * 1024 * 1024
CORE_MASK = 1


def masks_of(devices):
    plane = tuple(2 * step for step in range(4))
    line = tuple(8 * step for step in range(devices // 8))
    return (plane, line)


def swap(field, mask, devices):
    return lax.ppermute(field, "dp", [(place, place ^ mask) for place in range(devices)])


def gather_pieces(piece, devices):
    plane, line = masks_of(devices)
    held = jnp.stack([piece] + [swap(piece, mask, devices) for mask in line[1:]])
    held = jnp.concatenate([held] + [swap(held, mask, devices) for mask in plane[1:]])
    return (held, swap(held, CORE_MASK, devices))


def tree_sum(terms):
    while len(terms) > 1:
        terms = [terms[at] + terms[at + 1] for at in range(0, len(terms), 2)]
    return terms[0]


def widen(field):
    return field.astype(jnp.float32)


def scatter_pieces(kept, sent, devices):
    plane, line = masks_of(devices)
    got = swap(sent, CORE_MASK, devices)
    block = kept.shape[0] // len(plane)
    parts = [
        (widen(kept[at * block : (at + 1) * block]) + widen(got[at * block : (at + 1) * block])).astype(jnp.bfloat16)
        for at in range(len(plane))
    ]
    arrived = [swap(part, mask, devices) for part, mask in zip(parts[1:], plane[1:])]
    parts = [
        tree_sum([widen(term[at]) for term in [parts[0]] + arrived]).astype(jnp.bfloat16)
        for at in range(len(line))
    ]
    arrived = [swap(part, mask, devices) for part, mask in zip(parts[1:], line[1:])]
    return tree_sum([widen(term) for term in [parts[0]] + arrived])


def slot_mask(core, slot, devices):
    line = devices // 8
    return core * CORE_MASK + 2 * (slot // line) + 8 * (slot % line)


def each_group(devices, step, body):
    group = 4

    def run(at, carry):
        for inner in range(group):
            body(at * group + inner, pl.multiple_of(at * group * step, 8) + inner * step)
        return carry

    lax.fori_loop(0, devices // group, run, 0)


def half_tiles(tiles):
    lane = lax.broadcasted_iota(jnp.int32, tiles[0].shape, 1)
    rolled = [pltpu.roll(tile, LANES // 2, 1) for tile in tiles]
    shifted = [
        jnp.where(lane < LANES // 2, rolled[at], rolled[at + 1]) for at in range(len(tiles) - 1)
    ]
    return shifted + [rolled[-1]]


def unpack_rows(stage, owner, start, rows, wide, target, row):
    whole = wide // LANES
    if wide % LANES == 0:
        for at in range(whole):
            target[at, pl.ds(row, rows), :] = stage[
                owner, pl.ds(start + at, rows, stride=whole), :
            ]
        return
    pairs, tiles_in = rows // 2, 2 * wide // LANES
    tiles = [stage[owner, pl.ds(start + at, pairs, stride=tiles_in), :] for at in range(tiles_in)]
    for at in range(whole):
        target[at, pl.ds(row, pairs, stride=2), :] = tiles[at]
    target[whole, pl.ds(row, pairs, stride=2), :] = tiles[whole]
    for at, tile in enumerate(half_tiles(tiles[whole:])):
        target[at, pl.ds(row + 1, pairs, stride=2), :] = tile


def pack_rows(source, row, rows, wide, stage, owner, start):
    whole = wide // LANES
    if wide % LANES == 0:
        for at in range(whole):
            stage[owner, pl.ds(start + at, rows, stride=whole), :] = source[
                at, pl.ds(row, rows), :
            ]
        return
    pairs, tiles_in = rows // 2, 2 * wide // LANES
    even = [
        source[at, pl.ds(row, pairs, stride=2), :] for at in range(whole + 1)
    ]
    odd = [
        source[at, pl.ds(row + 1, pairs, stride=2), :]
        for at in range(whole + 1)
    ]
    lane = lax.broadcasted_iota(jnp.int32, even[0].shape, 1)
    rolled = [pltpu.roll(tile, LANES // 2, 1) for tile in odd]
    tiles = even[:whole]
    tiles.append(jnp.where(lane < LANES // 2, even[whole], rolled[0]))
    for at in range(whole):
        tiles.append(jnp.where(lane < LANES // 2, rolled[at], rolled[at + 1]))
    for at in range(tiles_in):
        stage[owner, pl.ds(start + at, pairs, stride=tiles_in), :] = tiles[at]


def tile_widths(wide):
    return [min(LANES, wide - at) for at in range(0, wide, LANES)]


def load_stage(place_ref, own_ref, got_ref, stage, devices):
    place = place_ref[0]
    for core, pieces in enumerate((own_ref, got_ref)):

        def load(slot, carry, core=core, pieces=pieces):
            owner = place ^ slot_mask(core, slot, devices)
            stage[owner] = pieces[slot].astype(jnp.float32)
            return carry

        lax.fori_loop(0, devices // 2, load, 0)


def store_stage(kept_ref, sent_ref, stage, devices):
    for core, pieces in enumerate((kept_ref, sent_ref)):

        def store(slot, carry, core=core, pieces=pieces):
            pieces[slot] = stage[slot_mask(core, slot, devices)].astype(jnp.bfloat16)
            return carry

        lax.fori_loop(0, devices // 2, store, 0)


def unpack_kernel(place_ref, own_ref, got_ref, *refs, devices, shapes):
    count = len(shapes)
    outs, stage, wides = refs[:count], refs[count], refs[count + 1 :]
    load_stage(place_ref, own_ref, got_ref, stage, devices)
    start = 0
    for (rows, wide), out, target in zip(shapes, outs, wides):
        each = rows // devices
        each_group(
            devices,
            each,
            lambda owner, row, start=start, each=each, wide=wide, target=target: unpack_rows(
                stage, owner, start, each, wide, target, row
            ),
        )
        start += each * wide // LANES
        for at, width in enumerate(tile_widths(wide)):
            out[:, at * LANES : at * LANES + width] = target[at][:, :width].astype(jnp.bfloat16)


def unpack_pieces(place, pieces, shapes, devices):
    rows_in = pieces[0].shape[1]
    return pl.pallas_call(
        functools.partial(unpack_kernel, devices=devices, shapes=shapes),
        out_shape=[jax.ShapeDtypeStruct(shape, jnp.bfloat16) for shape in shapes],
        in_specs=[pl.BlockSpec(memory_space=pltpu.SMEM)] + [pl.BlockSpec(memory_space=pltpu.VMEM)] * 2,
        out_specs=[pl.BlockSpec(memory_space=pltpu.VMEM)] * len(shapes),
        scratch_shapes=[pltpu.VMEM((devices, rows_in, LANES), jnp.float32)]
        + [pltpu.VMEM((-(-wide // LANES), rows, LANES), jnp.float32) for rows, wide in shapes],
        compiler_params=pltpu.CompilerParams(vmem_limit_bytes=VMEM_LIMIT),
        name="unpack",
    )(place, *pieces)


def pack_kernel(place_ref, *refs, devices, shapes):
    count = len(shapes)
    sources, kept_ref, sent_ref, stage = refs[:count], refs[count], refs[count + 1], refs[count + 2]
    wides = refs[count + 3 :]
    place = place_ref[0]
    start = 0
    for (rows, wide), source, tiled in zip(shapes, sources, wides):
        each = rows // devices
        for at, width in enumerate(tile_widths(wide)):
            tiled[at, :, :width] = source[:, at * LANES : at * LANES + width]
        each_group(
            devices,
            each,
            lambda owner, row, start=start, each=each, wide=wide, tiled=tiled: pack_rows(
                tiled, row, each, wide, stage, place ^ owner, start
            ),
        )
        start += each * wide // LANES
    store_stage(kept_ref, sent_ref, stage, devices)


def pack_grads(place, grads, shapes, devices):
    rows_out = sum(rows * wide for rows, wide in shapes) // (devices * LANES)
    half = jax.ShapeDtypeStruct((devices // 2, rows_out, LANES), jnp.bfloat16)
    return pl.pallas_call(
        functools.partial(pack_kernel, devices=devices, shapes=shapes),
        out_shape=[half, half],
        in_specs=[pl.BlockSpec(memory_space=pltpu.SMEM)]
        + [pl.BlockSpec(memory_space=pltpu.VMEM)] * len(shapes),
        out_specs=[pl.BlockSpec(memory_space=pltpu.VMEM)] * 2,
        scratch_shapes=[pltpu.VMEM((devices, rows_out, LANES), jnp.float32)]
        + [pltpu.VMEM((-(-wide // LANES), rows, LANES), jnp.float32) for rows, wide in shapes],
        compiler_params=pltpu.CompilerParams(vmem_limit_bytes=VMEM_LIMIT),
        name="pack",
    )(place, *grads)


def rotary_tables(length, head_dim):
    half_dim = head_dim // 2
    frequency = THETA ** (-(jnp.arange(half_dim, dtype=jnp.float32) * 2.0 / head_dim))
    angles = jnp.arange(length, dtype=jnp.float32)[:, None] * frequency[None, :]
    return (jnp.cos(angles), jnp.sin(angles))


def rotate_heads(field, cosine, sine):
    half_dim = field.shape[-1] // 2
    first_half = field[..., :half_dim]
    second_half = field[..., half_dim:]
    cosine = cosine[None, :, None, :]
    sine = sine[None, :, None, :]
    return jnp.concatenate(
        [first_half * cosine - second_half * sine, second_half * cosine + first_half * sine], -1
    )


def normalize(hidden, gain):
    inv_rms = lax.rsqrt(jnp.mean(hidden * hidden, -1, keepdims=True) + EPS)
    return (hidden * inv_rms * gain, inv_rms)


def normalize_back(grad, hidden, inv_rms, gain):
    weighted = grad * gain
    cubed = inv_rms * inv_rms * inv_rms
    hidden_grad = inv_rms * weighted - hidden * cubed * jnp.mean(
        weighted * hidden, -1, keepdims=True
    )
    gain_part = jnp.sum(grad * hidden * inv_rms, 0)
    return (hidden_grad, gain_part)


def outer_prod(left, right):
    return lax.dot_general(
        left, right, (((0,), (0,)), ((), ())), preferred_element_type=jnp.float32
    )


def times_transposed(left, matrix):
    return lax.dot_general(
        left, matrix, (((1,), (1,)), ((), ())), preferred_element_type=jnp.float32
    )


def block_scores(query_blk, keys_part, q_start):
    scores = jnp.einsum(
        "sqkgd,stkd->skgqt", query_blk, keys_part, preferred_element_type=jnp.float32
    )
    scores = scores * HEAD_DIM ** (-0.5)
    row_index = q_start + jnp.arange(query_blk.shape[1])[:, None]
    col_index = jnp.arange(keys_part.shape[1])[None, :]
    return jnp.where(row_index >= col_index, scores, NEG_BIG)


def whole_rows(shapes, devices):
    return devices % 8 == 0 and all(
        rows % (2 * devices) == 0 and wide % (LANES // 2) == 0 for rows, wide in shapes
    ) and (devices & (devices - 1)) == 0


def gather_weights(shards, shapes, devices):
    if not whole_rows(shapes, devices):
        return [
            lax.all_gather(shard, "dp", axis=0, tiled=True).reshape(shape)
            for shard, shape in zip(shards, shapes)
        ]
    place = lax.axis_index("dp").astype(jnp.int32).reshape(1)
    mats = []
    for part in (slice(0, 3), slice(3, 7)):
        piece = jnp.concatenate([shard.reshape(-1, LANES) for shard in shards[part]])
        mats += unpack_pieces(place, gather_pieces(piece, devices), shapes[part], devices)
    return mats


def scatter_grads(grads, shapes, devices):
    if not whole_rows(shapes, devices):
        return [
            lax.psum_scatter(grad.reshape(-1), "dp", scatter_dimension=0, tiled=True)
            for grad in grads
        ]
    place = lax.axis_index("dp").astype(jnp.int32).reshape(1)
    sums = []
    for part in (slice(0, 4), slice(4, 7)):
        pieces = scatter_pieces(*pack_grads(place, grads[part], shapes[part], devices), devices)
        start = 0
        for rows, wide in shapes[part]:
            count = rows * wide // (devices * LANES)
            sums.append(pieces[start : start + count].reshape(-1))
            start += count
    return sums


def sum_all(field, devices):
    plane, line = masks_of(devices)
    for masks in ((0, CORE_MASK), plane, line):
        field = tree_sum([field] + [swap(field, mask, devices) for mask in masks[1:]])
    return field


def body(tokens, cotangent, w_query, w_key, w_value, w_out, w_gate, w_up, w_down, norm_gains):
    model_width = tokens.shape[1]
    seq_count = tokens.shape[0] // LENGTH
    group_size = HEADS // KV_HEADS
    block_rows = min(512, LENGTH)
    scale_factor = HEAD_DIM ** (-0.5)
    gain_f = norm_gains.astype(jnp.float32)
    shards = (w_query, w_key, w_value, w_out, w_gate, w_up, w_down)
    devices = lax.axis_size("dp")
    widths = [shards[at].shape[0] * devices // model_width for at in range(6)]
    shapes = [(model_width, wide) for wide in widths] + [
        (shards[6].shape[0] * devices // model_width, model_width)
    ]
    wq_mat, wk_mat, wv_mat, wo_mat, wg_mat, wu_mat, wd_mat = gather_weights(shards, shapes, devices)
    resid_in = tokens.astype(jnp.float32)
    normed_one, rms_one = normalize(resid_in, gain_f[0])
    normed_one = normed_one.astype(jnp.bfloat16)
    query_lin = jnp.dot(normed_one, wq_mat, preferred_element_type=jnp.float32)
    key_lin = jnp.dot(normed_one, wk_mat, preferred_element_type=jnp.float32)
    value_lin = jnp.dot(normed_one, wv_mat, preferred_element_type=jnp.float32)
    cosine, sine = rotary_tables(LENGTH, HEAD_DIM)
    query_rot = rotate_heads(
        query_lin.reshape(seq_count, LENGTH, HEADS, HEAD_DIM), cosine, sine
    ).astype(jnp.bfloat16)
    query_rot = query_rot.reshape(seq_count, LENGTH, KV_HEADS, group_size, HEAD_DIM)
    key_rot = rotate_heads(
        key_lin.reshape(seq_count, LENGTH, KV_HEADS, HEAD_DIM), cosine, sine
    ).astype(jnp.bfloat16)
    values = value_lin.astype(jnp.bfloat16).reshape(seq_count, LENGTH, KV_HEADS, HEAD_DIM)
    mixed_blocks = []
    total_blocks = []
    for index in range(LENGTH // block_rows):
        q_start = index * block_rows
        key_end = q_start + block_rows
        scores = block_scores(query_rot[:, q_start:key_end], key_rot[:, :key_end], q_start)
        maxima = jnp.max(scores, -1, keepdims=True)
        expo = jnp.exp(scores - maxima)
        totals = jnp.sum(expo, -1, keepdims=True)
        probs = (expo / totals).astype(jnp.bfloat16)
        mixed_blocks.append(
            jnp.einsum(
                "skgqt,stkd->sqkgd", probs, values[:, :key_end], preferred_element_type=jnp.float32
            )
        )
        total_blocks.append((maxima + jnp.log(totals))[..., 0])
    mixed = (
        jnp.concatenate(mixed_blocks, 1)
        .reshape(seq_count * LENGTH, model_width)
        .astype(jnp.bfloat16)
    )
    attn_out = jnp.dot(mixed, wo_mat, preferred_element_type=jnp.float32)
    middle = resid_in + attn_out
    normed_two, rms_two = normalize(middle, gain_f[1])
    normed_two = normed_two.astype(jnp.bfloat16)
    gate = jnp.dot(normed_two, wg_mat, preferred_element_type=jnp.float32)
    upward = jnp.dot(normed_two, wu_mat, preferred_element_type=jnp.float32)
    sigmoid_g = jax.nn.sigmoid(gate)
    activated = gate * sigmoid_g
    hidden = (activated * upward).astype(jnp.bfloat16)
    ffn_out = jnp.dot(hidden, wd_mat, preferred_element_type=jnp.float32)
    output = (middle + ffn_out).astype(jnp.bfloat16)
    grad_down = outer_prod(hidden, cotangent)
    hidden_back = times_transposed(cotangent, wd_mat)
    gate_back = (hidden_back * upward * sigmoid_g * (1.0 + gate * (1.0 - sigmoid_g))).astype(
        jnp.bfloat16
    )
    up_back = (hidden_back * activated).astype(jnp.bfloat16)
    grad_gate = outer_prod(normed_two, gate_back)
    grad_up = outer_prod(normed_two, up_back)
    two_back = times_transposed(gate_back, wg_mat) + times_transposed(up_back, wu_mat)
    norm_two_back, gain_two = normalize_back(two_back, middle, rms_two, gain_f[1])
    mid_back = cotangent.astype(jnp.float32) + norm_two_back
    mid_low = mid_back.astype(jnp.bfloat16)
    grad_out = outer_prod(mixed, mid_low)
    mixed_back = times_transposed(mid_low, wo_mat).astype(jnp.bfloat16)
    mixed_back = mixed_back.reshape(seq_count, LENGTH, KV_HEADS, group_size, HEAD_DIM)
    query_parts = []
    key_acc = jnp.zeros((seq_count, LENGTH, KV_HEADS, HEAD_DIM), jnp.float32)
    value_acc = jnp.zeros((seq_count, LENGTH, KV_HEADS, HEAD_DIM), jnp.float32)
    for index in range(LENGTH // block_rows):
        q_start = index * block_rows
        key_end = q_start + block_rows
        query_blk = query_rot[:, q_start:key_end]
        keys_part = key_rot[:, :key_end]
        values_part = values[:, :key_end]
        back_blk = mixed_back[:, q_start:key_end]
        scores = block_scores(query_blk, keys_part, q_start)
        probs = jnp.exp(scores - total_blocks[index][..., None])
        prob_back = jnp.einsum(
            "sqkgd,stkd->skgqt", back_blk, values_part, preferred_element_type=jnp.float32
        )
        centred = prob_back - jnp.sum(probs * prob_back, -1, keepdims=True)
        score_back = (probs * centred).astype(jnp.bfloat16)
        query_parts.append(
            jnp.einsum(
                "skgqt,stkd->sqkgd", score_back, keys_part, preferred_element_type=jnp.float32
            )
            * scale_factor
        )
        key_part = (
            jnp.einsum(
                "skgqt,sqkgd->stkd", score_back, query_blk, preferred_element_type=jnp.float32
            )
            * scale_factor
        )
        value_part = jnp.einsum(
            "skgqt,sqkgd->stkd",
            probs.astype(jnp.bfloat16),
            back_blk,
            preferred_element_type=jnp.float32,
        )
        padding = ((0, 0), (0, LENGTH - key_end), (0, 0), (0, 0))
        key_acc = key_acc + jnp.pad(key_part, padding)
        value_acc = value_acc + jnp.pad(value_part, padding)
    rot_query_back = jnp.concatenate(query_parts, 1).reshape(seq_count, LENGTH, HEADS, HEAD_DIM)
    query_back = (
        rotate_heads(rot_query_back, cosine, -sine)
        .reshape(seq_count * LENGTH, model_width)
        .astype(jnp.bfloat16)
    )
    key_back = (
        rotate_heads(key_acc, cosine, -sine).reshape(seq_count * LENGTH, -1).astype(jnp.bfloat16)
    )
    value_back = value_acc.reshape(seq_count * LENGTH, -1).astype(jnp.bfloat16)
    grad_query = outer_prod(normed_one, query_back)
    grad_key = outer_prod(normed_one, key_back)
    grad_value = outer_prod(normed_one, value_back)
    one_back = (
        times_transposed(query_back, wq_mat)
        + times_transposed(key_back, wk_mat)
        + times_transposed(value_back, wv_mat)
    )
    norm_one_back, gain_one = normalize_back(one_back, resid_in, rms_one, gain_f[0])
    input_grad = (mid_back + norm_one_back).astype(jnp.bfloat16)
    grads = (grad_query, grad_key, grad_value, grad_out, grad_gate, grad_up, grad_down)
    all_parts = scatter_grads(grads, shapes, devices)
    gain_grad = sum_all(jnp.stack([gain_one, gain_two]), devices)
    return (output, input_grad) + tuple(all_parts) + (gain_grad,)


def solution(mesh):
    return jax.shard_map(
        body,
        mesh=mesh,
        in_specs=(
            P("dp", None),
            P("dp", None),
            P("dp"),
            P("dp"),
            P("dp"),
            P("dp"),
            P("dp"),
            P("dp"),
            P("dp"),
            P(),
        ),
        out_specs=(
            P("dp", None),
            P("dp", None),
            P("dp"),
            P("dp"),
            P("dp"),
            P("dp"),
            P("dp"),
            P("dp"),
            P("dp"),
            P(),
        ),
        check_vma=False,
    )
```

```python
import functools

import jax
import jax.numpy as jnp
from jax import lax
from jax.experimental import pallas as pl
from jax.experimental.pallas import tpu as pltpu
from jax.sharding import PartitionSpec as P

HEADS = 9
KV_HEADS = 3
HEAD_DIM = 64
LENGTH = 1024


EPS = 1e-05
THETA = 100000.0
NEG_BIG = -1e30
LANES = 128
VMEM_LIMIT = 56 * 1024 * 1024
CORE_MASK = 1


def masks_of(devices):
    plane = tuple(2 * step for step in range(4))
    line = tuple(8 * step for step in range(devices // 8))
    return (plane, line)


def swap(field, mask, devices):
    return lax.ppermute(field, "dp", [(place, place ^ mask) for place in range(devices)])


def tree_sum(terms):
    while len(terms) > 1:
        terms = [terms[at] + terms[at + 1] for at in range(0, len(terms), 2)]
    return terms[0]


def widen(field):
    return field.astype(jnp.float32)


def slot_mask(core, slot, devices):
    line = devices // 8
    return core * CORE_MASK + 2 * (slot // line) + 8 * (slot % line)


def each_group(devices, step, body):
    group = 4

    def run(at, carry):
        for inner in range(group):
            body(at * group + inner, pl.multiple_of(at * group * step, 8) + inner * step)
        return carry

    lax.fori_loop(0, devices // group, run, 0)


def half_tiles(tiles):
    lane = lax.broadcasted_iota(jnp.int32, tiles[0].shape, 1)
    rolled = [pltpu.roll(tile, LANES // 2, 1) for tile in tiles]
    shifted = [
        jnp.where(lane < LANES // 2, rolled[at], rolled[at + 1]) for at in range(len(tiles) - 1)
    ]
    return shifted + [rolled[-1]]


def unpack_rows(stage, owner, start, rows, wide, target, row):
    whole = wide // LANES
    if wide % LANES == 0:
        for at in range(whole):
            target[at, pl.ds(row, rows), :] = stage[
                owner, pl.ds(start + at, rows, stride=whole), :
            ]
        return
    pairs, tiles_in = rows // 2, 2 * wide // LANES
    tiles = [stage[owner, pl.ds(start + at, pairs, stride=tiles_in), :] for at in range(tiles_in)]
    for at in range(whole):
        target[at, pl.ds(row, pairs, stride=2), :] = tiles[at]
    target[whole, pl.ds(row, pairs, stride=2), :] = tiles[whole]
    for at, tile in enumerate(half_tiles(tiles[whole:])):
        target[at, pl.ds(row + 1, pairs, stride=2), :] = tile


def pack_rows(source, row, rows, wide, stage, owner, start):
    whole = wide // LANES
    if wide % LANES == 0:
        for at in range(whole):
            stage[owner, pl.ds(start + at, rows, stride=whole), :] = source[
                at, pl.ds(row, rows), :
            ]
        return
    pairs, tiles_in = rows // 2, 2 * wide // LANES
    even = [
        source[at, pl.ds(row, pairs, stride=2), :] for at in range(whole + 1)
    ]
    odd = [
        source[at, pl.ds(row + 1, pairs, stride=2), :]
        for at in range(whole + 1)
    ]
    lane = lax.broadcasted_iota(jnp.int32, even[0].shape, 1)
    rolled = [pltpu.roll(tile, LANES // 2, 1) for tile in odd]
    tiles = even[:whole]
    tiles.append(jnp.where(lane < LANES // 2, even[whole], rolled[0]))
    for at in range(whole):
        tiles.append(jnp.where(lane < LANES // 2, rolled[at], rolled[at + 1]))
    for at in range(tiles_in):
        stage[owner, pl.ds(start + at, pairs, stride=tiles_in), :] = tiles[at]


def tile_widths(wide):
    return [min(LANES, wide - at) for at in range(0, wide, LANES)]


def load_stage(place_ref, own_ref, got_ref, stage, devices):
    place = place_ref[0]
    for core, pieces in enumerate((own_ref, got_ref)):

        def load(slot, carry, core=core, pieces=pieces):
            owner = place ^ slot_mask(core, slot, devices)
            stage[owner] = pieces[slot].astype(jnp.float32)
            return carry

        lax.fori_loop(0, devices // 2, load, 0)


def store_stage(kept_ref, sent_ref, stage, devices):
    for core, pieces in enumerate((kept_ref, sent_ref)):

        def store(slot, carry, core=core, pieces=pieces):
            pieces[slot] = stage[slot_mask(core, slot, devices)].astype(jnp.bfloat16)
            return carry

        lax.fori_loop(0, devices // 2, store, 0)


def unpack_kernel(place_ref, own_ref, got_ref, *refs, devices, shapes):
    count = len(shapes)
    outs, stage, wides = refs[:count], refs[count], refs[count + 1 :]
    load_stage(place_ref, own_ref, got_ref, stage, devices)
    start = 0
    for (rows, wide), out, target in zip(shapes, outs, wides):
        each = rows // devices
        each_group(
            devices,
            each,
            lambda owner, row, start=start, each=each, wide=wide, target=target: unpack_rows(
                stage, owner, start, each, wide, target, row
            ),
        )
        start += each * wide // LANES
        for at, width in enumerate(tile_widths(wide)):
            out[:, at * LANES : at * LANES + width] = target[at][:, :width].astype(jnp.bfloat16)


def unpack_pieces(place, pieces, shapes, devices):
    rows_in = pieces[0].shape[1]
    return pl.pallas_call(
        functools.partial(unpack_kernel, devices=devices, shapes=shapes),
        out_shape=[jax.ShapeDtypeStruct(shape, jnp.bfloat16) for shape in shapes],
        in_specs=[pl.BlockSpec(memory_space=pltpu.SMEM)] + [pl.BlockSpec(memory_space=pltpu.VMEM)] * 2,
        out_specs=[pl.BlockSpec(memory_space=pltpu.VMEM)] * len(shapes),
        scratch_shapes=[pltpu.VMEM((devices, rows_in, LANES), jnp.float32)]
        + [pltpu.VMEM((-(-wide // LANES), rows, LANES), jnp.float32) for rows, wide in shapes],
        compiler_params=pltpu.CompilerParams(vmem_limit_bytes=VMEM_LIMIT),
        name="unpack",
    )(place, *pieces)


def pack_kernel(place_ref, *refs, devices, shapes):
    count = len(shapes)
    sources, kept_ref, sent_ref, stage = refs[:count], refs[count], refs[count + 1], refs[count + 2]
    wides = refs[count + 3 :]
    place = place_ref[0]
    start = 0
    for (rows, wide), source, tiled in zip(shapes, sources, wides):
        each = rows // devices
        for at, width in enumerate(tile_widths(wide)):
            tiled[at, :, :width] = source[:, at * LANES : at * LANES + width]
        each_group(
            devices,
            each,
            lambda owner, row, start=start, each=each, wide=wide, tiled=tiled: pack_rows(
                tiled, row, each, wide, stage, place ^ owner, start
            ),
        )
        start += each * wide // LANES
    store_stage(kept_ref, sent_ref, stage, devices)


def pack_grads(place, grads, shapes, devices):
    rows_out = sum(rows * wide for rows, wide in shapes) // (devices * LANES)
    half = jax.ShapeDtypeStruct((devices // 2, rows_out, LANES), jnp.bfloat16)
    return pl.pallas_call(
        functools.partial(pack_kernel, devices=devices, shapes=shapes),
        out_shape=[half, half],
        in_specs=[pl.BlockSpec(memory_space=pltpu.SMEM)]
        + [pl.BlockSpec(memory_space=pltpu.VMEM)] * len(shapes),
        out_specs=[pl.BlockSpec(memory_space=pltpu.VMEM)] * 2,
        scratch_shapes=[pltpu.VMEM((devices, rows_out, LANES), jnp.float32)]
        + [pltpu.VMEM((-(-wide // LANES), rows, LANES), jnp.float32) for rows, wide in shapes],
        compiler_params=pltpu.CompilerParams(vmem_limit_bytes=VMEM_LIMIT),
        name="pack",
    )(place, *grads)


BLOCK = 256


def dot_nt(left, right):
    return lax.dot_general(
        left, right, (((1,), (1,)), ((), ())), preferred_element_type=jnp.float32
    )


def dot_tn(left, right):
    return lax.dot_general(
        left, right, (((0,), (0,)), ((), ())), preferred_element_type=jnp.float32
    )


def dot_nn(left, right):
    return jnp.dot(left, right, preferred_element_type=jnp.float32)


def attend_kernel(query_ref, keys_ref, values_ref, mixed_ref, total_ref, *, head, group):
    length = query_ref.shape[0]
    keys = keys_ref[:, head * HEAD_DIM : (head + 1) * HEAD_DIM]
    values = values_ref[:, head * HEAD_DIM : (head + 1) * HEAD_DIM]
    lower = lax.broadcasted_iota(jnp.int32, (BLOCK, BLOCK), 0) >= lax.broadcasted_iota(
        jnp.int32, (BLOCK, BLOCK), 1
    )
    lane = lax.broadcasted_iota(jnp.int32, (BLOCK, LANES), 1)
    for start in range(0, length, BLOCK):
        mixed, totals_row = [], jnp.zeros((BLOCK, LANES), jnp.float32)
        for member in range(group):
            at = (head * group + member) * HEAD_DIM
            query = query_ref[start : start + BLOCK, at : at + HEAD_DIM]
            diagonal = jnp.where(lower, dot_nt(query, keys[start : start + BLOCK]), NEG_BIG)
            maxima = jnp.max(diagonal, 1, keepdims=True)
            if start:
                before = dot_nt(query, keys[:start])
                maxima = jnp.maximum(maxima, jnp.max(before, 1, keepdims=True))
            expo = jnp.exp(diagonal - maxima)
            totals = jnp.sum(expo, 1, keepdims=True)
            result = dot_nn(expo.astype(jnp.bfloat16), values[start : start + BLOCK])
            if start:
                expo = jnp.exp(before - maxima)
                totals = totals + jnp.sum(expo, 1, keepdims=True)
                result = result + dot_nn(expo.astype(jnp.bfloat16), values[:start])
            mixed.append(result / totals)
            totals_row = jnp.where(lane == member, maxima + jnp.log(totals), totals_row)
        mixed_ref[start : start + BLOCK, :] = jnp.concatenate(mixed, 1).astype(jnp.bfloat16)
        total_ref[start : start + BLOCK, :] = totals_row


def attend(query, keys, values, head, group):
    length = query.shape[0]
    return pl.pallas_call(
        functools.partial(attend_kernel, head=head, group=group),
        out_shape=[
            jax.ShapeDtypeStruct((length, group * HEAD_DIM), jnp.bfloat16),
            jax.ShapeDtypeStruct((length, LANES), jnp.float32),
        ],
        in_specs=[pl.BlockSpec(memory_space=pltpu.VMEM)] * 3,
        out_specs=[pl.BlockSpec(memory_space=pltpu.VMEM)] * 2,
        compiler_params=pltpu.CompilerParams(vmem_limit_bytes=VMEM_LIMIT),
        cost_estimate=pl.CostEstimate(
            flops=12 * 10**9, bytes_accessed=4 * 10**6, transcendentals=2 * 10**6
        ),
        name="attend",
    )(query, keys, values)


def attend_back_kernel(
    query_ref, keys_ref, values_ref, back_ref, mixed_ref, total_ref,
    query_back_ref, key_back_ref, queries, backs, totals, deltas, query_sum, key_sum, value_sum,
    *, head, group,
):
    length = query_ref.shape[0]
    ones = jnp.ones((8, HEAD_DIM), jnp.float32)
    totals[...] = total_ref[...].T[:8]
    for member in range(group):
        at = (head * group + member) * HEAD_DIM
        queries[member] = query_ref[:, at : at + HEAD_DIM]
        back = back_ref[:, at : at + HEAD_DIM]
        backs[member] = back
        product = back.astype(jnp.float32) * mixed_ref[
            :, member * HEAD_DIM : (member + 1) * HEAD_DIM
        ].astype(jnp.float32)
        deltas[member] = lax.dot_general(
            ones, product, (((1,), (1,)), ((), ())),
            precision=lax.Precision.HIGHEST, preferred_element_type=jnp.float32,
        )
    keys_all = keys_ref[:, head * HEAD_DIM : (head + 1) * HEAD_DIM]
    values_all = values_ref[:, head * HEAD_DIM : (head + 1) * HEAD_DIM]
    upper = lax.broadcasted_iota(jnp.int32, (BLOCK, BLOCK), 0) <= lax.broadcasted_iota(
        jnp.int32, (BLOCK, BLOCK), 1
    )
    for member in range(group):
        total_row = totals[member : member + 1, :]
        delta_row = deltas[member][0:1]
        for start in range(0, length, BLOCK):
            keys = keys_all[start : start + BLOCK]
            values = values_all[start : start + BLOCK]
            query = queries[member, start:, :]
            back = backs[member, start:, :]
            scores = dot_nt(keys, query)
            probs = jnp.exp(scores - total_row[:, start:])
            first = jnp.where(upper, probs[:, :BLOCK], 0.0)
            probs = first if start + BLOCK == length else jnp.concatenate(
                [first, probs[:, BLOCK:]], 1
            )
            prob_back = dot_nt(values, back)
            score_back = (probs * (prob_back - delta_row[:, start:])).astype(jnp.bfloat16)
            value_part = dot_nn(probs.astype(jnp.bfloat16), back)
            key_part = dot_nn(score_back, query)
            query_part = dot_tn(score_back, keys)
            if member:
                key_sum[start : start + BLOCK, :] += key_part
                value_sum[start : start + BLOCK, :] += value_part
            else:
                key_sum[start : start + BLOCK, :] = key_part
                value_sum[start : start + BLOCK, :] = value_part
            if start:
                query_sum[member, start:, :] += query_part
            else:
                query_sum[member] = query_part
    query_back_ref[...] = (
        jnp.concatenate([query_sum[member] for member in range(group)], 1) * HEAD_DIM ** (-0.5)
    )
    key_back_ref[...] = jnp.concatenate([key_sum[...], value_sum[...]], 1)


def attend_back(query, keys, values, back, mixed, total, head, group):
    length = query.shape[0]
    return pl.pallas_call(
        functools.partial(attend_back_kernel, head=head, group=group),
        out_shape=[
            jax.ShapeDtypeStruct((length, group * HEAD_DIM), jnp.float32),
            jax.ShapeDtypeStruct((length, 2 * HEAD_DIM), jnp.float32),
        ],
        in_specs=[pl.BlockSpec(memory_space=pltpu.VMEM)] * 6,
        out_specs=[pl.BlockSpec(memory_space=pltpu.VMEM)] * 2,
        scratch_shapes=[
            pltpu.VMEM((group, length, HEAD_DIM), jnp.bfloat16),
            pltpu.VMEM((group, length, HEAD_DIM), jnp.bfloat16),
            pltpu.VMEM((8, length), jnp.float32),
            pltpu.VMEM((group, 8, length), jnp.float32),
            pltpu.VMEM((group, length, HEAD_DIM), jnp.float32),
            pltpu.VMEM((length, HEAD_DIM), jnp.float32),
            pltpu.VMEM((length, HEAD_DIM), jnp.float32),
        ],
        compiler_params=pltpu.CompilerParams(vmem_limit_bytes=VMEM_LIMIT),
        cost_estimate=pl.CostEstimate(
            flops=24 * 10**9, bytes_accessed=8 * 10**6, transcendentals=2 * 10**6
        ),
        name="attend_back",
    )(query, keys, values, back, mixed, total)


def rotary_tables(length, head_dim):
    half_dim = head_dim // 2
    frequency = THETA ** (-(jnp.arange(half_dim, dtype=jnp.float32) * 2.0 / head_dim))
    angles = jnp.arange(length, dtype=jnp.float32)[:, None] * frequency[None, :]
    return (jnp.cos(angles), jnp.sin(angles))


def rotate_heads(field, cosine, sine):
    half_dim = field.shape[-1] // 2
    first_half = field[..., :half_dim]
    second_half = field[..., half_dim:]
    cosine = cosine[None, :, None, :]
    sine = sine[None, :, None, :]
    return jnp.concatenate(
        [first_half * cosine - second_half * sine, second_half * cosine + first_half * sine], -1
    )


def normalize(hidden, gain):
    inv_rms = lax.rsqrt(jnp.mean(hidden * hidden, -1, keepdims=True) + EPS)
    return (hidden * inv_rms * gain, inv_rms)


def normalize_back(grad, hidden, inv_rms, gain):
    weighted = grad * gain
    cubed = inv_rms * inv_rms * inv_rms
    hidden_grad = inv_rms * weighted - hidden * cubed * jnp.mean(
        weighted * hidden, -1, keepdims=True
    )
    gain_part = jnp.sum(grad * hidden * inv_rms, 0)
    return (hidden_grad, gain_part)


def outer_prod(left, right):
    return lax.dot_general(
        left, right, (((0,), (0,)), ((), ())), preferred_element_type=jnp.float32
    )


def times_transposed(left, matrix):
    return lax.dot_general(
        left, matrix, (((1,), (1,)), ((), ())), preferred_element_type=jnp.float32
    )


def whole_rows(shapes, devices):
    return (devices & (devices - 1)) == 0 and all(
        rows % (8 * devices // 4) == 0 and rows * wide % (devices * LANES) == 0
        for rows, wide in shapes
    )


def place_of():
    return lax.axis_index("dp").astype(jnp.int32).reshape(1)


class WeightGather:
    def __init__(self, shards, shapes, devices):
        self.shards, self.shapes, self.devices = shards, shapes, devices
        self.stages = whole_rows(shapes, devices)
        if self.stages:
            self.held = jnp.concatenate([shard.reshape(-1, LANES) for shard in shards])

    def line_stage(self, other):
        if not self.stages:
            return other
        _, line = masks_of(self.devices)
        self.held, other = tied(self.held, other)
        self.arrived = [self.held] + [swap(self.held, mask, self.devices) for mask in line[1:]]
        return other

    def plane_stage(self, other):
        if not self.stages:
            return other
        plane, _ = masks_of(self.devices)
        self.held, other = tied(jnp.stack(self.arrived), other)
        self.arrived = [self.held] + [swap(self.held, mask, self.devices) for mask in plane[1:]]
        return other

    def core_stage(self, other):
        if not self.stages:
            return other
        self.arrived, other = tied(self.arrived, other)
        self.held = jnp.concatenate(self.arrived)
        self.got = swap(self.held, CORE_MASK, self.devices)
        return other

    def result(self):
        if not self.stages:
            return [
                lax.all_gather(shard, "dp", axis=0, tiled=True).reshape(shape)
                for shard, shape in zip(self.shards, self.shapes)
            ]
        return unpack_pieces(place_of(), (self.held, self.got), self.shapes, self.devices)


def sum_all(field, devices):
    step = 1
    while step < devices:
        field = field + swap(field, step, devices)
        step *= 2
    return field


def tied(first, second):
    return lax.optimization_barrier((first, second))


class GradSum:
    def __init__(self, grads, shapes, devices):
        self.grads, self.shapes, self.devices = grads, shapes, devices
        self.stages = whole_rows(shapes, devices)
        if self.stages:
            self.kept, self.sent = pack_grads(place_of(), grads, shapes, devices)

    def core_stage(self, other):
        if not self.stages:
            return other
        (self.kept, self.sent), other = tied((self.kept, self.sent), other)
        self.got = swap(self.sent, CORE_MASK, self.devices)
        return other

    def plane_stage(self, other):
        if not self.stages:
            return other
        plane, _ = masks_of(self.devices)
        block = self.kept.shape[0] // len(plane)
        cuts = [slice(at * block, (at + 1) * block) for at in range(len(plane))]
        parts = [(widen(self.kept[cut]) + widen(self.got[cut])).astype(jnp.bfloat16) for cut in cuts]
        self.parts, other = tied(parts, other)
        self.arrived = [
            swap(part, mask, self.devices) for part, mask in zip(self.parts[1:], plane[1:])
        ]
        return other

    def line_stage(self, other):
        if not self.stages:
            return other
        _, line = masks_of(self.devices)
        terms = [self.parts[0]] + self.arrived
        parts = [
            tree_sum([widen(term[at]) for term in terms]).astype(jnp.bfloat16)
            for at in range(len(line))
        ]
        self.parts, other = tied(parts, other)
        self.arrived = [
            swap(part, mask, self.devices) for part, mask in zip(self.parts[1:], line[1:])
        ]
        return other

    def result(self):
        if not self.stages:
            return [
                lax.psum_scatter(grad.reshape(-1), "dp", scatter_dimension=0, tiled=True)
                for grad in self.grads
            ]
        pieces = tree_sum([widen(term) for term in [self.parts[0]] + self.arrived])
        sums, start = [], 0
        for rows, wide in self.shapes:
            count = rows * wide // (self.devices * LANES)
            sums.append(pieces[start : start + count].reshape(-1))
            start += count
        return sums


def body(tokens, cotangent, w_query, w_key, w_value, w_out, w_gate, w_up, w_down, norm_gains):
    model_width = tokens.shape[1]
    seq_count = tokens.shape[0] // LENGTH
    group_size = HEADS // KV_HEADS
    scale_factor = HEAD_DIM ** (-0.5)
    gain_f = norm_gains.astype(jnp.float32)
    shards = (w_query, w_key, w_value, w_out, w_gate, w_up, w_down)
    devices = lax.axis_size("dp")
    widths = [shards[at].shape[0] * devices // model_width for at in range(6)]
    shapes = [(model_width, wide) for wide in widths] + [
        (shards[6].shape[0] * devices // model_width, model_width)
    ]
    first = WeightGather(shards[:3], shapes[:3], devices)
    second = WeightGather(shards[3:], shapes[3:], devices)
    tokens = first.line_stage(tokens)
    tokens = first.plane_stage(tokens)
    tokens = second.line_stage(tokens)
    tokens = first.core_stage(tokens)
    wq_mat, wk_mat, wv_mat = first.result()
    resid_in = tokens.astype(jnp.float32)
    normed_one, rms_one = normalize(resid_in, gain_f[0])
    normed_one = normed_one.astype(jnp.bfloat16)
    query_lin = jnp.dot(normed_one, wq_mat, preferred_element_type=jnp.float32)
    key_lin = jnp.dot(normed_one, wk_mat, preferred_element_type=jnp.float32)
    value_lin = jnp.dot(normed_one, wv_mat, preferred_element_type=jnp.float32)
    cosine, sine = rotary_tables(LENGTH, HEAD_DIM)
    tokens_here = seq_count * LENGTH
    query_rot = rotate_heads(
        query_lin.reshape(seq_count, LENGTH, HEADS, HEAD_DIM), cosine, sine
    ).reshape(tokens_here, -1)
    query_rot = (query_rot.astype(jnp.bfloat16).astype(jnp.float32) * scale_factor).astype(
        jnp.bfloat16
    )
    key_rot = (
        rotate_heads(key_lin.reshape(seq_count, LENGTH, KV_HEADS, HEAD_DIM), cosine, sine)
        .reshape(tokens_here, -1)
        .astype(jnp.bfloat16)
    )
    values = value_lin.astype(jnp.bfloat16)
    values = second.plane_stage(values)
    attended = [attend(query_rot, key_rot, values, head, group_size) for head in range(2)]
    values, attended = second.core_stage((values, attended))
    attended.append(attend(query_rot, key_rot, values, 2, group_size))
    wo_mat, wg_mat, wu_mat, wd_mat = second.result()
    mixed = jnp.concatenate([part for part, _ in attended], 1)
    attn_out = jnp.dot(mixed, wo_mat, preferred_element_type=jnp.float32)
    middle = resid_in + attn_out
    normed_two, rms_two = normalize(middle, gain_f[1])
    normed_two = normed_two.astype(jnp.bfloat16)
    gate = jnp.dot(normed_two, wg_mat, preferred_element_type=jnp.float32)
    upward = jnp.dot(normed_two, wu_mat, preferred_element_type=jnp.float32)
    sigmoid_g = jax.nn.sigmoid(gate)
    activated = gate * sigmoid_g
    hidden = (activated * upward).astype(jnp.bfloat16)
    ffn_out = jnp.dot(hidden, wd_mat, preferred_element_type=jnp.float32)
    output = (middle + ffn_out).astype(jnp.bfloat16)
    grad_down = outer_prod(hidden, cotangent)
    hidden_back = times_transposed(cotangent, wd_mat)
    gate_back = (hidden_back * upward * sigmoid_g * (1.0 + gate * (1.0 - sigmoid_g))).astype(
        jnp.bfloat16
    )
    up_back = (hidden_back * activated).astype(jnp.bfloat16)
    grad_gate = outer_prod(normed_two, gate_back)
    grad_up = outer_prod(normed_two, up_back)
    two_back = times_transposed(gate_back, wg_mat) + times_transposed(up_back, wu_mat)
    norm_two_back, gain_two = normalize_back(two_back, middle, rms_two, gain_f[1])
    mid_back = cotangent.astype(jnp.float32) + norm_two_back
    mid_low = mid_back.astype(jnp.bfloat16)
    grad_out = outer_prod(mixed, mid_low)
    mixed_back = times_transposed(mid_low, wo_mat).astype(jnp.bfloat16)
    feed_sum = GradSum((grad_gate, grad_up, grad_down), shapes[4:], devices)

    def back_of(head, field):
        part, total = attended[head]
        return attend_back(query_rot, key_rot, values, field, part, total, head, group_size)

    mixed_back = feed_sum.core_stage(mixed_back)
    backs = [back_of(0, mixed_back)]
    mixed_back, _ = tied(mixed_back, backs[0])
    mixed_back = feed_sum.plane_stage(mixed_back)
    backs += [back_of(head, mixed_back) for head in range(1, KV_HEADS)]
    backs = feed_sum.line_stage(backs)
    rot_query_back = jnp.concatenate([back for back, _ in backs], 1).reshape(
        seq_count, LENGTH, HEADS, HEAD_DIM
    )
    key_acc = jnp.concatenate([back[:, :HEAD_DIM] for _, back in backs], 1).reshape(
        seq_count, LENGTH, KV_HEADS, HEAD_DIM
    )
    value_acc = jnp.concatenate([back[:, HEAD_DIM:] for _, back in backs], 1)
    query_back = (
        rotate_heads(rot_query_back, cosine, -sine)
        .reshape(seq_count * LENGTH, model_width)
        .astype(jnp.bfloat16)
    )
    key_back = (
        rotate_heads(key_acc, cosine, -sine).reshape(seq_count * LENGTH, -1).astype(jnp.bfloat16)
    )
    value_back = value_acc.reshape(seq_count * LENGTH, -1).astype(jnp.bfloat16)
    grad_query = outer_prod(normed_one, query_back)
    grad_key = outer_prod(normed_one, key_back)
    grad_value = outer_prod(normed_one, value_back)
    one_back = (
        times_transposed(query_back, wq_mat)
        + times_transposed(key_back, wk_mat)
        + times_transposed(value_back, wv_mat)
    )
    norm_one_back, gain_one = normalize_back(one_back, resid_in, rms_one, gain_f[0])
    input_grad = (mid_back + norm_one_back).astype(jnp.bfloat16)
    mix_sum = GradSum((grad_query, grad_key, grad_value, grad_out), shapes[:4], devices)
    input_grad = mix_sum.core_stage(input_grad)
    input_grad = mix_sum.plane_stage(input_grad)
    input_grad = mix_sum.line_stage(input_grad)
    all_parts = mix_sum.result() + feed_sum.result()
    gain_grad = sum_all(jnp.stack([gain_one, gain_two]), devices)
    return (output, input_grad) + tuple(all_parts) + (gain_grad,)


def solution(mesh):
    return jax.shard_map(
        body,
        mesh=mesh,
        in_specs=(
            P("dp", None),
            P("dp", None),
            P("dp"),
            P("dp"),
            P("dp"),
            P("dp"),
            P("dp"),
            P("dp"),
            P("dp"),
            P(),
        ),
        out_specs=(
            P("dp", None),
            P("dp", None),
            P("dp"),
            P("dp"),
            P("dp"),
            P("dp"),
            P("dp"),
            P("dp"),
            P("dp"),
            P(),
        ),
        check_vma=False,
    )
```

```python
import functools

import jax
import jax.numpy as jnp
from jax import lax
from jax.experimental import pallas as pl
from jax.experimental.pallas import tpu as pltpu
from jax.sharding import PartitionSpec as P

HEADS = 9
KV_HEADS = 3
HEAD_DIM = 64
LENGTH = 1024


EPS = 1e-05
THETA = 100000.0
NEG_BIG = -1e30
LANES = 128
VMEM_LIMIT = 56 * 1024 * 1024
CORE_MASK = 1


def masks_of(devices):
    plane = tuple(2 * step for step in range(4))
    line = tuple(8 * step for step in range(devices // 8))
    return (plane, line)


def swap(field, mask, devices):
    return lax.ppermute(field, "dp", [(place, place ^ mask) for place in range(devices)])


def tree_sum(terms):
    while len(terms) > 1:
        terms = [terms[at] + terms[at + 1] for at in range(0, len(terms), 2)]
    return terms[0]


def widen(field):
    return field.astype(jnp.float32)


def slot_mask(core, slot, devices):
    line = devices // 8
    return core * CORE_MASK + 2 * (slot // line) + 8 * (slot % line)


def each_group(devices, step, body):
    group = 4

    def run(at, carry):
        for inner in range(group):
            body(at * group + inner, pl.multiple_of(at * group * step, 8) + inner * step)
        return carry

    lax.fori_loop(0, devices // group, run, 0)


def half_tiles(tiles):
    lane = lax.broadcasted_iota(jnp.int32, tiles[0].shape, 1)
    rolled = [pltpu.roll(tile, LANES // 2, 1) for tile in tiles]
    shifted = [
        jnp.where(lane < LANES // 2, rolled[at], rolled[at + 1]) for at in range(len(tiles) - 1)
    ]
    return shifted + [rolled[-1]]


def unpack_rows(stage, owner, start, rows, wide, target, row):
    whole = wide // LANES
    if wide % LANES == 0:
        for at in range(whole):
            target[at, pl.ds(row, rows), :] = stage[
                owner, pl.ds(start + at, rows, stride=whole), :
            ]
        return
    pairs, tiles_in = rows // 2, 2 * wide // LANES
    tiles = [stage[owner, pl.ds(start + at, pairs, stride=tiles_in), :] for at in range(tiles_in)]
    for at in range(whole):
        target[at, pl.ds(row, pairs, stride=2), :] = tiles[at]
    target[whole, pl.ds(row, pairs, stride=2), :] = tiles[whole]
    for at, tile in enumerate(half_tiles(tiles[whole:])):
        target[at, pl.ds(row + 1, pairs, stride=2), :] = tile


def pack_rows(source, row, rows, wide, stage, owner, start):
    whole = wide // LANES
    if wide % LANES == 0:
        for at in range(whole):
            stage[owner, pl.ds(start + at, rows, stride=whole), :] = source[
                at, pl.ds(row, rows), :
            ]
        return
    pairs, tiles_in = rows // 2, 2 * wide // LANES
    even = [
        source[at, pl.ds(row, pairs, stride=2), :] for at in range(whole + 1)
    ]
    odd = [
        source[at, pl.ds(row + 1, pairs, stride=2), :]
        for at in range(whole + 1)
    ]
    lane = lax.broadcasted_iota(jnp.int32, even[0].shape, 1)
    rolled = [pltpu.roll(tile, LANES // 2, 1) for tile in odd]
    tiles = even[:whole]
    tiles.append(jnp.where(lane < LANES // 2, even[whole], rolled[0]))
    for at in range(whole):
        tiles.append(jnp.where(lane < LANES // 2, rolled[at], rolled[at + 1]))
    for at in range(tiles_in):
        stage[owner, pl.ds(start + at, pairs, stride=tiles_in), :] = tiles[at]


def tiles_of(wide):
    return -(-wide // LANES)


def tile_widths(wide):
    return [min(LANES, wide - at) for at in range(0, wide, LANES)]


def load_stage(place_ref, own_ref, got_ref, stage, devices):
    place = place_ref[0]
    for core, pieces in enumerate((own_ref, got_ref)):

        def load(slot, carry, core=core, pieces=pieces):
            owner = place ^ slot_mask(core, slot, devices)
            stage[owner] = pieces[slot].astype(jnp.float32)
            return carry

        lax.fori_loop(0, devices // 2, load, 0)


def store_stage(kept_ref, sent_ref, stage, devices):
    for core, pieces in enumerate((kept_ref, sent_ref)):

        def store(slot, carry, core=core, pieces=pieces):
            pieces[slot] = stage[slot_mask(core, slot, devices)].astype(jnp.bfloat16)
            return carry

        lax.fori_loop(0, devices // 2, store, 0)


def unpack_kernel(place_ref, own_ref, got_ref, *refs, devices, shapes, joined):
    count = 1 if joined else len(shapes)
    outs, stage, wides = refs[:count], refs[count], refs[count + 1 :]
    load_stage(place_ref, own_ref, got_ref, stage, devices)
    start, column = 0, 0
    for index, ((rows, wide), target) in enumerate(zip(shapes, wides)):
        out = outs[0 if joined else index]
        each = rows // devices
        each_group(
            devices,
            each,
            lambda owner, row, start=start, each=each, wide=wide, target=target: unpack_rows(
                stage, owner, start, each, wide, target, row
            ),
        )
        start += each * wide // LANES
        for at, width in enumerate(tile_widths(wide)):
            tile = target[at]
            if joined and width < LANES:
                lane = lax.broadcasted_iota(jnp.int32, tile.shape, 1)
                tile = jnp.where(lane < width, tile, 0.0)
                width = LANES
            out[:, column : column + width] = tile[:, :width].astype(jnp.bfloat16)
            column += width
        if not joined:
            column = 0


def unpack_pieces(place, pieces, shapes, devices, joined):
    rows_in = pieces[0].shape[1]
    outs = shapes
    if joined:
        outs = [(shapes[0][0], sum(tiles_of(wide) for _, wide in shapes) * LANES)]
    return pl.pallas_call(
        functools.partial(unpack_kernel, devices=devices, shapes=shapes, joined=joined),
        out_shape=[jax.ShapeDtypeStruct(shape, jnp.bfloat16) for shape in outs],
        in_specs=[pl.BlockSpec(memory_space=pltpu.SMEM)] + [pl.BlockSpec(memory_space=pltpu.VMEM)] * 2,
        out_specs=[pl.BlockSpec(memory_space=pltpu.VMEM)] * len(outs),
        scratch_shapes=[pltpu.VMEM((devices, rows_in, LANES), jnp.float32)]
        + [pltpu.VMEM((-(-wide // LANES), rows, LANES), jnp.float32) for rows, wide in shapes],
        compiler_params=pltpu.CompilerParams(vmem_limit_bytes=VMEM_LIMIT),
        name="unpack",
    )(place, *pieces)


def pack_kernel(place_ref, *refs, devices, shapes, tiled_in, extra):
    count = len(shapes) + (1 if extra else 0)
    sources, kept_ref, sent_ref, stage = refs[:count], refs[count], refs[count + 1], refs[count + 2]
    wides = list(refs[count + 3 :])
    place = place_ref[0]
    start = 0
    for index, (rows, wide) in enumerate(shapes):
        each = rows // devices
        source = sources[index]
        if not tiled_in[index]:
            tiled = wides.pop(0)
            for at, width in enumerate(tile_widths(wide)):
                tiled[at, :, :width] = source[:, at * LANES : at * LANES + width]
            source = tiled
        each_group(
            devices,
            each,
            lambda owner, row, start=start, each=each, wide=wide, source=source: pack_rows(
                source, row, each, wide, stage, place ^ owner, start
            ),
        )
        start += each * wide // LANES
    if extra:
        row = jnp.concatenate([sources[-1][at : at + 1, :] for at in range(extra[0])], 1)
        for at in range(extra[0] * extra[1] // LANES):
            tile = row[:, at * LANES : (at + 1) * LANES].reshape(1, 1, LANES)
            stage[:, start + at : start + at + 1, :] = jnp.broadcast_to(tile, (devices, 1, LANES))
        start += extra[0] * extra[1] // LANES
        spare = stage.shape[1] - start
        if spare:
            stage[:, start:, :] = jnp.zeros((devices, spare, LANES), jnp.float32)
    store_stage(kept_ref, sent_ref, stage, devices)


def pack_grads(place, grads, shapes, devices, extra):
    rows_out = sum(rows * wide for rows, wide in shapes) // (devices * LANES)
    sources = list(grads)
    if extra is not None:
        rows_out = -(-(rows_out + extra.size // LANES) // 8) * 8
        sources.append(extra)
    tiled_in = tuple(grad.ndim == 3 for grad in grads)
    half = jax.ShapeDtypeStruct((devices // 2, rows_out, LANES), jnp.bfloat16)
    return pl.pallas_call(
        functools.partial(
            pack_kernel, devices=devices, shapes=shapes, tiled_in=tiled_in,
            extra=None if extra is None else extra.shape,
        ),
        out_shape=[half, half],
        in_specs=[pl.BlockSpec(memory_space=pltpu.SMEM)]
        + [pl.BlockSpec(memory_space=pltpu.VMEM)] * len(sources),
        out_specs=[pl.BlockSpec(memory_space=pltpu.VMEM)] * 2,
        scratch_shapes=[pltpu.VMEM((devices, rows_out, LANES), jnp.float32)]
        + [
            pltpu.VMEM((tiles_of(wide), rows, LANES), jnp.float32)
            for (rows, wide), tiled in zip(shapes, tiled_in)
            if not tiled
        ],
        compiler_params=pltpu.CompilerParams(vmem_limit_bytes=VMEM_LIMIT),
        name="pack",
    )(place, *sources)


BLOCK = 256


def dot_nt(left, right):
    return lax.dot_general(
        left, right, (((1,), (1,)), ((), ())), preferred_element_type=jnp.float32
    )


def dot_tn(left, right):
    return lax.dot_general(
        left, right, (((0,), (0,)), ((), ())), preferred_element_type=jnp.float32
    )


def dot_nn(left, right):
    return jnp.dot(left, right, preferred_element_type=jnp.float32)


def key_columns(head):
    first = tiles_of(HEADS * HEAD_DIM) * LANES + head * HEAD_DIM
    return slice(first, first + HEAD_DIM)


def value_columns(head):
    first = (tiles_of(HEADS * HEAD_DIM) + tiles_of(KV_HEADS * HEAD_DIM)) * LANES + head * HEAD_DIM
    return slice(first, first + HEAD_DIM)


def attend_kernel(fields_ref, mixed_ref, total_ref, *, head, group):
    length = fields_ref.shape[0]
    keys = fields_ref[:, key_columns(head)]
    values = fields_ref[:, value_columns(head)]
    lower = lax.broadcasted_iota(jnp.int32, (BLOCK, BLOCK), 0) >= lax.broadcasted_iota(
        jnp.int32, (BLOCK, BLOCK), 1
    )
    lane = lax.broadcasted_iota(jnp.int32, (BLOCK, LANES), 1)
    for start in range(0, length, BLOCK):
        mixed, totals_row = [], jnp.zeros((BLOCK, LANES), jnp.float32)
        for member in range(group):
            at = (head * group + member) * HEAD_DIM
            query = fields_ref[start : start + BLOCK, at : at + HEAD_DIM]
            diagonal = jnp.where(lower, dot_nt(query, keys[start : start + BLOCK]), NEG_BIG)
            maxima = jnp.max(diagonal, 1, keepdims=True)
            if start:
                before = dot_nt(query, keys[:start])
                maxima = jnp.maximum(maxima, jnp.max(before, 1, keepdims=True))
            expo = jnp.exp(diagonal - maxima)
            totals = jnp.sum(expo, 1, keepdims=True)
            result = dot_nn(expo.astype(jnp.bfloat16), values[start : start + BLOCK])
            if start:
                expo = jnp.exp(before - maxima)
                totals = totals + jnp.sum(expo, 1, keepdims=True)
                result = result + dot_nn(expo.astype(jnp.bfloat16), values[:start])
            mixed.append(result / totals)
            totals_row = jnp.where(lane == member, maxima + jnp.log(totals), totals_row)
        mixed_ref[start : start + BLOCK, :] = jnp.concatenate(mixed, 1).astype(jnp.bfloat16)
        total_ref[start : start + BLOCK, :] = totals_row


def attend(fields, head, group):
    length = fields.shape[0]
    return pl.pallas_call(
        functools.partial(attend_kernel, head=head, group=group),
        out_shape=[
            jax.ShapeDtypeStruct((length, group * HEAD_DIM), jnp.bfloat16),
            jax.ShapeDtypeStruct((length, LANES), jnp.float32),
        ],
        in_specs=[pl.BlockSpec(memory_space=pltpu.VMEM)],
        out_specs=[pl.BlockSpec(memory_space=pltpu.VMEM)] * 2,
        compiler_params=pltpu.CompilerParams(vmem_limit_bytes=VMEM_LIMIT),
        cost_estimate=pl.CostEstimate(
            flops=12 * 10**9, bytes_accessed=4 * 10**6, transcendentals=2 * 10**6
        ),
        name="attend",
    )(fields)


def attend_back_kernel(
    fields_ref, back_ref, mixed_ref, total_ref,
    query_back_ref, key_back_ref, queries, backs, totals, deltas, query_sum, key_sum, value_sum,
    *, head, group,
):
    length = fields_ref.shape[0]
    ones = jnp.ones((8, HEAD_DIM), jnp.float32)
    totals[...] = total_ref[...].T[:8]
    for member in range(group):
        at = (head * group + member) * HEAD_DIM
        queries[member] = fields_ref[:, at : at + HEAD_DIM]
        back = back_ref[:, at : at + HEAD_DIM]
        backs[member] = back
        product = back.astype(jnp.float32) * mixed_ref[
            :, member * HEAD_DIM : (member + 1) * HEAD_DIM
        ].astype(jnp.float32)
        deltas[member] = lax.dot_general(
            ones, product, (((1,), (1,)), ((), ())),
            precision=lax.Precision.HIGHEST, preferred_element_type=jnp.float32,
        )
    keys_all = fields_ref[:, key_columns(head)]
    values_all = fields_ref[:, value_columns(head)]
    upper = lax.broadcasted_iota(jnp.int32, (BLOCK, BLOCK), 0) <= lax.broadcasted_iota(
        jnp.int32, (BLOCK, BLOCK), 1
    )
    for member in range(group):
        total_row = totals[member : member + 1, :]
        delta_row = deltas[member][0:1]
        for start in range(0, length, BLOCK):
            keys = keys_all[start : start + BLOCK]
            values = values_all[start : start + BLOCK]
            query = queries[member, start:, :]
            back = backs[member, start:, :]
            scores = dot_nt(keys, query)
            probs = jnp.exp(scores - total_row[:, start:])
            first = jnp.where(upper, probs[:, :BLOCK], 0.0)
            probs = first if start + BLOCK == length else jnp.concatenate(
                [first, probs[:, BLOCK:]], 1
            )
            prob_back = dot_nt(values, back)
            score_back = (probs * (prob_back - delta_row[:, start:])).astype(jnp.bfloat16)
            value_part = dot_nn(probs.astype(jnp.bfloat16), back)
            key_part = dot_nn(score_back, query)
            query_part = dot_tn(score_back, keys)
            if member:
                key_sum[start : start + BLOCK, :] += key_part
                value_sum[start : start + BLOCK, :] += value_part
            else:
                key_sum[start : start + BLOCK, :] = key_part
                value_sum[start : start + BLOCK, :] = value_part
            if start:
                query_sum[member, start:, :] += query_part
            else:
                query_sum[member] = query_part
    query_back_ref[...] = (
        jnp.concatenate([query_sum[member] for member in range(group)], 1) * HEAD_DIM ** (-0.5)
    )
    key_back_ref[...] = jnp.concatenate([key_sum[...], value_sum[...]], 1)


def attend_back(fields, back, mixed, total, head, group):
    length = fields.shape[0]
    return pl.pallas_call(
        functools.partial(attend_back_kernel, head=head, group=group),
        out_shape=[
            jax.ShapeDtypeStruct((length, group * HEAD_DIM), jnp.float32),
            jax.ShapeDtypeStruct((length, 2 * HEAD_DIM), jnp.float32),
        ],
        in_specs=[pl.BlockSpec(memory_space=pltpu.VMEM)] * 4,
        out_specs=[pl.BlockSpec(memory_space=pltpu.VMEM)] * 2,
        scratch_shapes=[
            pltpu.VMEM((group, length, HEAD_DIM), jnp.bfloat16),
            pltpu.VMEM((group, length, HEAD_DIM), jnp.bfloat16),
            pltpu.VMEM((8, length), jnp.float32),
            pltpu.VMEM((group, 8, length), jnp.float32),
            pltpu.VMEM((group, length, HEAD_DIM), jnp.float32),
            pltpu.VMEM((length, HEAD_DIM), jnp.float32),
            pltpu.VMEM((length, HEAD_DIM), jnp.float32),
        ],
        compiler_params=pltpu.CompilerParams(vmem_limit_bytes=VMEM_LIMIT),
        cost_estimate=pl.CostEstimate(
            flops=24 * 10**9, bytes_accessed=8 * 10**6, transcendentals=2 * 10**6
        ),
        name="attend_back",
    )(fields, back, mixed, total)


def partner_of(tile):
    lane = lax.broadcasted_iota(jnp.int32, tile.shape, 1)
    half = HEAD_DIM // 2
    return jnp.where(
        lane % HEAD_DIM < half, pltpu.roll(tile, LANES - half, 1), pltpu.roll(tile, half, 1)
    )


def normed_rows(tokens_ref, gains_ref):
    resid = tokens_ref[...].astype(jnp.float32)
    inv_rms = lax.rsqrt(jnp.mean(resid * resid, 1, keepdims=True) + EPS)
    return resid, inv_rms, (resid * inv_rms * gains_ref[0:1, :]).astype(jnp.bfloat16)


def project_kernel(tokens_ref, gains_ref, wide_ref, cosine_ref, sine_ref, fields_ref, normed):
    _, _, normed[...] = normed_rows(tokens_ref, gains_ref)
    first_key = tiles_of(HEADS * HEAD_DIM)
    first_value = first_key + tiles_of(KV_HEADS * HEAD_DIM)
    count = fields_ref.shape[1] // LANES
    for start in range(0, count, 2):
        stop = min(start + 2, count)
        pair = dot_nn(normed[...], wide_ref[:, start * LANES : stop * LANES])
        for at in range(start, stop):
            tile = pair[:, (at - start) * LANES : (at - start + 1) * LANES]
            if at < first_value:
                tile = tile * cosine_ref[...] - partner_of(tile) * sine_ref[...]
            tile = tile.astype(jnp.bfloat16)
            if at < first_key:
                tile = (tile.astype(jnp.float32) * HEAD_DIM ** (-0.5)).astype(jnp.bfloat16)
            fields_ref[:, at * LANES : (at + 1) * LANES] = tile


def vmem_call(kernel, out_shape, scratch_shapes, name, flops, *args):
    single = not isinstance(out_shape, list)
    return pl.pallas_call(
        kernel,
        out_shape=out_shape,
        in_specs=[pl.BlockSpec(memory_space=pltpu.VMEM)] * len(args),
        out_specs=pl.BlockSpec(memory_space=pltpu.VMEM)
        if single
        else [pl.BlockSpec(memory_space=pltpu.VMEM)] * len(out_shape),
        scratch_shapes=scratch_shapes,
        compiler_params=pltpu.CompilerParams(vmem_limit_bytes=VMEM_LIMIT),
        cost_estimate=pl.CostEstimate(flops=flops, bytes_accessed=10**7, transcendentals=0),
        name=name,
    )(*args)


def project(tokens, gains, wide, cosine, sine):
    return vmem_call(
        project_kernel,
        jax.ShapeDtypeStruct((tokens.shape[0], wide.shape[1]), jnp.bfloat16),
        [pltpu.VMEM(tokens.shape, jnp.bfloat16)],
        "project",
        8 * 10**9,
        tokens, gains, wide, cosine, sine,
    )


def finish_kernel(
    tokens_ref, gains_ref, wide_ref, cosine_ref, sine_ref, mid_back_ref, *refs, heads
):
    backs = refs[: 2 * heads]
    input_grad_ref, tiled_ref, gain_ref, fields, normed_t = refs[2 * heads :]
    half = HEAD_DIM
    group = HEADS // heads
    wide_heads = [(backs[2 * (at // group)], at % group * half) for at in range(HEADS)]
    wide_heads += [None] * (HEADS % 2)
    for offset in (0, half):
        wide_heads += [(backs[2 * at + 1], offset) for at in range(heads)] + [None] * (heads % 2)
    turned = tiles_of(HEADS * HEAD_DIM) + tiles_of(heads * HEAD_DIM)
    for at in range(len(wide_heads) // 2):
        cols = []
        for item in wide_heads[2 * at : 2 * at + 2]:
            if item is None:
                cols.append(jnp.zeros((fields.shape[0], half), jnp.float32))
            else:
                cols.append(item[0][:, item[1] : item[1] + half])
        tile = jnp.concatenate(cols, 1)
        if at < turned:
            tile = tile * cosine_ref[...] + partner_of(tile) * sine_ref[...]
        fields[:, at * LANES : (at + 1) * LANES] = tile.astype(jnp.bfloat16)
    resid, inv_rms, normed = normed_rows(tokens_ref, gains_ref)
    normed_t[...] = normed.T
    count = fields.shape[1] // LANES
    for start in range(0, count, 2):
        stop = min(start + 2, count)
        pair = dot_nn(normed_t[...], fields[:, start * LANES : stop * LANES])
        for at in range(start, stop):
            tiled_ref[at] = pair[:, (at - start) * LANES : (at - start + 1) * LANES]
    one_back = dot_nt(fields[...], wide_ref[...])
    weighted = one_back * gains_ref[0:1, :]
    cubed = inv_rms * inv_rms * inv_rms
    scaled = resid * inv_rms
    gain_ref[...] = jnp.sum(one_back * scaled, 0, keepdims=True)
    mean = jnp.mean(weighted * resid, 1, keepdims=True)
    grad = mid_back_ref[...] + inv_rms * weighted - resid * (cubed * mean)
    input_grad_ref[...] = grad.astype(jnp.bfloat16)


def finish(tokens, gains, wide, cosine, sine, mid_back, backs):
    heads = len(backs)
    rows, width = tokens.shape
    return vmem_call(
        functools.partial(finish_kernel, heads=heads),
        [
            jax.ShapeDtypeStruct(tokens.shape, jnp.bfloat16),
            jax.ShapeDtypeStruct((wide.shape[1] // LANES, width, LANES), jnp.float32),
            jax.ShapeDtypeStruct((1, width), jnp.float32),
        ],
        [
            pltpu.VMEM((rows, wide.shape[1]), jnp.bfloat16),
            pltpu.VMEM((width, rows), jnp.bfloat16),
        ],
        "finish",
        12 * 10**9,
        tokens, gains, wide, cosine, sine, mid_back, *[part for back in backs for part in back],
    )


def rotary_tables(length, head_dim):
    half_dim = head_dim // 2
    frequency = THETA ** (-(jnp.arange(half_dim, dtype=jnp.float32) * 2.0 / head_dim))
    angles = jnp.arange(length, dtype=jnp.float32)[:, None] * frequency[None, :]
    return (jnp.cos(angles), jnp.sin(angles))


def rotate_heads(field, cosine, sine):
    half_dim = field.shape[-1] // 2
    first_half = field[..., :half_dim]
    second_half = field[..., half_dim:]
    cosine = cosine[None, :, None, :]
    sine = sine[None, :, None, :]
    return jnp.concatenate(
        [first_half * cosine - second_half * sine, second_half * cosine + first_half * sine], -1
    )


def normalize(hidden, gain):
    inv_rms = lax.rsqrt(jnp.mean(hidden * hidden, -1, keepdims=True) + EPS)
    return (hidden * inv_rms * gain, inv_rms)


def normalize_back(grad, hidden, inv_rms, gain):
    weighted = grad * gain
    cubed = inv_rms * inv_rms * inv_rms
    hidden_grad = inv_rms * weighted - hidden * cubed * jnp.mean(
        weighted * hidden, -1, keepdims=True
    )
    gain_part = jnp.sum(grad * hidden * inv_rms, 0)
    return (hidden_grad, gain_part)


def outer_prod(left, right):
    return lax.dot_general(
        left, right, (((0,), (0,)), ((), ())), preferred_element_type=jnp.float32
    )


def times_transposed(left, matrix):
    return lax.dot_general(
        left, matrix, (((1,), (1,)), ((), ())), preferred_element_type=jnp.float32
    )


def whole_rows(shapes, devices):
    return (devices & (devices - 1)) == 0 and all(
        rows % (8 * devices // 4) == 0 and rows * wide % (devices * LANES) == 0
        for rows, wide in shapes
    )


def place_of():
    return lax.axis_index("dp").astype(jnp.int32).reshape(1)


class WeightGather:
    def __init__(self, shards, shapes, devices):
        self.shards, self.shapes, self.devices = shards, shapes, devices
        self.stages = whole_rows(shapes, devices)
        if self.stages:
            self.held = jnp.concatenate([shard.reshape(-1, LANES) for shard in shards])

    def line_stage(self, other):
        if not self.stages:
            return other
        _, line = masks_of(self.devices)
        self.held, other = tied(self.held, other)
        self.arrived = [self.held] + [swap(self.held, mask, self.devices) for mask in line[1:]]
        return other

    def plane_stage(self, other):
        if not self.stages:
            return other
        plane, _ = masks_of(self.devices)
        self.held, other = tied(jnp.stack(self.arrived), other)
        self.arrived = [self.held] + [swap(self.held, mask, self.devices) for mask in plane[1:]]
        return other

    def core_stage(self, other):
        if not self.stages:
            return other
        self.arrived, other = tied(self.arrived, other)
        self.held = jnp.concatenate(self.arrived)
        self.got = swap(self.held, CORE_MASK, self.devices)
        return other

    def result(self, joined):
        if not self.stages:
            mats = [
                lax.all_gather(shard, "dp", axis=0, tiled=True).reshape(shape)
                for shard, shape in zip(self.shards, self.shapes)
            ]
            if not joined:
                return mats
            pads = [((0, 0), (0, tiles_of(mat.shape[1]) * LANES - mat.shape[1])) for mat in mats]
            return [jnp.concatenate([jnp.pad(mat, pad) for mat, pad in zip(mats, pads)], 1)]
        pieces = (self.held, self.got)
        return unpack_pieces(place_of(), pieces, self.shapes, self.devices, joined)


def tied(first, second):
    return lax.optimization_barrier((first, second))


class GradSum:
    def __init__(self, grads, shapes, devices, extra=None):
        self.grads, self.shapes, self.devices, self.extra = grads, shapes, devices, extra
        self.stages = whole_rows(shapes, devices)
        if self.stages:
            self.kept, self.sent = pack_grads(place_of(), grads, shapes, devices, extra)

    def core_stage(self, other):
        if not self.stages:
            return other
        (self.kept, self.sent), other = tied((self.kept, self.sent), other)
        self.got = swap(self.sent, CORE_MASK, self.devices)
        return other

    def plane_stage(self, other):
        if not self.stages:
            return other
        plane, _ = masks_of(self.devices)
        block = self.kept.shape[0] // len(plane)
        cuts = [slice(at * block, (at + 1) * block) for at in range(len(plane))]
        parts = [(widen(self.kept[cut]) + widen(self.got[cut])).astype(jnp.bfloat16) for cut in cuts]
        self.parts, other = tied(parts, other)
        self.arrived = [
            swap(part, mask, self.devices) for part, mask in zip(self.parts[1:], plane[1:])
        ]
        return other

    def line_stage(self, other):
        if not self.stages:
            return other
        _, line = masks_of(self.devices)
        terms = [self.parts[0]] + self.arrived
        parts = [
            tree_sum([widen(term[at]) for term in terms]).astype(jnp.bfloat16)
            for at in range(len(line))
        ]
        self.parts, other = tied(parts, other)
        self.arrived = [
            swap(part, mask, self.devices) for part, mask in zip(self.parts[1:], line[1:])
        ]
        return other

    def result(self):
        if not self.stages:
            grads = [
                grad.swapaxes(0, 1).reshape(rows, -1)[:, :wide] if grad.ndim == 3 else grad
                for grad, (rows, wide) in zip(self.grads, self.shapes)
            ]
            sums = [
                lax.psum_scatter(grad.reshape(-1), "dp", scatter_dimension=0, tiled=True)
                for grad in grads
            ]
            return sums if self.extra is None else sums + [lax.psum(self.extra, "dp")]
        pieces = tree_sum([widen(term) for term in [self.parts[0]] + self.arrived])
        sums, start = [], 0
        for rows, wide in self.shapes:
            count = rows * wide // (self.devices * LANES)
            sums.append(pieces[start : start + count].reshape(-1))
            start += count
        if self.extra is not None:
            count = self.extra.size // LANES
            sums.append(pieces[start : start + count].reshape(self.extra.shape))
        return sums


def body(tokens, cotangent, w_query, w_key, w_value, w_out, w_gate, w_up, w_down, norm_gains):
    model_width = tokens.shape[1]
    seq_count = tokens.shape[0] // LENGTH
    group_size = HEADS // KV_HEADS
    scale_factor = HEAD_DIM ** (-0.5)
    gain_f = norm_gains.astype(jnp.float32)
    shards = (w_query, w_key, w_value, w_out, w_gate, w_up, w_down)
    devices = lax.axis_size("dp")
    widths = [shards[at].shape[0] * devices // model_width for at in range(6)]
    shapes = [(model_width, wide) for wide in widths] + [
        (shards[6].shape[0] * devices // model_width, model_width)
    ]
    first = WeightGather(shards[:3], shapes[:3], devices)
    second = WeightGather(shards[3:], shapes[3:], devices)
    tokens = first.line_stage(tokens)
    tokens = first.plane_stage(tokens)
    tokens = second.line_stage(tokens)
    tokens = first.core_stage(tokens)
    (wide_mat,) = first.result(True)
    resid_in = tokens.astype(jnp.float32)
    cosine, sine = rotary_tables(LENGTH, HEAD_DIM)
    pairs = LANES // HEAD_DIM
    cosine = jnp.tile(cosine, (seq_count, 2 * pairs))
    sine = jnp.tile(jnp.concatenate([sine, -sine], 1), (seq_count, pairs))
    fields = project(tokens, gain_f, wide_mat, cosine, sine)
    fields = second.plane_stage(fields)
    attended = [attend(fields, head, group_size) for head in range(2)]
    fields, attended = second.core_stage((fields, attended))
    attended.append(attend(fields, 2, group_size))
    wo_mat, wg_mat, wu_mat, wd_mat = second.result(False)
    mixed = jnp.concatenate([part for part, _ in attended], 1)
    attn_out = jnp.dot(mixed, wo_mat, preferred_element_type=jnp.float32)
    middle = resid_in + attn_out
    normed_two, rms_two = normalize(middle, gain_f[1])
    normed_two = normed_two.astype(jnp.bfloat16)
    gate = jnp.dot(normed_two, wg_mat, preferred_element_type=jnp.float32)
    upward = jnp.dot(normed_two, wu_mat, preferred_element_type=jnp.float32)
    sigmoid_g = jax.nn.sigmoid(gate)
    activated = gate * sigmoid_g
    hidden = (activated * upward).astype(jnp.bfloat16)
    ffn_out = jnp.dot(hidden, wd_mat, preferred_element_type=jnp.float32)
    output = (middle + ffn_out).astype(jnp.bfloat16)
    grad_down = outer_prod(hidden, cotangent)
    hidden_back = times_transposed(cotangent, wd_mat)
    gate_back = (hidden_back * upward * sigmoid_g * (1.0 + gate * (1.0 - sigmoid_g))).astype(
        jnp.bfloat16
    )
    up_back = (hidden_back * activated).astype(jnp.bfloat16)
    grad_gate = outer_prod(normed_two, gate_back)
    grad_up = outer_prod(normed_two, up_back)
    two_back = times_transposed(gate_back, wg_mat) + times_transposed(up_back, wu_mat)
    norm_two_back, gain_two = normalize_back(two_back, middle, rms_two, gain_f[1])
    mid_back = cotangent.astype(jnp.float32) + norm_two_back
    mid_low = mid_back.astype(jnp.bfloat16)
    grad_out = outer_prod(mixed, mid_low)
    mixed_back = times_transposed(mid_low, wo_mat).astype(jnp.bfloat16)
    feed_sum = GradSum((grad_gate, grad_up, grad_down), shapes[4:], devices)

    def back_of(head, field):
        part, total = attended[head]
        return attend_back(fields, field, part, total, head, group_size)

    mixed_back = feed_sum.core_stage(mixed_back)
    backs = [back_of(0, mixed_back)]
    mixed_back, _ = tied(mixed_back, backs[0])
    mixed_back = feed_sum.plane_stage(mixed_back)
    backs += [back_of(head, mixed_back) for head in range(1, KV_HEADS)]
    input_grad, tiled, gain_one = finish(tokens, gain_f, wide_mat, cosine, sine, mid_back, backs)
    input_grad, tiled = feed_sum.line_stage((input_grad, tiled))
    gains_back = jnp.concatenate([gain_one, gain_two[None]], 0)
    cuts = [0]
    for _, wide in shapes[:3]:
        cuts.append(cuts[-1] + tiles_of(wide))
    grads = tuple(tiled[start:stop] for start, stop in zip(cuts, cuts[1:])) + (grad_out,)
    mix_sum = GradSum(grads, shapes[:4], devices, gains_back)
    input_grad = mix_sum.core_stage(input_grad)
    input_grad = mix_sum.plane_stage(input_grad)
    input_grad = mix_sum.line_stage(input_grad)
    mix_parts = mix_sum.result()
    all_parts, gain_grad = mix_parts[:4] + feed_sum.result(), mix_parts[4]
    return (output, input_grad) + tuple(all_parts) + (gain_grad,)


def solution(mesh):
    return jax.shard_map(
        body,
        mesh=mesh,
        in_specs=(
            P("dp", None),
            P("dp", None),
            P("dp"),
            P("dp"),
            P("dp"),
            P("dp"),
            P("dp"),
            P("dp"),
            P("dp"),
            P(),
        ),
        out_specs=(
            P("dp", None),
            P("dp", None),
            P("dp"),
            P("dp"),
            P("dp"),
            P("dp"),
            P("dp"),
            P("dp"),
            P("dp"),
            P(),
        ),
        check_vma=False,
    )
```

```python
import functools

import jax
import jax.numpy as jnp
from jax import lax
from jax.experimental import pallas as pl
from jax.experimental.pallas import tpu as pltpu
from jax.sharding import PartitionSpec as P

HEADS = 9
KV_HEADS = 3
HEAD_DIM = 64
LENGTH = 1024


EPS = 1e-05
THETA = 100000.0
NEG_BIG = -1e30
LANES = 128
VMEM_LIMIT = 56 * 1024 * 1024
CORE_MASK = 1
LIGHT = pl.CostEstimate(flops=10**8, bytes_accessed=10**6, transcendentals=0)


def masks_of(devices):
    plane = tuple(2 * step for step in range(4))
    line = tuple(8 * step for step in range(devices // 8))
    return (plane, line)


def swap(field, mask, devices):
    return lax.ppermute(field, "dp", [(place, place ^ mask) for place in range(devices)])


def tree_sum(terms):
    while len(terms) > 1:
        terms = [terms[at] + terms[at + 1] for at in range(0, len(terms), 2)]
    return terms[0]


def widen(field):
    return field.astype(jnp.float32)


def slot_mask(core, slot, devices):
    line = devices // 8
    return core * CORE_MASK + 2 * (slot // line) + 8 * (slot % line)


def tiles_of(wide):
    return -(-wide // LANES)


def tile_widths(wide):
    return [min(LANES, wide - at) for at in range(0, wide, LANES)]


def flat_starts(shapes, devices):
    starts = [0]
    for rows, wide in shapes:
        starts.append(starts[-1] + rows * wide // (devices * LANES))
    return starts


def tiled_shapes(shapes):
    return [(tiles_of(wide), rows, LANES) for rows, wide in shapes if wide % LANES]


def unpack_kernel(place_ref, *refs, devices, shapes, joined, count):
    pieces, refs = refs[:count], refs[count:]
    out_count = 1 if joined else len(shapes)
    outs, flats, refs = refs[:out_count], refs[out_count : out_count + len(shapes)], refs[out_count + len(shapes) :]
    stage, tiled_refs = refs[0], list(refs[1:])
    place = place_ref[0]
    starts = flat_starts(shapes, devices)
    block = pieces[0].shape[0]
    for index, piece_ref in enumerate(pieces):
        core, plane = index * block * 2 // devices, index % (devices // 2 // block)

        def load(slot, carry, core=core, plane=plane, piece_ref=piece_ref):
            owner = place ^ slot_mask(core, plane * block + slot, devices)
            piece = piece_ref[slot].astype(jnp.float32)
            if any(start % 8 for start in starts[:-1]):
                stage[slot % 4] = piece
            for flat, start, stop in zip(flats, starts, starts[1:]):
                each = stop - start
                rows = stage[slot % 4, start:stop, :] if start % 8 else piece[start:stop]
                flat[pl.ds(owner * each, each), :] = rows
            return carry

        lax.fori_loop(0, block, load, 0)
    column = 0
    for index, ((rows, wide), flat) in enumerate(zip(shapes, flats)):
        out = outs[0 if joined else index]
        whole = wide // LANES
        if wide % LANES == 0:
            for at in range(whole):
                tile = flat[pl.ds(at, rows, stride=whole), :]
                out[:, column + at * LANES : column + (at + 1) * LANES] = tile.astype(jnp.bfloat16)
        else:
            target = tiled_refs.pop(0)
            pairs, tiles_in = rows // 2, 2 * wide // LANES
            for at in range(whole + 1):
                target[at, pl.ds(0, pairs, stride=2), :] = flat[pl.ds(at, pairs, stride=tiles_in), :]
            rolled = None
            for at in range(whole, tiles_in):
                after = pltpu.roll(flat[pl.ds(at, pairs, stride=tiles_in), :], LANES // 2, 1)
                if rolled is not None:
                    lane = lax.broadcasted_iota(jnp.int32, after.shape, 1)
                    target[at - whole - 1, pl.ds(1, pairs, stride=2), :] = jnp.where(
                        lane < LANES // 2, rolled, after
                    )
                rolled = after
            target[whole, pl.ds(1, pairs, stride=2), :] = rolled
            for at, width in enumerate(tile_widths(wide)):
                tile = target[at]
                if joined and width < LANES:
                    lane = lax.broadcasted_iota(jnp.int32, tile.shape, 1)
                    tile = jnp.where(lane < width, tile, 0.0)
                    width = LANES
                start = column + at * LANES
                out[:, start : start + width] = tile[:, :width].astype(jnp.bfloat16)
        if joined:
            column += tiles_of(wide) * LANES


def unpack_pieces(place, pieces, shapes, devices, joined):
    rows_in = pieces[0].shape[1]
    outs = shapes
    if joined:
        outs = [(shapes[0][0], sum(tiles_of(wide) for _, wide in shapes) * LANES)]
    return pl.pallas_call(
        functools.partial(
            unpack_kernel, devices=devices, shapes=shapes, joined=joined, count=len(pieces)
        ),
        out_shape=[jax.ShapeDtypeStruct(shape, jnp.bfloat16) for shape in outs],
        in_specs=[pl.BlockSpec(memory_space=pltpu.SMEM)]
        + [pl.BlockSpec(memory_space=pltpu.VMEM)] * len(pieces),
        out_specs=[pl.BlockSpec(memory_space=pltpu.VMEM)] * len(outs),
        scratch_shapes=[
            pltpu.VMEM((rows * wide // LANES, LANES), jnp.float32) for rows, wide in shapes
        ]
        + [pltpu.VMEM((4, rows_in, LANES), jnp.float32)]
        + [pltpu.VMEM(shape, jnp.float32) for shape in tiled_shapes(shapes)],
        compiler_params=pltpu.CompilerParams(vmem_limit_bytes=VMEM_LIMIT),
        cost_estimate=LIGHT,
        name="unpack",
    )(place, *pieces)


def pack_kernel(place_ref, *refs, devices, shapes, tiled_in, extra):
    count = len(shapes) + (1 if extra else 0)
    sources, kept_ref, sent_ref, stage = refs[:count], refs[count], refs[count + 1], refs[count + 2]
    flats = refs[count + 3 : count + 3 + len(shapes)]
    tiled_refs = list(refs[count + 3 + len(shapes) :])
    place = place_ref[0]
    starts = flat_starts(shapes, devices)
    for index, ((rows, wide), flat) in enumerate(zip(shapes, flats)):
        source, whole = sources[index], wide // LANES
        if wide % LANES == 0:
            for at in range(whole):
                flat[pl.ds(at, rows, stride=whole), :] = (
                    source[at] if tiled_in[index] else source[:, at * LANES : (at + 1) * LANES]
                )
            continue
        if not tiled_in[index]:
            tiled = tiled_refs.pop(0)
            for at, width in enumerate(tile_widths(wide)):
                tiled[at, :, :width] = source[:, at * LANES : at * LANES + width]
            source = tiled
        pairs, tiles_in = rows // 2, 2 * wide // LANES
        for at in range(whole):
            flat[pl.ds(at, pairs, stride=tiles_in), :] = source[at, pl.ds(0, pairs, stride=2), :]
        before = source[whole, pl.ds(0, pairs, stride=2), :]
        lane = lax.broadcasted_iota(jnp.int32, before.shape, 1)
        for at in range(whole + 1):
            rolled = pltpu.roll(source[at, pl.ds(1, pairs, stride=2), :], LANES // 2, 1)
            flat[pl.ds(whole + at, pairs, stride=tiles_in), :] = jnp.where(
                lane < LANES // 2, before, rolled
            )
            before = rolled
    row_tiles = []
    if extra:
        row = jnp.concatenate([sources[-1][at : at + 1, :] for at in range(extra[0])], 1)
        row_tiles = [
            row[:, at * LANES : (at + 1) * LANES] for at in range(extra[0] * extra[1] // LANES)
        ]
    direct = not extra and all(start % 8 == 0 for start in starts)
    if not direct:
        for at in range(4):
            for index, tile in enumerate(row_tiles):
                stage[at, starts[-1] + index : starts[-1] + index + 1, :] = tile
            used = starts[-1] + len(row_tiles)
            if used < stage.shape[1]:
                stage[at, used:, :] = jnp.zeros((stage.shape[1] - used, LANES), jnp.float32)
    for core, pieces in enumerate((kept_ref, sent_ref)):

        def store(slot, carry, core=core, pieces=pieces):
            owner = place ^ slot_mask(core, slot, devices)
            parts = []
            for flat, start, stop in zip(flats, starts, starts[1:]):
                rows = flat[pl.ds(owner * (stop - start), stop - start), :]
                if direct:
                    parts.append(rows)
                else:
                    stage[slot % 4, start:stop, :] = rows
            piece = jnp.concatenate(parts, 0) if direct else stage[slot % 4]
            pieces[slot] = piece.astype(jnp.bfloat16)
            return carry

        lax.fori_loop(0, devices // 2, store, 0)


def pack_grads(place, grads, shapes, devices, extra):
    rows_out = sum(rows * wide for rows, wide in shapes) // (devices * LANES)
    sources = list(grads)
    if extra is not None:
        rows_out = -(-(rows_out + extra.size // LANES) // 8) * 8
        sources.append(extra)
    tiled_in = tuple(grad.ndim == 3 for grad in grads)
    half = jax.ShapeDtypeStruct((devices // 2, rows_out, LANES), jnp.bfloat16)
    untiled = [shape for shape, tiled in zip(shapes, tiled_in) if not tiled]
    return pl.pallas_call(
        functools.partial(
            pack_kernel, devices=devices, shapes=shapes, tiled_in=tiled_in,
            extra=None if extra is None else extra.shape,
        ),
        out_shape=[half, half],
        in_specs=[pl.BlockSpec(memory_space=pltpu.SMEM)]
        + [pl.BlockSpec(memory_space=pltpu.VMEM)] * len(sources),
        out_specs=[pl.BlockSpec(memory_space=pltpu.VMEM)] * 2,
        scratch_shapes=[pltpu.VMEM((4, rows_out, LANES), jnp.float32)]
        + [pltpu.VMEM((rows * wide // LANES, LANES), jnp.float32) for rows, wide in shapes]
        + [pltpu.VMEM(shape, jnp.float32) for shape in tiled_shapes(untiled)],
        compiler_params=pltpu.CompilerParams(vmem_limit_bytes=VMEM_LIMIT),
        cost_estimate=LIGHT,
        name="pack",
    )(place, *sources)


BLOCK = 256


def dot_nt(left, right):
    return lax.dot_general(
        left, right, (((1,), (1,)), ((), ())), preferred_element_type=jnp.float32
    )


def dot_tn(left, right):
    return lax.dot_general(
        left, right, (((0,), (0,)), ((), ())), preferred_element_type=jnp.float32
    )


def dot_nn(left, right):
    return jnp.dot(left, right, preferred_element_type=jnp.float32)


def key_columns(head):
    first = tiles_of(HEADS * HEAD_DIM) * LANES + head * HEAD_DIM
    return slice(first, first + HEAD_DIM)


def value_columns(head):
    first = (tiles_of(HEADS * HEAD_DIM) + tiles_of(KV_HEADS * HEAD_DIM)) * LANES + head * HEAD_DIM
    return slice(first, first + HEAD_DIM)


def attend_kernel(fields_ref, mixed_ref, total_ref, *, head, group):
    length = fields_ref.shape[0]
    keys = fields_ref[:, key_columns(head)]
    values = fields_ref[:, value_columns(head)]
    lower = lax.broadcasted_iota(jnp.int32, (BLOCK, BLOCK), 0) >= lax.broadcasted_iota(
        jnp.int32, (BLOCK, BLOCK), 1
    )
    lane = lax.broadcasted_iota(jnp.int32, (BLOCK, LANES), 1)
    for start in range(0, length, BLOCK):
        mixed, totals_row = [], jnp.zeros((BLOCK, LANES), jnp.float32)
        for member in range(group):
            at = (head * group + member) * HEAD_DIM
            query = fields_ref[start : start + BLOCK, at : at + HEAD_DIM]
            diagonal = jnp.where(lower, dot_nt(query, keys[start : start + BLOCK]), NEG_BIG)
            maxima = jnp.max(diagonal, 1, keepdims=True)
            if start:
                before = dot_nt(query, keys[:start])
                maxima = jnp.maximum(maxima, jnp.max(before, 1, keepdims=True))
            expo = jnp.exp(diagonal - maxima)
            totals = jnp.sum(expo, 1, keepdims=True)
            result = dot_nn(expo.astype(jnp.bfloat16), values[start : start + BLOCK])
            if start:
                expo = jnp.exp(before - maxima)
                totals = totals + jnp.sum(expo, 1, keepdims=True)
                result = result + dot_nn(expo.astype(jnp.bfloat16), values[:start])
            mixed.append(result / totals)
            totals_row = jnp.where(lane == member, maxima + jnp.log(totals), totals_row)
        mixed_ref[start : start + BLOCK, :] = jnp.concatenate(mixed, 1).astype(jnp.bfloat16)
        total_ref[start : start + BLOCK, :] = totals_row


def attend(fields, head, group):
    length = fields.shape[0]
    return pl.pallas_call(
        functools.partial(attend_kernel, head=head, group=group),
        out_shape=[
            jax.ShapeDtypeStruct((length, group * HEAD_DIM), jnp.bfloat16),
            jax.ShapeDtypeStruct((length, LANES), jnp.float32),
        ],
        in_specs=[pl.BlockSpec(memory_space=pltpu.VMEM)],
        out_specs=[pl.BlockSpec(memory_space=pltpu.VMEM)] * 2,
        compiler_params=pltpu.CompilerParams(vmem_limit_bytes=VMEM_LIMIT),
        cost_estimate=LIGHT,
        name="attend",
    )(fields)


def attend_back_kernel(
    fields_ref, back_ref, mixed_ref, total_ref,
    query_back_ref, key_back_ref, queries, backs, totals, deltas, query_sum, key_sum, value_sum,
    *, head, group,
):
    length = fields_ref.shape[0]
    ones = jnp.ones((8, HEAD_DIM), jnp.float32)
    totals[...] = total_ref[...].T[:8]
    for member in range(group):
        at = (head * group + member) * HEAD_DIM
        queries[member] = fields_ref[:, at : at + HEAD_DIM]
        back = back_ref[:, at : at + HEAD_DIM]
        backs[member] = back
        product = back.astype(jnp.float32) * mixed_ref[
            :, member * HEAD_DIM : (member + 1) * HEAD_DIM
        ].astype(jnp.float32)
        deltas[member] = lax.dot_general(
            ones, product, (((1,), (1,)), ((), ())),
            precision=lax.Precision.HIGHEST, preferred_element_type=jnp.float32,
        )
    keys_all = fields_ref[:, key_columns(head)]
    values_all = fields_ref[:, value_columns(head)]
    upper = lax.broadcasted_iota(jnp.int32, (BLOCK, BLOCK), 0) <= lax.broadcasted_iota(
        jnp.int32, (BLOCK, BLOCK), 1
    )
    for member in range(group):
        total_row = totals[member : member + 1, :]
        delta_row = deltas[member][0:1]
        for start in range(0, length, BLOCK):
            keys = keys_all[start : start + BLOCK]
            values = values_all[start : start + BLOCK]
            query = queries[member, start:, :]
            back = backs[member, start:, :]
            scores = dot_nt(keys, query)
            probs = jnp.exp(scores - total_row[:, start:])
            first = jnp.where(upper, probs[:, :BLOCK], 0.0)
            probs = first if start + BLOCK == length else jnp.concatenate(
                [first, probs[:, BLOCK:]], 1
            )
            prob_back = dot_nt(values, back)
            score_back = (probs * (prob_back - delta_row[:, start:])).astype(jnp.bfloat16)
            value_part = dot_nn(probs.astype(jnp.bfloat16), back)
            key_part = dot_nn(score_back, query)
            query_part = dot_tn(score_back, keys)
            if member:
                key_sum[start : start + BLOCK, :] += key_part
                value_sum[start : start + BLOCK, :] += value_part
            else:
                key_sum[start : start + BLOCK, :] = key_part
                value_sum[start : start + BLOCK, :] = value_part
            if start:
                query_sum[member, start:, :] += query_part
            else:
                query_sum[member] = query_part
    query_back_ref[...] = (
        jnp.concatenate([query_sum[member] for member in range(group)], 1) * HEAD_DIM ** (-0.5)
    )
    key_back_ref[...] = jnp.concatenate([key_sum[...], value_sum[...]], 1)


def attend_back(fields, back, mixed, total, head, group):
    length = fields.shape[0]
    return pl.pallas_call(
        functools.partial(attend_back_kernel, head=head, group=group),
        out_shape=[
            jax.ShapeDtypeStruct((length, group * HEAD_DIM), jnp.float32),
            jax.ShapeDtypeStruct((length, 2 * HEAD_DIM), jnp.float32),
        ],
        in_specs=[pl.BlockSpec(memory_space=pltpu.VMEM)] * 4,
        out_specs=[pl.BlockSpec(memory_space=pltpu.VMEM)] * 2,
        scratch_shapes=[
            pltpu.VMEM((group, length, HEAD_DIM), jnp.bfloat16),
            pltpu.VMEM((group, length, HEAD_DIM), jnp.bfloat16),
            pltpu.VMEM((8, length), jnp.float32),
            pltpu.VMEM((group, 8, length), jnp.float32),
            pltpu.VMEM((group, length, HEAD_DIM), jnp.float32),
            pltpu.VMEM((length, HEAD_DIM), jnp.float32),
            pltpu.VMEM((length, HEAD_DIM), jnp.float32),
        ],
        compiler_params=pltpu.CompilerParams(vmem_limit_bytes=VMEM_LIMIT),
        cost_estimate=LIGHT,
        name="attend_back",
    )(fields, back, mixed, total)


def partner_of(tile):
    lane = lax.broadcasted_iota(jnp.int32, tile.shape, 1)
    half = HEAD_DIM // 2
    return jnp.where(
        lane % HEAD_DIM < half, pltpu.roll(tile, LANES - half, 1), pltpu.roll(tile, half, 1)
    )


def normed_rows(tokens_ref, gains_ref):
    resid = tokens_ref[...].astype(jnp.float32)
    inv_rms = lax.rsqrt(jnp.mean(resid * resid, 1, keepdims=True) + EPS)
    return resid, inv_rms, (resid * inv_rms * gains_ref[0:1, :]).astype(jnp.bfloat16)


def project_kernel(tokens_ref, gains_ref, wide_ref, cosine_ref, sine_ref, fields_ref, normed):
    _, _, normed[...] = normed_rows(tokens_ref, gains_ref)
    first_key = tiles_of(HEADS * HEAD_DIM)
    first_value = first_key + tiles_of(KV_HEADS * HEAD_DIM)
    count = fields_ref.shape[1] // LANES
    for start in range(0, count, 2):
        stop = min(start + 2, count)
        pair = dot_nn(normed[...], wide_ref[:, start * LANES : stop * LANES])
        for at in range(start, stop):
            tile = pair[:, (at - start) * LANES : (at - start + 1) * LANES]
            if at < first_value:
                tile = tile * cosine_ref[...] - partner_of(tile) * sine_ref[...]
            tile = tile.astype(jnp.bfloat16)
            if at < first_key:
                tile = (tile.astype(jnp.float32) * HEAD_DIM ** (-0.5)).astype(jnp.bfloat16)
            fields_ref[:, at * LANES : (at + 1) * LANES] = tile


def vmem_call(kernel, out_shape, scratch_shapes, name, *args):
    single = not isinstance(out_shape, list)
    return pl.pallas_call(
        kernel,
        out_shape=out_shape,
        in_specs=[pl.BlockSpec(memory_space=pltpu.VMEM)] * len(args),
        out_specs=pl.BlockSpec(memory_space=pltpu.VMEM)
        if single
        else [pl.BlockSpec(memory_space=pltpu.VMEM)] * len(out_shape),
        scratch_shapes=scratch_shapes,
        compiler_params=pltpu.CompilerParams(vmem_limit_bytes=VMEM_LIMIT),
        cost_estimate=LIGHT,
        name=name,
    )(*args)


def project(tokens, gains, wide, cosine, sine):
    return vmem_call(
        project_kernel,
        jax.ShapeDtypeStruct((tokens.shape[0], wide.shape[1]), jnp.bfloat16),
        [pltpu.VMEM(tokens.shape, jnp.bfloat16)],
        "project",
        tokens, gains, wide, cosine, sine,
    )


def finish_kernel(
    tokens_ref, gains_ref, wide_ref, cosine_ref, sine_ref, mid_back_ref, *refs, heads
):
    backs = refs[: 2 * heads]
    input_grad_ref, tiled_ref, gain_ref, fields, normed_t = refs[2 * heads :]
    half = HEAD_DIM
    group = HEADS // heads
    wide_heads = [(backs[2 * (at // group)], at % group * half) for at in range(HEADS)]
    wide_heads += [None] * (HEADS % 2)
    for offset in (0, half):
        wide_heads += [(backs[2 * at + 1], offset) for at in range(heads)] + [None] * (heads % 2)
    turned = tiles_of(HEADS * HEAD_DIM) + tiles_of(heads * HEAD_DIM)
    for at in range(len(wide_heads) // 2):
        cols = []
        for item in wide_heads[2 * at : 2 * at + 2]:
            if item is None:
                cols.append(jnp.zeros((fields.shape[0], half), jnp.float32))
            else:
                cols.append(item[0][:, item[1] : item[1] + half])
        tile = jnp.concatenate(cols, 1)
        if at < turned:
            tile = tile * cosine_ref[...] + partner_of(tile) * sine_ref[...]
        fields[:, at * LANES : (at + 1) * LANES] = tile.astype(jnp.bfloat16)
    resid, inv_rms, normed = normed_rows(tokens_ref, gains_ref)
    normed_t[...] = normed.T
    count = fields.shape[1] // LANES
    for start in range(0, count, 2):
        stop = min(start + 2, count)
        pair = dot_nn(normed_t[...], fields[:, start * LANES : stop * LANES])
        for at in range(start, stop):
            tiled_ref[at] = pair[:, (at - start) * LANES : (at - start + 1) * LANES]
    one_back = dot_nt(fields[...], wide_ref[...])
    weighted = one_back * gains_ref[0:1, :]
    cubed = inv_rms * inv_rms * inv_rms
    scaled = resid * inv_rms
    gain_ref[...] = jnp.sum(one_back * scaled, 0, keepdims=True)
    mean = jnp.mean(weighted * resid, 1, keepdims=True)
    grad = mid_back_ref[...] + inv_rms * weighted - resid * (cubed * mean)
    input_grad_ref[...] = grad.astype(jnp.bfloat16)


def finish(tokens, gains, wide, cosine, sine, mid_back, backs):
    heads = len(backs)
    rows, width = tokens.shape
    return vmem_call(
        functools.partial(finish_kernel, heads=heads),
        [
            jax.ShapeDtypeStruct(tokens.shape, jnp.bfloat16),
            jax.ShapeDtypeStruct((wide.shape[1] // LANES, width, LANES), jnp.float32),
            jax.ShapeDtypeStruct((1, width), jnp.float32),
        ],
        [
            pltpu.VMEM((rows, wide.shape[1]), jnp.bfloat16),
            pltpu.VMEM((width, rows), jnp.bfloat16),
        ],
        "finish",
        tokens, gains, wide, cosine, sine, mid_back, *[part for back in backs for part in back],
    )


def rotary_tables(length, head_dim):
    half_dim = head_dim // 2
    frequency = THETA ** (-(jnp.arange(half_dim, dtype=jnp.float32) * 2.0 / head_dim))
    angles = jnp.arange(length, dtype=jnp.float32)[:, None] * frequency[None, :]
    return (jnp.cos(angles), jnp.sin(angles))


def rotate_heads(field, cosine, sine):
    half_dim = field.shape[-1] // 2
    first_half = field[..., :half_dim]
    second_half = field[..., half_dim:]
    cosine = cosine[None, :, None, :]
    sine = sine[None, :, None, :]
    return jnp.concatenate(
        [first_half * cosine - second_half * sine, second_half * cosine + first_half * sine], -1
    )


def normalize(hidden, gain):
    inv_rms = lax.rsqrt(jnp.mean(hidden * hidden, -1, keepdims=True) + EPS)
    return (hidden * inv_rms * gain, inv_rms)


def normalize_back(grad, hidden, inv_rms, gain):
    weighted = grad * gain
    cubed = inv_rms * inv_rms * inv_rms
    hidden_grad = inv_rms * weighted - hidden * cubed * jnp.mean(
        weighted * hidden, -1, keepdims=True
    )
    gain_part = jnp.sum(grad * hidden * inv_rms, 0)
    return (hidden_grad, gain_part)


def outer_prod(left, right):
    return lax.dot_general(
        left, right, (((0,), (0,)), ((), ())), preferred_element_type=jnp.float32
    )


def times_transposed(left, matrix):
    return lax.dot_general(
        left, matrix, (((1,), (1,)), ((), ())), preferred_element_type=jnp.float32
    )


def whole_rows(shapes, devices):
    return (devices & (devices - 1)) == 0 and all(
        rows % (8 * devices // 4) == 0 and rows * wide % (devices * LANES) == 0
        for rows, wide in shapes
    )


def place_of():
    return lax.axis_index("dp").astype(jnp.int32).reshape(1)


class WeightGather:
    def __init__(self, shards, shapes, devices):
        self.shards, self.shapes, self.devices = shards, shapes, devices
        self.stages = whole_rows(shapes, devices)
        if self.stages:
            self.held = jnp.concatenate([shard.reshape(-1, LANES) for shard in shards])

    def line_stage(self, other):
        if not self.stages:
            return other
        _, line = masks_of(self.devices)
        self.held, other = tied(self.held, other)
        self.arrived = [self.held] + [swap(self.held, mask, self.devices) for mask in line[1:]]
        return other

    def plane_stage(self, other):
        if not self.stages:
            return other
        plane, _ = masks_of(self.devices)
        self.held, other = tied(jnp.stack(self.arrived), other)
        self.arrived = [self.held] + [swap(self.held, mask, self.devices) for mask in plane[1:]]
        return other

    def core_stage(self, other):
        if not self.stages:
            return other
        self.arrived, other = tied(self.arrived, other)
        self.got = [swap(field, CORE_MASK, self.devices) for field in self.arrived]
        return other

    def result(self, joined):
        if not self.stages:
            mats = [
                lax.all_gather(shard, "dp", axis=0, tiled=True).reshape(shape)
                for shard, shape in zip(self.shards, self.shapes)
            ]
            if not joined:
                return mats
            pads = [((0, 0), (0, tiles_of(mat.shape[1]) * LANES - mat.shape[1])) for mat in mats]
            return [jnp.concatenate([jnp.pad(mat, pad) for mat, pad in zip(mats, pads)], 1)]
        pieces = self.arrived + self.got
        return unpack_pieces(place_of(), pieces, self.shapes, self.devices, joined)


def tied(first, second):
    return lax.optimization_barrier((first, second))


class GradSum:
    def __init__(self, grads, shapes, devices, extra=None):
        self.grads, self.shapes, self.devices, self.extra = grads, shapes, devices, extra
        self.stages = whole_rows(shapes, devices)
        if self.stages:
            self.kept, self.sent = pack_grads(place_of(), grads, shapes, devices, extra)

    def core_stage(self, other):
        if not self.stages:
            return other
        (self.kept, self.sent), other = tied((self.kept, self.sent), other)
        self.got = swap(self.sent, CORE_MASK, self.devices)
        return other

    def plane_stage(self, other):
        if not self.stages:
            return other
        plane, _ = masks_of(self.devices)
        block = self.kept.shape[0] // len(plane)
        cuts = [slice(at * block, (at + 1) * block) for at in range(len(plane))]
        parts = [(widen(self.kept[cut]) + widen(self.got[cut])).astype(jnp.bfloat16) for cut in cuts]
        self.parts, other = tied(parts, other)
        self.arrived = [
            swap(part, mask, self.devices) for part, mask in zip(self.parts[1:], plane[1:])
        ]
        return other

    def line_stage(self, other):
        if not self.stages:
            return other
        _, line = masks_of(self.devices)
        terms = [self.parts[0]] + self.arrived
        parts = [
            tree_sum([widen(term[at]) for term in terms]).astype(jnp.bfloat16)
            for at in range(len(line))
        ]
        self.parts, other = tied(parts, other)
        self.arrived = [
            swap(part, mask, self.devices) for part, mask in zip(self.parts[1:], line[1:])
        ]
        return other

    def result(self):
        if not self.stages:
            grads = [
                grad.swapaxes(0, 1).reshape(rows, -1)[:, :wide] if grad.ndim == 3 else grad
                for grad, (rows, wide) in zip(self.grads, self.shapes)
            ]
            sums = [
                lax.psum_scatter(grad.reshape(-1), "dp", scatter_dimension=0, tiled=True)
                for grad in grads
            ]
            return sums if self.extra is None else sums + [lax.psum(self.extra, "dp")]
        pieces = tree_sum([widen(term) for term in [self.parts[0]] + self.arrived])
        sums, start = [], 0
        for rows, wide in self.shapes:
            count = rows * wide // (self.devices * LANES)
            sums.append(pieces[start : start + count].reshape(-1))
            start += count
        if self.extra is not None:
            count = self.extra.size // LANES
            sums.append(pieces[start : start + count].reshape(self.extra.shape))
        return sums


def body(tokens, cotangent, w_query, w_key, w_value, w_out, w_gate, w_up, w_down, norm_gains):
    model_width = tokens.shape[1]
    seq_count = tokens.shape[0] // LENGTH
    group_size = HEADS // KV_HEADS
    scale_factor = HEAD_DIM ** (-0.5)
    gain_f = norm_gains.astype(jnp.float32)
    shards = (w_query, w_key, w_value, w_out, w_gate, w_up, w_down)
    devices = lax.axis_size("dp")
    widths = [shards[at].shape[0] * devices // model_width for at in range(6)]
    shapes = [(model_width, wide) for wide in widths] + [
        (shards[6].shape[0] * devices // model_width, model_width)
    ]
    first = WeightGather(shards[:3], shapes[:3], devices)
    rest = (4, 5, 6, 3)
    second = WeightGather(
        [shards[at] for at in rest], [shapes[at] for at in rest], devices
    )
    tokens = first.line_stage(tokens)
    tokens = first.plane_stage(tokens)
    tokens = second.line_stage(tokens)
    tokens = first.core_stage(tokens)
    (wide_mat,) = first.result(True)
    resid_in = tokens.astype(jnp.float32)
    cosine, sine = rotary_tables(LENGTH, HEAD_DIM)
    pairs = LANES // HEAD_DIM
    cosine = jnp.tile(cosine, (seq_count, 2 * pairs))
    sine = jnp.tile(jnp.concatenate([sine, -sine], 1), (seq_count, pairs))
    fields = project(tokens, gain_f, wide_mat, cosine, sine)
    fields = second.plane_stage(fields)
    attended = [attend(fields, head, group_size) for head in range(2)]
    fields, attended = second.core_stage((fields, attended))
    attended.append(attend(fields, 2, group_size))
    wg_mat, wu_mat, wd_mat, wo_mat = second.result(False)
    mixed = jnp.concatenate([part for part, _ in attended], 1)
    attn_out = jnp.dot(mixed, wo_mat, preferred_element_type=jnp.float32)
    middle = resid_in + attn_out
    normed_two, rms_two = normalize(middle, gain_f[1])
    normed_two = normed_two.astype(jnp.bfloat16)
    gate = jnp.dot(normed_two, wg_mat, preferred_element_type=jnp.float32)
    upward = jnp.dot(normed_two, wu_mat, preferred_element_type=jnp.float32)
    sigmoid_g = jax.nn.sigmoid(gate)
    activated = gate * sigmoid_g
    hidden = (activated * upward).astype(jnp.bfloat16)
    ffn_out = jnp.dot(hidden, wd_mat, preferred_element_type=jnp.float32)
    output = (middle + ffn_out).astype(jnp.bfloat16)
    grad_down = outer_prod(hidden, cotangent)
    hidden_back = times_transposed(cotangent, wd_mat)
    gate_back = (hidden_back * upward * sigmoid_g * (1.0 + gate * (1.0 - sigmoid_g))).astype(
        jnp.bfloat16
    )
    up_back = (hidden_back * activated).astype(jnp.bfloat16)
    grad_gate = outer_prod(normed_two, gate_back)
    grad_up = outer_prod(normed_two, up_back)
    two_back = times_transposed(gate_back, wg_mat) + times_transposed(up_back, wu_mat)
    norm_two_back, gain_two = normalize_back(two_back, middle, rms_two, gain_f[1])
    mid_back = cotangent.astype(jnp.float32) + norm_two_back
    mid_low = mid_back.astype(jnp.bfloat16)
    grad_out = outer_prod(mixed, mid_low)
    mixed_back = times_transposed(mid_low, wo_mat).astype(jnp.bfloat16)
    feed_sum = GradSum((grad_gate, grad_up, grad_down), shapes[4:], devices)

    def back_of(head, field):
        part, total = attended[head]
        return attend_back(fields, field, part, total, head, group_size)

    mixed_back = feed_sum.core_stage(mixed_back)
    backs = [back_of(0, mixed_back)]
    mixed_back, _ = tied(mixed_back, backs[0])
    mixed_back = feed_sum.plane_stage(mixed_back)
    backs += [back_of(head, mixed_back) for head in range(1, KV_HEADS)]
    input_grad, tiled, gain_one = finish(tokens, gain_f, wide_mat, cosine, sine, mid_back, backs)
    input_grad, tiled = feed_sum.line_stage((input_grad, tiled))
    gains_back = jnp.concatenate([gain_one, gain_two[None]], 0)
    cuts = [0]
    for _, wide in shapes[:3]:
        cuts.append(cuts[-1] + tiles_of(wide))
    grads = tuple(tiled[start:stop] for start, stop in zip(cuts, cuts[1:])) + (grad_out,)
    mix_sum = GradSum(grads, shapes[:4], devices, gains_back)
    input_grad = mix_sum.core_stage(input_grad)
    input_grad = mix_sum.plane_stage(input_grad)
    input_grad = mix_sum.line_stage(input_grad)
    mix_parts = mix_sum.result()
    all_parts, gain_grad = mix_parts[:4] + feed_sum.result(), mix_parts[4]
    return (output, input_grad) + tuple(all_parts) + (gain_grad,)


def solution(mesh):
    return jax.shard_map(
        body,
        mesh=mesh,
        in_specs=(
            P("dp", None),
            P("dp", None),
            P("dp"),
            P("dp"),
            P("dp"),
            P("dp"),
            P("dp"),
            P("dp"),
            P("dp"),
            P(),
        ),
        out_specs=(
            P("dp", None),
            P("dp", None),
            P("dp"),
            P("dp"),
            P("dp"),
            P("dp"),
            P("dp"),
            P("dp"),
            P("dp"),
            P(),
        ),
        check_vma=False,
    )
```

```python
import functools

import jax
import jax.numpy as jnp
from jax import lax
from jax.experimental import pallas as pl
from jax.experimental.pallas import tpu as pltpu
from jax.sharding import PartitionSpec as P

HEADS = 9
KV_HEADS = 3
HEAD_DIM = 64
LENGTH = 1024


EPS = 1e-05
THETA = 100000.0
NEG_BIG = -1e30
LANES = 128
VMEM_LIMIT = 56 * 1024 * 1024
CORE_MASK = 1
LIGHT = pl.CostEstimate(flops=10**8, bytes_accessed=10**6, transcendentals=0)


def masks_of(devices):
    plane = tuple(2 * step for step in range(4))
    line = tuple(8 * step for step in range(devices // 8))
    return (plane, line)


def swap(field, mask, devices):
    return lax.ppermute(field, "dp", [(place, place ^ mask) for place in range(devices)])


def tree_sum(terms):
    while len(terms) > 1:
        terms = [terms[at] + terms[at + 1] for at in range(0, len(terms), 2)]
    return terms[0]


def widen(field):
    return field.astype(jnp.float32)


def slot_mask(core, slot, devices):
    line = devices // 8
    return core * CORE_MASK + 2 * (slot // line) + 8 * (slot % line)


def tiles_of(wide):
    return -(-wide // LANES)


def tile_widths(wide):
    return [min(LANES, wide - at) for at in range(0, wide, LANES)]


def flat_starts(shapes, devices):
    starts = [0]
    for rows, wide in shapes:
        starts.append(starts[-1] + rows * wide // (devices * LANES))
    return starts


def tiled_shapes(shapes):
    return [(tiles_of(wide), rows, LANES) for rows, wide in shapes if wide % LANES]


def unpack_kernel(place_ref, *refs, devices, shapes, joined, count):
    pieces, refs = refs[:count], refs[count:]
    out_count = 1 if joined else len(shapes)
    outs, flats, refs = refs[:out_count], refs[out_count : out_count + len(shapes)], refs[out_count + len(shapes) :]
    stage, landed, arrival, tiled_refs = refs[0], refs[1], refs[2], list(refs[3:])
    place = place_ref[0]
    starts = flat_starts(shapes, devices)
    block = pieces[0].shape[0]
    copies = [
        pltpu.make_async_copy(piece, landed.at[index], arrival.at[index])
        for index, piece in enumerate(pieces)
    ]
    for copy in copies:
        copy.start()
    for index in range(count):
        copies[index].wait()
        piece_ref = landed.at[index]
        core, plane = index * block * 2 // devices, index % (devices // 2 // block)

        def load(slot, carry, core=core, plane=plane, piece_ref=piece_ref):
            owner = place ^ slot_mask(core, plane * block + slot, devices)
            piece = piece_ref[slot].astype(jnp.float32)
            if any(start % 8 for start in starts[:-1]):
                stage[slot % 4] = piece
            for flat, start, stop in zip(flats, starts, starts[1:]):
                each = stop - start
                rows = stage[slot % 4, start:stop, :] if start % 8 else piece[start:stop]
                flat[pl.ds(owner * each, each), :] = rows
            return carry

        lax.fori_loop(0, block, load, 0)
    column = 0
    for index, ((rows, wide), flat) in enumerate(zip(shapes, flats)):
        out = outs[0 if joined else index]
        whole = wide // LANES
        if wide % LANES == 0:
            for at in range(whole):
                tile = flat[pl.ds(at, rows, stride=whole), :]
                out[:, column + at * LANES : column + (at + 1) * LANES] = tile.astype(jnp.bfloat16)
        else:
            target = tiled_refs.pop(0)
            pairs, tiles_in = rows // 2, 2 * wide // LANES
            for at in range(whole + 1):
                target[at, pl.ds(0, pairs, stride=2), :] = flat[pl.ds(at, pairs, stride=tiles_in), :]
            rolled = None
            for at in range(whole, tiles_in):
                after = pltpu.roll(flat[pl.ds(at, pairs, stride=tiles_in), :], LANES // 2, 1)
                if rolled is not None:
                    lane = lax.broadcasted_iota(jnp.int32, after.shape, 1)
                    target[at - whole - 1, pl.ds(1, pairs, stride=2), :] = jnp.where(
                        lane < LANES // 2, rolled, after
                    )
                rolled = after
            target[whole, pl.ds(1, pairs, stride=2), :] = rolled
            for at, width in enumerate(tile_widths(wide)):
                tile = target[at]
                if joined and width < LANES:
                    lane = lax.broadcasted_iota(jnp.int32, tile.shape, 1)
                    tile = jnp.where(lane < width, tile, 0.0)
                    width = LANES
                start = column + at * LANES
                out[:, start : start + width] = tile[:, :width].astype(jnp.bfloat16)
        if joined:
            column += tiles_of(wide) * LANES


def unpack_pieces(place, pieces, shapes, devices, joined):
    rows_in = pieces[0].shape[1]
    outs = shapes
    if joined:
        outs = [(shapes[0][0], sum(tiles_of(wide) for _, wide in shapes) * LANES)]
    return pl.pallas_call(
        functools.partial(
            unpack_kernel, devices=devices, shapes=shapes, joined=joined, count=len(pieces)
        ),
        out_shape=[jax.ShapeDtypeStruct(shape, jnp.bfloat16) for shape in outs],
        in_specs=[pl.BlockSpec(memory_space=pltpu.SMEM)]
        + [pl.BlockSpec(memory_space=pl.ANY)] * len(pieces),
        out_specs=[pl.BlockSpec(memory_space=pltpu.VMEM)] * len(outs),
        scratch_shapes=[
            pltpu.VMEM((rows * wide // LANES, LANES), jnp.float32) for rows, wide in shapes
        ]
        + [
            pltpu.VMEM((4, rows_in, LANES), jnp.float32),
            pltpu.VMEM((len(pieces),) + pieces[0].shape, jnp.bfloat16),
            pltpu.SemaphoreType.DMA((len(pieces),)),
        ]
        + [pltpu.VMEM(shape, jnp.float32) for shape in tiled_shapes(shapes)],
        compiler_params=pltpu.CompilerParams(vmem_limit_bytes=VMEM_LIMIT),
        cost_estimate=LIGHT,
        name="unpack",
    )(place, *pieces)


def pack_kernel(place_ref, *refs, devices, shapes, tiled_in, extra):
    count = len(shapes) + (1 if extra else 0)
    sources, kept_ref, sent_ref, stage = refs[:count], refs[count], refs[count + 1], refs[count + 2]
    flats = refs[count + 3 : count + 3 + len(shapes)]
    tiled_refs = list(refs[count + 3 + len(shapes) :])
    place = place_ref[0]
    starts = flat_starts(shapes, devices)
    for index, ((rows, wide), flat) in enumerate(zip(shapes, flats)):
        source, whole = sources[index], wide // LANES
        if wide % LANES == 0:
            for at in range(whole):
                flat[pl.ds(at, rows, stride=whole), :] = (
                    source[at] if tiled_in[index] else source[:, at * LANES : (at + 1) * LANES]
                )
            continue
        if not tiled_in[index]:
            tiled = tiled_refs.pop(0)
            for at, width in enumerate(tile_widths(wide)):
                tiled[at, :, :width] = source[:, at * LANES : at * LANES + width]
            source = tiled
        pairs, tiles_in = rows // 2, 2 * wide // LANES
        for at in range(whole):
            flat[pl.ds(at, pairs, stride=tiles_in), :] = source[at, pl.ds(0, pairs, stride=2), :]
        before = source[whole, pl.ds(0, pairs, stride=2), :]
        lane = lax.broadcasted_iota(jnp.int32, before.shape, 1)
        for at in range(whole + 1):
            rolled = pltpu.roll(source[at, pl.ds(1, pairs, stride=2), :], LANES // 2, 1)
            flat[pl.ds(whole + at, pairs, stride=tiles_in), :] = jnp.where(
                lane < LANES // 2, before, rolled
            )
            before = rolled
    row_tiles = []
    if extra:
        row = jnp.concatenate([sources[-1][at : at + 1, :] for at in range(extra[0])], 1)
        row_tiles = [
            row[:, at * LANES : (at + 1) * LANES] for at in range(extra[0] * extra[1] // LANES)
        ]
    direct = not extra and all(start % 8 == 0 for start in starts)
    if not direct:
        for at in range(4):
            for index, tile in enumerate(row_tiles):
                stage[at, starts[-1] + index : starts[-1] + index + 1, :] = tile
            used = starts[-1] + len(row_tiles)
            if used < stage.shape[1]:
                stage[at, used:, :] = jnp.zeros((stage.shape[1] - used, LANES), jnp.float32)
    for core, pieces in enumerate((kept_ref, sent_ref)):

        def store(slot, carry, core=core, pieces=pieces):
            owner = place ^ slot_mask(core, slot, devices)
            parts = []
            for flat, start, stop in zip(flats, starts, starts[1:]):
                rows = flat[pl.ds(owner * (stop - start), stop - start), :]
                if direct:
                    parts.append(rows)
                else:
                    stage[slot % 4, start:stop, :] = rows
            spare = stage.shape[1] - starts[-1]
            if direct and spare:
                parts.append(jnp.zeros((spare, LANES), jnp.float32))
            piece = jnp.concatenate(parts, 0) if direct else stage[slot % 4]
            pieces[slot] = piece.astype(jnp.bfloat16)
            return carry

        lax.fori_loop(0, devices // 2, store, 0)


def pack_grads(place, grads, shapes, devices, extra):
    rows_out = sum(rows * wide for rows, wide in shapes) // (devices * LANES)
    sources = list(grads)
    if extra is not None:
        rows_out += extra.size // LANES
        sources.append(extra)
    rows_out = -(-rows_out // 16) * 16
    tiled_in = tuple(grad.ndim == 3 for grad in grads)
    half = jax.ShapeDtypeStruct((devices // 2, rows_out, LANES), jnp.bfloat16)
    untiled = [shape for shape, tiled in zip(shapes, tiled_in) if not tiled]
    return pl.pallas_call(
        functools.partial(
            pack_kernel, devices=devices, shapes=shapes, tiled_in=tiled_in,
            extra=None if extra is None else extra.shape,
        ),
        out_shape=[half, half],
        in_specs=[pl.BlockSpec(memory_space=pltpu.SMEM)]
        + [pl.BlockSpec(memory_space=pltpu.VMEM)] * len(sources),
        out_specs=[pl.BlockSpec(memory_space=pltpu.VMEM)] * 2,
        scratch_shapes=[pltpu.VMEM((4, rows_out, LANES), jnp.float32)]
        + [pltpu.VMEM((rows * wide // LANES, LANES), jnp.float32) for rows, wide in shapes]
        + [pltpu.VMEM(shape, jnp.float32) for shape in tiled_shapes(untiled)],
        compiler_params=pltpu.CompilerParams(vmem_limit_bytes=VMEM_LIMIT),
        cost_estimate=LIGHT,
        name="pack",
    )(place, *sources)


BLOCK = 256


def dot_nt(left, right):
    return lax.dot_general(
        left, right, (((1,), (1,)), ((), ())), preferred_element_type=jnp.float32
    )


def dot_tn(left, right):
    return lax.dot_general(
        left, right, (((0,), (0,)), ((), ())), preferred_element_type=jnp.float32
    )


def dot_nn(left, right):
    return jnp.dot(left, right, preferred_element_type=jnp.float32)


def key_columns(head):
    first = tiles_of(HEADS * HEAD_DIM) * LANES + head * HEAD_DIM
    return slice(first, first + HEAD_DIM)


def value_columns(head):
    first = (tiles_of(HEADS * HEAD_DIM) + tiles_of(KV_HEADS * HEAD_DIM)) * LANES + head * HEAD_DIM
    return slice(first, first + HEAD_DIM)


def attend_kernel(fields_ref, mixed_ref, total_ref, *, head, group):
    length = fields_ref.shape[0]
    keys = fields_ref[:, key_columns(head)]
    values = fields_ref[:, value_columns(head)]
    lower = lax.broadcasted_iota(jnp.int32, (BLOCK, BLOCK), 0) >= lax.broadcasted_iota(
        jnp.int32, (BLOCK, BLOCK), 1
    )
    lane = lax.broadcasted_iota(jnp.int32, (BLOCK, LANES), 1)
    for start in range(0, length, BLOCK):
        mixed, totals_row = [], jnp.zeros((BLOCK, LANES), jnp.float32)
        for member in range(group):
            at = (head * group + member) * HEAD_DIM
            query = fields_ref[start : start + BLOCK, at : at + HEAD_DIM]
            diagonal = jnp.where(lower, dot_nt(query, keys[start : start + BLOCK]), NEG_BIG)
            maxima = jnp.max(diagonal, 1, keepdims=True)
            if start:
                before = dot_nt(query, keys[:start])
                maxima = jnp.maximum(maxima, jnp.max(before, 1, keepdims=True))
            expo = jnp.exp(diagonal - maxima)
            totals = jnp.sum(expo, 1, keepdims=True)
            result = dot_nn(expo.astype(jnp.bfloat16), values[start : start + BLOCK])
            if start:
                expo = jnp.exp(before - maxima)
                totals = totals + jnp.sum(expo, 1, keepdims=True)
                result = result + dot_nn(expo.astype(jnp.bfloat16), values[:start])
            mixed.append(result / totals)
            totals_row = jnp.where(lane == member, maxima + jnp.log(totals), totals_row)
        mixed_ref[start : start + BLOCK, :] = jnp.concatenate(mixed, 1).astype(jnp.bfloat16)
        total_ref[start : start + BLOCK, :] = totals_row


def attend(fields, head, group):
    length = fields.shape[0]
    return pl.pallas_call(
        functools.partial(attend_kernel, head=head, group=group),
        out_shape=[
            jax.ShapeDtypeStruct((length, group * HEAD_DIM), jnp.bfloat16),
            jax.ShapeDtypeStruct((length, LANES), jnp.float32),
        ],
        in_specs=[pl.BlockSpec(memory_space=pltpu.VMEM)],
        out_specs=[pl.BlockSpec(memory_space=pltpu.VMEM)] * 2,
        compiler_params=pltpu.CompilerParams(vmem_limit_bytes=VMEM_LIMIT),
        cost_estimate=LIGHT,
        name="attend",
    )(fields)


def attend_back_kernel(
    fields_ref, back_ref, mixed_ref, total_ref,
    query_back_ref, key_back_ref, queries, backs, totals, deltas, query_sum, key_sum, value_sum,
    *, head, group,
):
    length = fields_ref.shape[0]
    ones = jnp.ones((8, HEAD_DIM), jnp.float32)
    totals[...] = total_ref[...].T[:8]
    for member in range(group):
        at = (head * group + member) * HEAD_DIM
        queries[member] = fields_ref[:, at : at + HEAD_DIM]
        back = back_ref[:, at : at + HEAD_DIM]
        backs[member] = back
        product = back.astype(jnp.float32) * mixed_ref[
            :, member * HEAD_DIM : (member + 1) * HEAD_DIM
        ].astype(jnp.float32)
        deltas[member] = lax.dot_general(
            ones, product, (((1,), (1,)), ((), ())),
            precision=lax.Precision.HIGHEST, preferred_element_type=jnp.float32,
        )
    keys_all = fields_ref[:, key_columns(head)]
    values_all = fields_ref[:, value_columns(head)]
    upper = lax.broadcasted_iota(jnp.int32, (BLOCK, BLOCK), 0) <= lax.broadcasted_iota(
        jnp.int32, (BLOCK, BLOCK), 1
    )
    for member in range(group):
        total_row = totals[member : member + 1, :]
        delta_row = deltas[member][0:1]
        for start in range(0, length, BLOCK):
            keys = keys_all[start : start + BLOCK]
            values = values_all[start : start + BLOCK]
            query = queries[member, start:, :]
            back = backs[member, start:, :]
            scores = dot_nt(keys, query)
            probs = jnp.exp(scores - total_row[:, start:])
            first = jnp.where(upper, probs[:, :BLOCK], 0.0)
            probs = first if start + BLOCK == length else jnp.concatenate(
                [first, probs[:, BLOCK:]], 1
            )
            prob_back = dot_nt(values, back)
            score_back = (probs * (prob_back - delta_row[:, start:])).astype(jnp.bfloat16)
            value_part = dot_nn(probs.astype(jnp.bfloat16), back)
            key_part = dot_nn(score_back, query)
            query_part = dot_tn(score_back, keys)
            if member:
                key_sum[start : start + BLOCK, :] += key_part
                value_sum[start : start + BLOCK, :] += value_part
            else:
                key_sum[start : start + BLOCK, :] = key_part
                value_sum[start : start + BLOCK, :] = value_part
            if start:
                query_sum[member, start:, :] += query_part
            else:
                query_sum[member] = query_part
    query_back_ref[...] = (
        jnp.concatenate([query_sum[member] for member in range(group)], 1) * HEAD_DIM ** (-0.5)
    )
    key_back_ref[...] = jnp.concatenate([key_sum[...], value_sum[...]], 1)


def attend_back(fields, back, mixed, total, head, group):
    length = fields.shape[0]
    return pl.pallas_call(
        functools.partial(attend_back_kernel, head=head, group=group),
        out_shape=[
            jax.ShapeDtypeStruct((length, group * HEAD_DIM), jnp.float32),
            jax.ShapeDtypeStruct((length, 2 * HEAD_DIM), jnp.float32),
        ],
        in_specs=[pl.BlockSpec(memory_space=pltpu.VMEM)] * 4,
        out_specs=[pl.BlockSpec(memory_space=pltpu.VMEM)] * 2,
        scratch_shapes=[
            pltpu.VMEM((group, length, HEAD_DIM), jnp.bfloat16),
            pltpu.VMEM((group, length, HEAD_DIM), jnp.bfloat16),
            pltpu.VMEM((8, length), jnp.float32),
            pltpu.VMEM((group, 8, length), jnp.float32),
            pltpu.VMEM((group, length, HEAD_DIM), jnp.float32),
            pltpu.VMEM((length, HEAD_DIM), jnp.float32),
            pltpu.VMEM((length, HEAD_DIM), jnp.float32),
        ],
        compiler_params=pltpu.CompilerParams(vmem_limit_bytes=VMEM_LIMIT),
        cost_estimate=LIGHT,
        name="attend_back",
    )(fields, back, mixed, total)


def partner_of(tile):
    lane = lax.broadcasted_iota(jnp.int32, tile.shape, 1)
    half = HEAD_DIM // 2
    return jnp.where(
        lane % HEAD_DIM < half, pltpu.roll(tile, LANES - half, 1), pltpu.roll(tile, half, 1)
    )


def normed_rows(tokens_ref, gains_ref):
    resid = tokens_ref[...].astype(jnp.float32)
    inv_rms = lax.rsqrt(jnp.mean(resid * resid, 1, keepdims=True) + EPS)
    return resid, inv_rms, (resid * inv_rms * gains_ref[0:1, :]).astype(jnp.bfloat16)


def project_kernel(tokens_ref, gains_ref, wide_ref, cosine_ref, sine_ref, fields_ref, normed):
    _, _, normed[...] = normed_rows(tokens_ref, gains_ref)
    first_key = tiles_of(HEADS * HEAD_DIM)
    first_value = first_key + tiles_of(KV_HEADS * HEAD_DIM)
    count = fields_ref.shape[1] // LANES
    for start in range(0, count, 2):
        stop = min(start + 2, count)
        pair = dot_nn(normed[...], wide_ref[:, start * LANES : stop * LANES])
        for at in range(start, stop):
            tile = pair[:, (at - start) * LANES : (at - start + 1) * LANES]
            if at < first_value:
                tile = tile * cosine_ref[...] - partner_of(tile) * sine_ref[...]
            tile = tile.astype(jnp.bfloat16)
            if at < first_key:
                tile = (tile.astype(jnp.float32) * HEAD_DIM ** (-0.5)).astype(jnp.bfloat16)
            fields_ref[:, at * LANES : (at + 1) * LANES] = tile


def vmem_call(kernel, out_shape, scratch_shapes, name, *args):
    single = not isinstance(out_shape, list)
    return pl.pallas_call(
        kernel,
        out_shape=out_shape,
        in_specs=[pl.BlockSpec(memory_space=pltpu.VMEM)] * len(args),
        out_specs=pl.BlockSpec(memory_space=pltpu.VMEM)
        if single
        else [pl.BlockSpec(memory_space=pltpu.VMEM)] * len(out_shape),
        scratch_shapes=scratch_shapes,
        compiler_params=pltpu.CompilerParams(vmem_limit_bytes=VMEM_LIMIT),
        cost_estimate=LIGHT,
        name=name,
    )(*args)


def project(tokens, gains, wide, cosine, sine):
    return vmem_call(
        project_kernel,
        jax.ShapeDtypeStruct((tokens.shape[0], wide.shape[1]), jnp.bfloat16),
        [pltpu.VMEM(tokens.shape, jnp.bfloat16)],
        "project",
        tokens, gains, wide, cosine, sine,
    )


def finish_kernel(
    tokens_ref, gains_ref, wide_ref, cosine_ref, sine_ref, mid_back_ref, *refs, heads
):
    backs = refs[: 2 * heads]
    input_grad_ref, tiled_ref, gain_ref, fields, normed_t = refs[2 * heads :]
    half = HEAD_DIM
    group = HEADS // heads
    wide_heads = [(backs[2 * (at // group)], at % group * half) for at in range(HEADS)]
    wide_heads += [None] * (HEADS % 2)
    for offset in (0, half):
        wide_heads += [(backs[2 * at + 1], offset) for at in range(heads)] + [None] * (heads % 2)
    turned = tiles_of(HEADS * HEAD_DIM) + tiles_of(heads * HEAD_DIM)
    for at in range(len(wide_heads) // 2):
        cols = []
        for item in wide_heads[2 * at : 2 * at + 2]:
            if item is None:
                cols.append(jnp.zeros((fields.shape[0], half), jnp.float32))
            else:
                cols.append(item[0][:, item[1] : item[1] + half])
        tile = jnp.concatenate(cols, 1)
        if at < turned:
            tile = tile * cosine_ref[...] + partner_of(tile) * sine_ref[...]
        fields[:, at * LANES : (at + 1) * LANES] = tile.astype(jnp.bfloat16)
    resid, inv_rms, normed = normed_rows(tokens_ref, gains_ref)
    normed_t[...] = normed.T
    count = fields.shape[1] // LANES
    for start in range(0, count, 2):
        stop = min(start + 2, count)
        pair = dot_nn(normed_t[...], fields[:, start * LANES : stop * LANES])
        for at in range(start, stop):
            tiled_ref[at] = pair[:, (at - start) * LANES : (at - start + 1) * LANES]
    one_back = dot_nt(fields[...], wide_ref[...])
    weighted = one_back * gains_ref[0:1, :]
    cubed = inv_rms * inv_rms * inv_rms
    scaled = resid * inv_rms
    gain_ref[...] = jnp.sum(one_back * scaled, 0, keepdims=True)
    mean = jnp.mean(weighted * resid, 1, keepdims=True)
    grad = mid_back_ref[...] + inv_rms * weighted - resid * (cubed * mean)
    input_grad_ref[...] = grad.astype(jnp.bfloat16)


def finish(tokens, gains, wide, cosine, sine, mid_back, backs):
    heads = len(backs)
    rows, width = tokens.shape
    return vmem_call(
        functools.partial(finish_kernel, heads=heads),
        [
            jax.ShapeDtypeStruct(tokens.shape, jnp.bfloat16),
            jax.ShapeDtypeStruct((wide.shape[1] // LANES, width, LANES), jnp.float32),
            jax.ShapeDtypeStruct((1, width), jnp.float32),
        ],
        [
            pltpu.VMEM((rows, wide.shape[1]), jnp.bfloat16),
            pltpu.VMEM((width, rows), jnp.bfloat16),
        ],
        "finish",
        tokens, gains, wide, cosine, sine, mid_back, *[part for back in backs for part in back],
    )


def rotary_tables(length, head_dim):
    half_dim = head_dim // 2
    frequency = THETA ** (-(jnp.arange(half_dim, dtype=jnp.float32) * 2.0 / head_dim))
    angles = jnp.arange(length, dtype=jnp.float32)[:, None] * frequency[None, :]
    return (jnp.cos(angles), jnp.sin(angles))


def rotate_heads(field, cosine, sine):
    half_dim = field.shape[-1] // 2
    first_half = field[..., :half_dim]
    second_half = field[..., half_dim:]
    cosine = cosine[None, :, None, :]
    sine = sine[None, :, None, :]
    return jnp.concatenate(
        [first_half * cosine - second_half * sine, second_half * cosine + first_half * sine], -1
    )


def normalize(hidden, gain):
    inv_rms = lax.rsqrt(jnp.mean(hidden * hidden, -1, keepdims=True) + EPS)
    return (hidden * inv_rms * gain, inv_rms)


def normalize_back(grad, hidden, inv_rms, gain):
    weighted = grad * gain
    cubed = inv_rms * inv_rms * inv_rms
    hidden_grad = inv_rms * weighted - hidden * cubed * jnp.mean(
        weighted * hidden, -1, keepdims=True
    )
    gain_part = jnp.sum(grad * hidden * inv_rms, 0)
    return (hidden_grad, gain_part)


def outer_prod(left, right):
    return lax.dot_general(
        left, right, (((0,), (0,)), ((), ())), preferred_element_type=jnp.float32
    )


def times_transposed(left, matrix):
    return lax.dot_general(
        left, matrix, (((1,), (1,)), ((), ())), preferred_element_type=jnp.float32
    )


def whole_rows(shapes, devices):
    return (devices & (devices - 1)) == 0 and all(
        rows % (8 * devices // 4) == 0 and rows * wide % (devices * LANES) == 0
        for rows, wide in shapes
    )


def place_of():
    return lax.axis_index("dp").astype(jnp.int32).reshape(1)


class WeightGather:
    def __init__(self, shards, shapes, devices):
        self.shards, self.shapes, self.devices = shards, shapes, devices
        self.stages = whole_rows(shapes, devices)
        if self.stages:
            held = jnp.concatenate([shard.reshape(-1, LANES) for shard in shards])
            self.held = jnp.pad(held, ((0, -held.shape[0] % 16), (0, 0)))

    def line_stage(self, other):
        if not self.stages:
            return other
        _, line = masks_of(self.devices)
        self.held, other = tied(self.held, other)
        self.arrived = [self.held] + [swap(self.held, mask, self.devices) for mask in line[1:]]
        return other

    def plane_stage(self, other):
        if not self.stages:
            return other
        plane, _ = masks_of(self.devices)
        self.held, other = tied(jnp.stack(self.arrived), other)
        self.arrived = [self.held] + [swap(self.held, mask, self.devices) for mask in plane[1:]]
        return other

    def core_stage(self, other, joined):
        if not self.stages:
            return other
        self.arrived, other = tied(self.arrived, other)
        if joined:
            self.arrived = [jnp.concatenate(self.arrived)]
        self.got = [swap(field, CORE_MASK, self.devices) for field in self.arrived]
        return other

    def result(self, joined):
        if not self.stages:
            mats = [
                lax.all_gather(shard, "dp", axis=0, tiled=True).reshape(shape)
                for shard, shape in zip(self.shards, self.shapes)
            ]
            if not joined:
                return mats
            pads = [((0, 0), (0, tiles_of(mat.shape[1]) * LANES - mat.shape[1])) for mat in mats]
            return [jnp.concatenate([jnp.pad(mat, pad) for mat, pad in zip(mats, pads)], 1)]
        pieces = self.arrived + self.got
        return unpack_pieces(place_of(), pieces, self.shapes, self.devices, joined)


def tied(first, second):
    return lax.optimization_barrier((first, second))


class GradSum:
    def __init__(self, grads, shapes, devices, extra=None):
        self.grads, self.shapes, self.devices, self.extra = grads, shapes, devices, extra
        self.stages = whole_rows(shapes, devices)
        if self.stages:
            self.kept, self.sent = pack_grads(place_of(), grads, shapes, devices, extra)

    def core_stage(self, other):
        if not self.stages:
            return other
        (self.kept, self.sent), other = tied((self.kept, self.sent), other)
        self.got = swap(self.sent, CORE_MASK, self.devices)
        return other

    def plane_stage(self, other):
        if not self.stages:
            return other
        plane, _ = masks_of(self.devices)
        block = self.kept.shape[0] // len(plane)
        cuts = [slice(at * block, (at + 1) * block) for at in range(len(plane))]
        parts = [(widen(self.kept[cut]) + widen(self.got[cut])).astype(jnp.bfloat16) for cut in cuts]
        self.parts, other = tied(parts, other)
        self.arrived = [
            swap(part, mask, self.devices) for part, mask in zip(self.parts[1:], plane[1:])
        ]
        return other

    def line_stage(self, other):
        if not self.stages:
            return other
        _, line = masks_of(self.devices)
        terms = [self.parts[0]] + self.arrived
        parts = [
            tree_sum([widen(term[at]) for term in terms]).astype(jnp.bfloat16)
            for at in range(len(line))
        ]
        self.parts, other = tied(parts, other)
        self.arrived = [
            swap(part, mask, self.devices) for part, mask in zip(self.parts[1:], line[1:])
        ]
        return other

    def result(self):
        if not self.stages:
            grads = [
                grad.swapaxes(0, 1).reshape(rows, -1)[:, :wide] if grad.ndim == 3 else grad
                for grad, (rows, wide) in zip(self.grads, self.shapes)
            ]
            sums = [
                lax.psum_scatter(grad.reshape(-1), "dp", scatter_dimension=0, tiled=True)
                for grad in grads
            ]
            return sums if self.extra is None else sums + [lax.psum(self.extra, "dp")]
        pieces = tree_sum([widen(term) for term in [self.parts[0]] + self.arrived])
        sums, start = [], 0
        for rows, wide in self.shapes:
            count = rows * wide // (self.devices * LANES)
            sums.append(pieces[start : start + count].reshape(-1))
            start += count
        if self.extra is not None:
            count = self.extra.size // LANES
            sums.append(pieces[start : start + count].reshape(self.extra.shape))
        return sums


def body(tokens, cotangent, w_query, w_key, w_value, w_out, w_gate, w_up, w_down, norm_gains):
    model_width = tokens.shape[1]
    seq_count = tokens.shape[0] // LENGTH
    group_size = HEADS // KV_HEADS
    scale_factor = HEAD_DIM ** (-0.5)
    gain_f = norm_gains.astype(jnp.float32)
    shards = (w_query, w_key, w_value, w_out, w_gate, w_up, w_down)
    devices = lax.axis_size("dp")
    widths = [shards[at].shape[0] * devices // model_width for at in range(6)]
    shapes = [(model_width, wide) for wide in widths] + [
        (shards[6].shape[0] * devices // model_width, model_width)
    ]
    first = WeightGather(shards[:3], shapes[:3], devices)
    rest = (4, 5, 6, 3)
    second = WeightGather(
        [shards[at] for at in rest], [shapes[at] for at in rest], devices
    )
    tokens = first.line_stage(tokens)
    tokens = first.plane_stage(tokens)
    tokens = second.line_stage(tokens)
    tokens = first.core_stage(tokens, True)
    if first.stages:
        first.got = second.plane_stage(first.got)
    (wide_mat,) = first.result(True)
    resid_in = tokens.astype(jnp.float32)
    cosine, sine = rotary_tables(LENGTH, HEAD_DIM)
    pairs = LANES // HEAD_DIM
    cosine = jnp.tile(cosine, (seq_count, 2 * pairs))
    sine = jnp.tile(jnp.concatenate([sine, -sine], 1), (seq_count, pairs))
    fields = project(tokens, gain_f, wide_mat, cosine, sine)
    attended = [attend(fields, head, group_size) for head in range(2)]
    fields, attended = second.core_stage((fields, attended), False)
    attended.append(attend(fields, 2, group_size))
    wg_mat, wu_mat, wd_mat, wo_mat = second.result(False)
    mixed = jnp.concatenate([part for part, _ in attended], 1)
    attn_out = jnp.dot(mixed, wo_mat, preferred_element_type=jnp.float32)
    middle = resid_in + attn_out
    normed_two, rms_two = normalize(middle, gain_f[1])
    normed_two = normed_two.astype(jnp.bfloat16)
    gate = jnp.dot(normed_two, wg_mat, preferred_element_type=jnp.float32)
    upward = jnp.dot(normed_two, wu_mat, preferred_element_type=jnp.float32)
    sigmoid_g = jax.nn.sigmoid(gate)
    activated = gate * sigmoid_g
    hidden = (activated * upward).astype(jnp.bfloat16)
    ffn_out = jnp.dot(hidden, wd_mat, preferred_element_type=jnp.float32)
    output = (middle + ffn_out).astype(jnp.bfloat16)
    grad_down = outer_prod(hidden, cotangent)
    hidden_back = times_transposed(cotangent, wd_mat)
    gate_back = (hidden_back * upward * sigmoid_g * (1.0 + gate * (1.0 - sigmoid_g))).astype(
        jnp.bfloat16
    )
    up_back = (hidden_back * activated).astype(jnp.bfloat16)
    grad_gate = outer_prod(normed_two, gate_back)
    grad_up = outer_prod(normed_two, up_back)
    two_back = times_transposed(gate_back, wg_mat) + times_transposed(up_back, wu_mat)
    norm_two_back, gain_two = normalize_back(two_back, middle, rms_two, gain_f[1])
    mid_back = cotangent.astype(jnp.float32) + norm_two_back
    mid_low = mid_back.astype(jnp.bfloat16)
    grad_out = outer_prod(mixed, mid_low)
    mixed_back = times_transposed(mid_low, wo_mat).astype(jnp.bfloat16)
    feed_sum = GradSum(
        (grad_gate, grad_up, grad_down, grad_out), [shapes[at] for at in rest], devices
    )

    def back_of(head, field):
        part, total = attended[head]
        return attend_back(fields, field, part, total, head, group_size)

    mixed_back = feed_sum.core_stage(mixed_back)
    backs = [back_of(0, mixed_back)]
    mixed_back, _ = tied(mixed_back, backs[0])
    mixed_back = feed_sum.plane_stage(mixed_back)
    backs += [back_of(head, mixed_back) for head in range(1, KV_HEADS)]
    input_grad, tiled, gain_one = finish(tokens, gain_f, wide_mat, cosine, sine, mid_back, backs)
    input_grad, tiled = feed_sum.line_stage((input_grad, tiled))
    gains_back = jnp.concatenate([gain_one, gain_two[None]], 0)
    cuts = [0]
    for _, wide in shapes[:3]:
        cuts.append(cuts[-1] + tiles_of(wide))
    grads = tuple(tiled[start:stop] for start, stop in zip(cuts, cuts[1:]))
    mix_sum = GradSum(grads, shapes[:3], devices, gains_back)
    input_grad = mix_sum.core_stage(input_grad)
    input_grad = mix_sum.plane_stage(input_grad)
    input_grad = mix_sum.line_stage(input_grad)
    mix_parts = mix_sum.result()
    gate_part, up_part, down_part, out_part = feed_sum.result()
    all_parts = mix_parts[:3] + [out_part, gate_part, up_part, down_part]
    gain_grad = mix_parts[3]
    return (output, input_grad) + tuple(all_parts) + (gain_grad,)


def solution(mesh):
    return jax.shard_map(
        body,
        mesh=mesh,
        in_specs=(
            P("dp", None),
            P("dp", None),
            P("dp"),
            P("dp"),
            P("dp"),
            P("dp"),
            P("dp"),
            P("dp"),
            P("dp"),
            P(),
        ),
        out_specs=(
            P("dp", None),
            P("dp", None),
            P("dp"),
            P("dp"),
            P("dp"),
            P("dp"),
            P("dp"),
            P("dp"),
            P("dp"),
            P(),
        ),
        check_vma=False,
    )
```

```python
import functools

import jax
import jax.numpy as jnp
from jax import lax
from jax.experimental import pallas as pl
from jax.experimental.pallas import tpu as pltpu
from jax.sharding import PartitionSpec as P

HEADS = 9
KV_HEADS = 3
HEAD_DIM = 64
LENGTH = 1024


EPS = 1e-05
THETA = 100000.0
NEG_BIG = -1e30
LANES = 128
VMEM_LIMIT = 56 * 1024 * 1024
CORE_MASK = 1
LIGHT = pl.CostEstimate(flops=10**8, bytes_accessed=10**6, transcendentals=0)


def masks_of(devices):
    plane = tuple(2 * step for step in range(4))
    line = tuple(8 * step for step in range(devices // 8))
    return (plane, line)


def swap(field, mask, devices):
    return lax.ppermute(field, "dp", [(place, place ^ mask) for place in range(devices)])


def tree_sum(terms):
    while len(terms) > 1:
        terms = [terms[at] + terms[at + 1] for at in range(0, len(terms), 2)]
    return terms[0]


def widen(field):
    return field.astype(jnp.float32)


def slot_mask(core, slot, devices):
    line = devices // 8
    return core * CORE_MASK + 2 * (slot // line) + 8 * (slot % line)


def tiles_of(wide):
    return -(-wide // LANES)


def tile_widths(wide):
    return [min(LANES, wide - at) for at in range(0, wide, LANES)]


def flat_starts(shapes, devices):
    starts = [0]
    for rows, wide in shapes:
        starts.append(starts[-1] + rows * wide // (devices * LANES))
    return starts


def tiled_shapes(shapes):
    return [(tiles_of(wide), rows, LANES) for rows, wide in shapes if wide % LANES]


def unpack_kernel(place_ref, *refs, devices, shapes, joined, origins):
    count = len(origins)
    pieces, refs = refs[:count], refs[count:]
    out_count = 1 if joined else len(shapes)
    outs, flats, refs = refs[:out_count], refs[out_count : out_count + len(shapes)], refs[out_count + len(shapes) :]
    stage, landed, arrival, tiled_refs = refs[0], refs[1], refs[2], list(refs[3:])
    place = place_ref[0]
    starts = flat_starts(shapes, devices)
    block = pieces[0].shape[0]
    copies = [
        pltpu.make_async_copy(piece, landed.at[index], arrival.at[index])
        for index, piece in enumerate(pieces)
    ]
    for copy in copies:
        copy.start()
    for index, (core, plane, offset) in enumerate(origins):
        copies[index].wait()
        piece_ref = landed.at[index]
        cuts = []
        for flat, start, stop in zip(flats, starts, starts[1:]):
            low, high = max(start, offset), min(stop, offset + piece_ref.shape[1])
            if low < high:
                cuts.append((flat, stop - start, low - start, low - offset, high - offset))

        def load(slot, carry, core=core, plane=plane, piece_ref=piece_ref, cuts=cuts):
            owner = place ^ slot_mask(core, plane * block + slot, devices)
            piece = piece_ref[slot].astype(jnp.float32)
            if any(low % 8 for _, _, _, low, _ in cuts):
                stage[slot % 4] = piece
            for flat, each, inner, low, high in cuts:
                rows = stage[slot % 4, low:high, :] if low % 8 else piece[low:high]
                flat[pl.ds(owner * each + inner, high - low), :] = rows
            return carry

        lax.fori_loop(0, block, load, 0)
    column = 0
    for index, ((rows, wide), flat) in enumerate(zip(shapes, flats)):
        out = outs[0 if joined else index]
        whole = wide // LANES
        if wide % LANES == 0:
            for at in range(whole):
                tile = flat[pl.ds(at, rows, stride=whole), :]
                out[:, column + at * LANES : column + (at + 1) * LANES] = tile.astype(jnp.bfloat16)
        else:
            target = tiled_refs.pop(0)
            pairs, tiles_in = rows // 2, 2 * wide // LANES
            for at in range(whole + 1):
                target[at, pl.ds(0, pairs, stride=2), :] = flat[pl.ds(at, pairs, stride=tiles_in), :]
            rolled = None
            for at in range(whole, tiles_in):
                after = pltpu.roll(flat[pl.ds(at, pairs, stride=tiles_in), :], LANES // 2, 1)
                if rolled is not None:
                    lane = lax.broadcasted_iota(jnp.int32, after.shape, 1)
                    target[at - whole - 1, pl.ds(1, pairs, stride=2), :] = jnp.where(
                        lane < LANES // 2, rolled, after
                    )
                rolled = after
            target[whole, pl.ds(1, pairs, stride=2), :] = rolled
            for at, width in enumerate(tile_widths(wide)):
                tile = target[at]
                if joined and width < LANES:
                    lane = lax.broadcasted_iota(jnp.int32, tile.shape, 1)
                    tile = jnp.where(lane < width, tile, 0.0)
                    width = LANES
                start = column + at * LANES
                out[:, start : start + width] = tile[:, :width].astype(jnp.bfloat16)
        if joined:
            column += tiles_of(wide) * LANES


def unpack_pieces(place, pieces, origins, shapes, devices, joined):
    rows_in = pieces[0].shape[1]
    outs = shapes
    if joined:
        outs = [(shapes[0][0], sum(tiles_of(wide) for _, wide in shapes) * LANES)]
    return pl.pallas_call(
        functools.partial(
            unpack_kernel, devices=devices, shapes=shapes, joined=joined, origins=origins
        ),
        out_shape=[jax.ShapeDtypeStruct(shape, jnp.bfloat16) for shape in outs],
        in_specs=[pl.BlockSpec(memory_space=pltpu.SMEM)]
        + [pl.BlockSpec(memory_space=pl.ANY)] * len(pieces),
        out_specs=[pl.BlockSpec(memory_space=pltpu.VMEM)] * len(outs),
        scratch_shapes=[
            pltpu.VMEM((rows * wide // LANES, LANES), jnp.float32) for rows, wide in shapes
        ]
        + [
            pltpu.VMEM((4, rows_in, LANES), jnp.float32),
            pltpu.VMEM((len(pieces),) + pieces[0].shape, jnp.bfloat16),
            pltpu.SemaphoreType.DMA((len(pieces),)),
        ]
        + [pltpu.VMEM(shape, jnp.float32) for shape in tiled_shapes(shapes)],
        compiler_params=pltpu.CompilerParams(vmem_limit_bytes=VMEM_LIMIT),
        cost_estimate=LIGHT,
        name="unpack",
    )(place, *pieces)


def pack_kernel(place_ref, *refs, devices, shapes, tiled_in, extra):
    count = len(shapes) + (1 if extra else 0)
    sources, kept_ref, sent_ref, stage = refs[:count], refs[count], refs[count + 1], refs[count + 2]
    flats = refs[count + 3 : count + 3 + len(shapes)]
    tiled_refs = list(refs[count + 3 + len(shapes) :])
    place = place_ref[0]
    starts = flat_starts(shapes, devices)
    for index, ((rows, wide), flat) in enumerate(zip(shapes, flats)):
        source, whole = sources[index], wide // LANES
        if wide % LANES == 0:
            for at in range(whole):
                flat[pl.ds(at, rows, stride=whole), :] = (
                    source[at] if tiled_in[index] else source[:, at * LANES : (at + 1) * LANES]
                )
            continue
        if not tiled_in[index]:
            tiled = tiled_refs.pop(0)
            for at, width in enumerate(tile_widths(wide)):
                tiled[at, :, :width] = source[:, at * LANES : at * LANES + width]
            source = tiled
        pairs, tiles_in = rows // 2, 2 * wide // LANES
        for at in range(whole):
            flat[pl.ds(at, pairs, stride=tiles_in), :] = source[at, pl.ds(0, pairs, stride=2), :]
        before = source[whole, pl.ds(0, pairs, stride=2), :]
        lane = lax.broadcasted_iota(jnp.int32, before.shape, 1)
        for at in range(whole + 1):
            rolled = pltpu.roll(source[at, pl.ds(1, pairs, stride=2), :], LANES // 2, 1)
            flat[pl.ds(whole + at, pairs, stride=tiles_in), :] = jnp.where(
                lane < LANES // 2, before, rolled
            )
            before = rolled
    row_tiles = []
    if extra:
        row = jnp.concatenate([sources[-1][at : at + 1, :] for at in range(extra[0])], 1)
        row_tiles = [
            row[:, at * LANES : (at + 1) * LANES] for at in range(extra[0] * extra[1] // LANES)
        ]
    direct = not extra and all(start % 8 == 0 for start in starts)
    if not direct:
        for at in range(4):
            for index, tile in enumerate(row_tiles):
                stage[at, starts[-1] + index : starts[-1] + index + 1, :] = tile
            used = starts[-1] + len(row_tiles)
            if used < stage.shape[1]:
                stage[at, used:, :] = jnp.zeros((stage.shape[1] - used, LANES), jnp.float32)
    for core, pieces in enumerate((kept_ref, sent_ref)):

        def store(slot, carry, core=core, pieces=pieces):
            owner = place ^ slot_mask(core, slot, devices)
            parts = []
            for flat, start, stop in zip(flats, starts, starts[1:]):
                rows = flat[pl.ds(owner * (stop - start), stop - start), :]
                if direct:
                    parts.append(rows)
                else:
                    stage[slot % 4, start:stop, :] = rows
            spare = stage.shape[1] - starts[-1]
            if direct and spare:
                parts.append(jnp.zeros((spare, LANES), jnp.float32))
            piece = jnp.concatenate(parts, 0) if direct else stage[slot % 4]
            pieces[slot] = piece.astype(jnp.bfloat16)
            return carry

        lax.fori_loop(0, devices // 2, store, 0)


def pack_grads(place, grads, shapes, devices, extra):
    rows_out = sum(rows * wide for rows, wide in shapes) // (devices * LANES)
    sources = list(grads)
    if extra is not None:
        rows_out += extra.size // LANES
        sources.append(extra)
    rows_out = -(-rows_out // 16) * 16
    tiled_in = tuple(grad.ndim == 3 for grad in grads)
    half = jax.ShapeDtypeStruct((devices // 2, rows_out, LANES), jnp.bfloat16)
    untiled = [shape for shape, tiled in zip(shapes, tiled_in) if not tiled]
    return pl.pallas_call(
        functools.partial(
            pack_kernel, devices=devices, shapes=shapes, tiled_in=tiled_in,
            extra=None if extra is None else extra.shape,
        ),
        out_shape=[half, half],
        in_specs=[pl.BlockSpec(memory_space=pltpu.SMEM)]
        + [pl.BlockSpec(memory_space=pltpu.VMEM)] * len(sources),
        out_specs=[pl.BlockSpec(memory_space=pltpu.VMEM)] * 2,
        scratch_shapes=[pltpu.VMEM((4, rows_out, LANES), jnp.float32)]
        + [pltpu.VMEM((rows * wide // LANES, LANES), jnp.float32) for rows, wide in shapes]
        + [pltpu.VMEM(shape, jnp.float32) for shape in tiled_shapes(untiled)],
        compiler_params=pltpu.CompilerParams(vmem_limit_bytes=VMEM_LIMIT),
        cost_estimate=LIGHT,
        name="pack",
    )(place, *sources)


BLOCK = 256


def dot_nt(left, right):
    return lax.dot_general(
        left, right, (((1,), (1,)), ((), ())), preferred_element_type=jnp.float32
    )


def dot_tn(left, right):
    return lax.dot_general(
        left, right, (((0,), (0,)), ((), ())), preferred_element_type=jnp.float32
    )


def dot_nn(left, right):
    return jnp.dot(left, right, preferred_element_type=jnp.float32)


def key_columns(head):
    first = tiles_of(HEADS * HEAD_DIM) * LANES + head * HEAD_DIM
    return slice(first, first + HEAD_DIM)


def value_columns(head):
    first = (tiles_of(HEADS * HEAD_DIM) + tiles_of(KV_HEADS * HEAD_DIM)) * LANES + head * HEAD_DIM
    return slice(first, first + HEAD_DIM)


def attend_kernel(fields_ref, mixed_ref, total_ref, *, head, group):
    length = fields_ref.shape[0]
    keys = fields_ref[:, key_columns(head)]
    values = fields_ref[:, value_columns(head)]
    lower = lax.broadcasted_iota(jnp.int32, (BLOCK, BLOCK), 0) >= lax.broadcasted_iota(
        jnp.int32, (BLOCK, BLOCK), 1
    )
    lane = lax.broadcasted_iota(jnp.int32, (BLOCK, LANES), 1)
    for start in range(0, length, BLOCK):
        mixed, totals_row = [], jnp.zeros((BLOCK, LANES), jnp.float32)
        for member in range(group):
            at = (head * group + member) * HEAD_DIM
            query = fields_ref[start : start + BLOCK, at : at + HEAD_DIM]
            diagonal = jnp.where(lower, dot_nt(query, keys[start : start + BLOCK]), NEG_BIG)
            maxima = jnp.max(diagonal, 1, keepdims=True)
            if start:
                before = dot_nt(query, keys[:start])
                maxima = jnp.maximum(maxima, jnp.max(before, 1, keepdims=True))
            expo = jnp.exp(diagonal - maxima)
            totals = jnp.sum(expo, 1, keepdims=True)
            result = dot_nn(expo.astype(jnp.bfloat16), values[start : start + BLOCK])
            if start:
                expo = jnp.exp(before - maxima)
                totals = totals + jnp.sum(expo, 1, keepdims=True)
                result = result + dot_nn(expo.astype(jnp.bfloat16), values[:start])
            mixed.append(result / totals)
            totals_row = jnp.where(lane == member, maxima + jnp.log(totals), totals_row)
        mixed_ref[start : start + BLOCK, :] = jnp.concatenate(mixed, 1).astype(jnp.bfloat16)
        total_ref[start : start + BLOCK, :] = totals_row


def attend(fields, head, group):
    length = fields.shape[0]
    return pl.pallas_call(
        functools.partial(attend_kernel, head=head, group=group),
        out_shape=[
            jax.ShapeDtypeStruct((length, group * HEAD_DIM), jnp.bfloat16),
            jax.ShapeDtypeStruct((length, LANES), jnp.float32),
        ],
        in_specs=[pl.BlockSpec(memory_space=pltpu.VMEM)],
        out_specs=[pl.BlockSpec(memory_space=pltpu.VMEM)] * 2,
        compiler_params=pltpu.CompilerParams(vmem_limit_bytes=VMEM_LIMIT),
        cost_estimate=LIGHT,
        name="attend",
    )(fields)


def attend_back_kernel(
    fields_ref, back_ref, mixed_ref, total_ref,
    query_back_ref, key_back_ref, queries, backs, totals, deltas, query_sum, key_sum, value_sum,
    *, head, group,
):
    length = fields_ref.shape[0]
    ones = jnp.ones((8, HEAD_DIM), jnp.float32)
    totals[...] = total_ref[...].T[:8]
    for member in range(group):
        at = (head * group + member) * HEAD_DIM
        queries[member] = fields_ref[:, at : at + HEAD_DIM]
        back = back_ref[:, at : at + HEAD_DIM]
        backs[member] = back
        product = back.astype(jnp.float32) * mixed_ref[
            :, member * HEAD_DIM : (member + 1) * HEAD_DIM
        ].astype(jnp.float32)
        deltas[member] = lax.dot_general(
            ones, product, (((1,), (1,)), ((), ())),
            precision=lax.Precision.HIGHEST, preferred_element_type=jnp.float32,
        )
    keys_all = fields_ref[:, key_columns(head)]
    values_all = fields_ref[:, value_columns(head)]
    upper = lax.broadcasted_iota(jnp.int32, (BLOCK, BLOCK), 0) <= lax.broadcasted_iota(
        jnp.int32, (BLOCK, BLOCK), 1
    )
    for member in range(group):
        total_row = totals[member : member + 1, :]
        delta_row = deltas[member][0:1]
        for start in range(0, length, BLOCK):
            keys = keys_all[start : start + BLOCK]
            values = values_all[start : start + BLOCK]
            query = queries[member, start:, :]
            back = backs[member, start:, :]
            scores = dot_nt(keys, query)
            probs = jnp.exp(scores - total_row[:, start:])
            first = jnp.where(upper, probs[:, :BLOCK], 0.0)
            probs = first if start + BLOCK == length else jnp.concatenate(
                [first, probs[:, BLOCK:]], 1
            )
            prob_back = dot_nt(values, back)
            score_back = (probs * (prob_back - delta_row[:, start:])).astype(jnp.bfloat16)
            value_part = dot_nn(probs.astype(jnp.bfloat16), back)
            key_part = dot_nn(score_back, query)
            query_part = dot_tn(score_back, keys)
            if member:
                key_sum[start : start + BLOCK, :] += key_part
                value_sum[start : start + BLOCK, :] += value_part
            else:
                key_sum[start : start + BLOCK, :] = key_part
                value_sum[start : start + BLOCK, :] = value_part
            if start:
                query_sum[member, start:, :] += query_part
            else:
                query_sum[member] = query_part
    query_back_ref[...] = (
        jnp.concatenate([query_sum[member] for member in range(group)], 1) * HEAD_DIM ** (-0.5)
    )
    key_back_ref[...] = jnp.concatenate([key_sum[...], value_sum[...]], 1)


def attend_back(fields, back, mixed, total, head, group):
    length = fields.shape[0]
    return pl.pallas_call(
        functools.partial(attend_back_kernel, head=head, group=group),
        out_shape=[
            jax.ShapeDtypeStruct((length, group * HEAD_DIM), jnp.float32),
            jax.ShapeDtypeStruct((length, 2 * HEAD_DIM), jnp.float32),
        ],
        in_specs=[pl.BlockSpec(memory_space=pltpu.VMEM)] * 4,
        out_specs=[pl.BlockSpec(memory_space=pltpu.VMEM)] * 2,
        scratch_shapes=[
            pltpu.VMEM((group, length, HEAD_DIM), jnp.bfloat16),
            pltpu.VMEM((group, length, HEAD_DIM), jnp.bfloat16),
            pltpu.VMEM((8, length), jnp.float32),
            pltpu.VMEM((group, 8, length), jnp.float32),
            pltpu.VMEM((group, length, HEAD_DIM), jnp.float32),
            pltpu.VMEM((length, HEAD_DIM), jnp.float32),
            pltpu.VMEM((length, HEAD_DIM), jnp.float32),
        ],
        compiler_params=pltpu.CompilerParams(vmem_limit_bytes=VMEM_LIMIT),
        cost_estimate=LIGHT,
        name="attend_back",
    )(fields, back, mixed, total)


def partner_of(tile):
    lane = lax.broadcasted_iota(jnp.int32, tile.shape, 1)
    half = HEAD_DIM // 2
    return jnp.where(
        lane % HEAD_DIM < half, pltpu.roll(tile, LANES - half, 1), pltpu.roll(tile, half, 1)
    )


def normed_rows(tokens_ref, gains_ref):
    resid = tokens_ref[...].astype(jnp.float32)
    inv_rms = lax.rsqrt(jnp.mean(resid * resid, 1, keepdims=True) + EPS)
    return resid, inv_rms, (resid * inv_rms * gains_ref[0:1, :]).astype(jnp.bfloat16)


def project_kernel(tokens_ref, gains_ref, wide_ref, cosine_ref, sine_ref, fields_ref, normed):
    _, _, normed[...] = normed_rows(tokens_ref, gains_ref)
    first_key = tiles_of(HEADS * HEAD_DIM)
    first_value = first_key + tiles_of(KV_HEADS * HEAD_DIM)
    count = fields_ref.shape[1] // LANES
    for start in range(0, count, 2):
        stop = min(start + 2, count)
        pair = dot_nn(normed[...], wide_ref[:, start * LANES : stop * LANES])
        for at in range(start, stop):
            tile = pair[:, (at - start) * LANES : (at - start + 1) * LANES]
            if at < first_value:
                tile = tile * cosine_ref[...] - partner_of(tile) * sine_ref[...]
            tile = tile.astype(jnp.bfloat16)
            if at < first_key:
                tile = (tile.astype(jnp.float32) * HEAD_DIM ** (-0.5)).astype(jnp.bfloat16)
            fields_ref[:, at * LANES : (at + 1) * LANES] = tile


def vmem_call(kernel, out_shape, scratch_shapes, name, *args):
    single = not isinstance(out_shape, list)
    return pl.pallas_call(
        kernel,
        out_shape=out_shape,
        in_specs=[pl.BlockSpec(memory_space=pltpu.VMEM)] * len(args),
        out_specs=pl.BlockSpec(memory_space=pltpu.VMEM)
        if single
        else [pl.BlockSpec(memory_space=pltpu.VMEM)] * len(out_shape),
        scratch_shapes=scratch_shapes,
        compiler_params=pltpu.CompilerParams(vmem_limit_bytes=VMEM_LIMIT),
        cost_estimate=LIGHT,
        name=name,
    )(*args)


def project(tokens, gains, wide, cosine, sine):
    return vmem_call(
        project_kernel,
        jax.ShapeDtypeStruct((tokens.shape[0], wide.shape[1]), jnp.bfloat16),
        [pltpu.VMEM(tokens.shape, jnp.bfloat16)],
        "project",
        tokens, gains, wide, cosine, sine,
    )


def finish_kernel(
    tokens_ref, gains_ref, wide_ref, cosine_ref, sine_ref, mid_back_ref, *refs, heads
):
    backs = refs[: 2 * heads]
    input_grad_ref, tiled_ref, gain_ref, fields, normed_t = refs[2 * heads :]
    half = HEAD_DIM
    group = HEADS // heads
    wide_heads = [(backs[2 * (at // group)], at % group * half) for at in range(HEADS)]
    wide_heads += [None] * (HEADS % 2)
    for offset in (0, half):
        wide_heads += [(backs[2 * at + 1], offset) for at in range(heads)] + [None] * (heads % 2)
    turned = tiles_of(HEADS * HEAD_DIM) + tiles_of(heads * HEAD_DIM)
    for at in range(len(wide_heads) // 2):
        cols = []
        for item in wide_heads[2 * at : 2 * at + 2]:
            if item is None:
                cols.append(jnp.zeros((fields.shape[0], half), jnp.float32))
            else:
                cols.append(item[0][:, item[1] : item[1] + half])
        tile = jnp.concatenate(cols, 1)
        if at < turned:
            tile = tile * cosine_ref[...] + partner_of(tile) * sine_ref[...]
        fields[:, at * LANES : (at + 1) * LANES] = tile.astype(jnp.bfloat16)
    resid, inv_rms, normed = normed_rows(tokens_ref, gains_ref)
    normed_t[...] = normed.T
    count = fields.shape[1] // LANES
    for start in range(0, count, 2):
        stop = min(start + 2, count)
        pair = dot_nn(normed_t[...], fields[:, start * LANES : stop * LANES])
        for at in range(start, stop):
            tiled_ref[at] = pair[:, (at - start) * LANES : (at - start + 1) * LANES]
    one_back = dot_nt(fields[...], wide_ref[...])
    weighted = one_back * gains_ref[0:1, :]
    cubed = inv_rms * inv_rms * inv_rms
    scaled = resid * inv_rms
    gain_ref[...] = jnp.sum(one_back * scaled, 0, keepdims=True)
    mean = jnp.mean(weighted * resid, 1, keepdims=True)
    grad = mid_back_ref[...] + inv_rms * weighted - resid * (cubed * mean)
    input_grad_ref[...] = grad.astype(jnp.bfloat16)


def finish(tokens, gains, wide, cosine, sine, mid_back, backs):
    heads = len(backs)
    rows, width = tokens.shape
    return vmem_call(
        functools.partial(finish_kernel, heads=heads),
        [
            jax.ShapeDtypeStruct(tokens.shape, jnp.bfloat16),
            jax.ShapeDtypeStruct((wide.shape[1] // LANES, width, LANES), jnp.float32),
            jax.ShapeDtypeStruct((1, width), jnp.float32),
        ],
        [
            pltpu.VMEM((rows, wide.shape[1]), jnp.bfloat16),
            pltpu.VMEM((width, rows), jnp.bfloat16),
        ],
        "finish",
        tokens, gains, wide, cosine, sine, mid_back, *[part for back in backs for part in back],
    )


def rotary_tables(length, head_dim):
    half_dim = head_dim // 2
    frequency = THETA ** (-(jnp.arange(half_dim, dtype=jnp.float32) * 2.0 / head_dim))
    angles = jnp.arange(length, dtype=jnp.float32)[:, None] * frequency[None, :]
    return (jnp.cos(angles), jnp.sin(angles))


def rotate_heads(field, cosine, sine):
    half_dim = field.shape[-1] // 2
    first_half = field[..., :half_dim]
    second_half = field[..., half_dim:]
    cosine = cosine[None, :, None, :]
    sine = sine[None, :, None, :]
    return jnp.concatenate(
        [first_half * cosine - second_half * sine, second_half * cosine + first_half * sine], -1
    )


def normalize(hidden, gain):
    inv_rms = lax.rsqrt(jnp.mean(hidden * hidden, -1, keepdims=True) + EPS)
    return (hidden * inv_rms * gain, inv_rms)


def normalize_back(grad, hidden, inv_rms, gain):
    weighted = grad * gain
    cubed = inv_rms * inv_rms * inv_rms
    hidden_grad = inv_rms * weighted - hidden * cubed * jnp.mean(
        weighted * hidden, -1, keepdims=True
    )
    gain_part = jnp.sum(grad * hidden * inv_rms, 0)
    return (hidden_grad, gain_part)


def outer_prod(left, right):
    return lax.dot_general(
        left, right, (((0,), (0,)), ((), ())), preferred_element_type=jnp.float32
    )


def times_transposed(left, matrix):
    return lax.dot_general(
        left, matrix, (((1,), (1,)), ((), ())), preferred_element_type=jnp.float32
    )


def whole_rows(shapes, devices):
    return (devices & (devices - 1)) == 0 and all(
        rows % (8 * devices // 4) == 0 and rows * wide % (devices * LANES) == 0
        for rows, wide in shapes
    )


def place_of():
    return lax.axis_index("dp").astype(jnp.int32).reshape(1)


class WeightGather:
    def __init__(self, shards, shapes, devices):
        self.shards, self.shapes, self.devices = shards, shapes, devices
        self.stages = whole_rows(shapes, devices)
        if self.stages:
            held = jnp.concatenate([shard.reshape(-1, LANES) for shard in shards])
            self.held = jnp.pad(held, ((0, -held.shape[0] % 16), (0, 0)))

    def line_stage(self, other):
        if not self.stages:
            return other
        _, line = masks_of(self.devices)
        self.held, other = tied(self.held, other)
        self.arrived = [self.held] + [swap(self.held, mask, self.devices) for mask in line[1:]]
        return other

    def plane_stage(self, other):
        if not self.stages:
            return other
        plane, _ = masks_of(self.devices)
        self.held, other = tied(jnp.stack(self.arrived), other)
        self.arrived = [self.held] + [swap(self.held, mask, self.devices) for mask in plane[1:]]
        self.origins = [(0, at, 0) for at in range(len(plane))]
        return other

    def first_half_stage(self, other):
        if not self.stages:
            return other
        plane, _ = masks_of(self.devices)
        cut = self.arrived[0].shape[0] // 2
        halves = [
            jnp.stack([field[at : at + cut] for field in self.arrived]) for at in (0, cut)
        ]
        halves, other = tied(halves, other)
        self.arrived = [
            [half, swap(half, mask, self.devices)] for half, mask in zip(halves, plane[1:3])
        ]
        return other

    def second_half_stage(self, other):
        if not self.stages:
            return other
        plane, _ = masks_of(self.devices)
        pairs, other = tied(self.arrived, other)
        cut = pairs[0][0].shape[1]
        self.arrived, self.origins = [], []
        for at, pair in enumerate(pairs):
            near, far = (1, 2) if at == 0 else (2, 1)
            self.arrived += pair + [swap(field, plane[far], self.devices) for field in pair]
            self.origins += [(0, where, at * cut) for where in (0, near, far, 3)]
        return other

    def core_stage(self, other, joined):
        if not self.stages:
            return other
        self.arrived, other = tied(self.arrived, other)
        if joined:
            self.arrived, self.origins = [jnp.concatenate(self.arrived)], [(0, 0, 0)]
        self.origins += [(1, where, offset) for _, where, offset in self.origins]
        self.got = [swap(field, CORE_MASK, self.devices) for field in self.arrived]
        return other

    def result(self, joined):
        if not self.stages:
            mats = [
                lax.all_gather(shard, "dp", axis=0, tiled=True).reshape(shape)
                for shard, shape in zip(self.shards, self.shapes)
            ]
            if not joined:
                return mats
            pads = [((0, 0), (0, tiles_of(mat.shape[1]) * LANES - mat.shape[1])) for mat in mats]
            return [jnp.concatenate([jnp.pad(mat, pad) for mat, pad in zip(mats, pads)], 1)]
        pieces = self.arrived + self.got
        return unpack_pieces(
            place_of(), pieces, tuple(self.origins), self.shapes, self.devices, joined
        )


def tied(first, second):
    return lax.optimization_barrier((first, second))


class GradSum:
    def __init__(self, grads, shapes, devices, extra=None):
        self.grads, self.shapes, self.devices, self.extra = grads, shapes, devices, extra
        self.stages = whole_rows(shapes, devices)
        if self.stages:
            self.kept, self.sent = pack_grads(place_of(), grads, shapes, devices, extra)

    def core_stage(self, other):
        if not self.stages:
            return other
        (self.kept, self.sent), other = tied((self.kept, self.sent), other)
        self.got = swap(self.sent, CORE_MASK, self.devices)
        return other

    def plane_stage(self, other):
        if not self.stages:
            return other
        plane, _ = masks_of(self.devices)
        block = self.kept.shape[0] // len(plane)
        cuts = [slice(at * block, (at + 1) * block) for at in range(len(plane))]
        parts = [(widen(self.kept[cut]) + widen(self.got[cut])).astype(jnp.bfloat16) for cut in cuts]
        self.parts, other = tied(parts, other)
        self.arrived = [
            swap(part, mask, self.devices) for part, mask in zip(self.parts[1:], plane[1:])
        ]
        return other

    def line_stage(self, other):
        if not self.stages:
            return other
        _, line = masks_of(self.devices)
        terms = [self.parts[0]] + self.arrived
        parts = [
            tree_sum([widen(term[at]) for term in terms]).astype(jnp.bfloat16)
            for at in range(len(line))
        ]
        self.parts, other = tied(parts, other)
        self.arrived = [
            swap(part, mask, self.devices) for part, mask in zip(self.parts[1:], line[1:])
        ]
        return other

    def result(self):
        if not self.stages:
            grads = [
                grad.swapaxes(0, 1).reshape(rows, -1)[:, :wide] if grad.ndim == 3 else grad
                for grad, (rows, wide) in zip(self.grads, self.shapes)
            ]
            sums = [
                lax.psum_scatter(grad.reshape(-1), "dp", scatter_dimension=0, tiled=True)
                for grad in grads
            ]
            return sums if self.extra is None else sums + [lax.psum(self.extra, "dp")]
        pieces = tree_sum([widen(term) for term in [self.parts[0]] + self.arrived])
        sums, start = [], 0
        for rows, wide in self.shapes:
            count = rows * wide // (self.devices * LANES)
            sums.append(pieces[start : start + count].reshape(-1))
            start += count
        if self.extra is not None:
            count = self.extra.size // LANES
            sums.append(pieces[start : start + count].reshape(self.extra.shape))
        return sums


def body(tokens, cotangent, w_query, w_key, w_value, w_out, w_gate, w_up, w_down, norm_gains):
    model_width = tokens.shape[1]
    seq_count = tokens.shape[0] // LENGTH
    group_size = HEADS // KV_HEADS
    scale_factor = HEAD_DIM ** (-0.5)
    gain_f = norm_gains.astype(jnp.float32)
    shards = (w_query, w_key, w_value, w_out, w_gate, w_up, w_down)
    devices = lax.axis_size("dp")
    widths = [shards[at].shape[0] * devices // model_width for at in range(6)]
    shapes = [(model_width, wide) for wide in widths] + [
        (shards[6].shape[0] * devices // model_width, model_width)
    ]
    first = WeightGather(shards[:3], shapes[:3], devices)
    rest = (4, 5, 6, 3)
    second = WeightGather(
        [shards[at] for at in rest], [shapes[at] for at in rest], devices
    )
    tokens = first.line_stage(tokens)
    if first.stages:
        first.arrived[1] = second.line_stage(first.arrived[1])
    tokens = first.plane_stage(tokens)
    tokens = first.core_stage(tokens, True)
    if first.stages:
        first.got = second.first_half_stage(first.got)
    (wide_mat,) = first.result(True)
    resid_in = tokens.astype(jnp.float32)
    cosine, sine = rotary_tables(LENGTH, HEAD_DIM)
    pairs = LANES // HEAD_DIM
    cosine = jnp.tile(cosine, (seq_count, 2 * pairs))
    sine = jnp.tile(jnp.concatenate([sine, -sine], 1), (seq_count, pairs))
    fields = project(tokens, gain_f, wide_mat, cosine, sine)
    fields = second.second_half_stage(fields)
    attended = [attend(fields, head, group_size) for head in range(2)]
    fields, attended = second.core_stage((fields, attended), False)
    attended.append(attend(fields, 2, group_size))
    wg_mat, wu_mat, wd_mat, wo_mat = second.result(False)
    mixed = jnp.concatenate([part for part, _ in attended], 1)
    attn_out = jnp.dot(mixed, wo_mat, preferred_element_type=jnp.float32)
    middle = resid_in + attn_out
    normed_two, rms_two = normalize(middle, gain_f[1])
    normed_two = normed_two.astype(jnp.bfloat16)
    gate = jnp.dot(normed_two, wg_mat, preferred_element_type=jnp.float32)
    upward = jnp.dot(normed_two, wu_mat, preferred_element_type=jnp.float32)
    sigmoid_g = jax.nn.sigmoid(gate)
    activated = gate * sigmoid_g
    hidden = (activated * upward).astype(jnp.bfloat16)
    ffn_out = jnp.dot(hidden, wd_mat, preferred_element_type=jnp.float32)
    output = (middle + ffn_out).astype(jnp.bfloat16)
    grad_down = outer_prod(hidden, cotangent)
    hidden_back = times_transposed(cotangent, wd_mat)
    gate_back = (hidden_back * upward * sigmoid_g * (1.0 + gate * (1.0 - sigmoid_g))).astype(
        jnp.bfloat16
    )
    up_back = (hidden_back * activated).astype(jnp.bfloat16)
    grad_gate = outer_prod(normed_two, gate_back)
    grad_up = outer_prod(normed_two, up_back)
    two_back = times_transposed(gate_back, wg_mat) + times_transposed(up_back, wu_mat)
    norm_two_back, gain_two = normalize_back(two_back, middle, rms_two, gain_f[1])
    mid_back = cotangent.astype(jnp.float32) + norm_two_back
    mid_low = mid_back.astype(jnp.bfloat16)
    grad_out = outer_prod(mixed, mid_low)
    mixed_back = times_transposed(mid_low, wo_mat).astype(jnp.bfloat16)
    feed_sum = GradSum(
        (grad_gate, grad_up, grad_down, grad_out), [shapes[at] for at in rest], devices
    )

    def back_of(head, field):
        part, total = attended[head]
        return attend_back(fields, field, part, total, head, group_size)

    mixed_back = feed_sum.core_stage(mixed_back)
    backs = [back_of(0, mixed_back)]
    mixed_back, _ = tied(mixed_back, backs[0])
    mixed_back = feed_sum.plane_stage(mixed_back)
    backs += [back_of(head, mixed_back) for head in range(1, KV_HEADS)]
    input_grad, tiled, gain_one = finish(tokens, gain_f, wide_mat, cosine, sine, mid_back, backs)
    input_grad, tiled = feed_sum.line_stage((input_grad, tiled))
    gains_back = jnp.concatenate([gain_one, gain_two[None]], 0)
    cuts = [0]
    for _, wide in shapes[:3]:
        cuts.append(cuts[-1] + tiles_of(wide))
    grads = tuple(tiled[start:stop] for start, stop in zip(cuts, cuts[1:]))
    mix_sum = GradSum(grads, shapes[:3], devices, gains_back)
    input_grad = mix_sum.core_stage(input_grad)
    input_grad = mix_sum.plane_stage(input_grad)
    if feed_sum.stages:
        feed_sum.arrived = mix_sum.line_stage(feed_sum.arrived)
    mix_parts = mix_sum.result()
    gate_part, up_part, down_part, out_part = feed_sum.result()
    all_parts = mix_parts[:3] + [out_part, gate_part, up_part, down_part]
    gain_grad = mix_parts[3]
    return (output, input_grad) + tuple(all_parts) + (gain_grad,)


def solution(mesh):
    return jax.shard_map(
        body,
        mesh=mesh,
        in_specs=(
            P("dp", None),
            P("dp", None),
            P("dp"),
            P("dp"),
            P("dp"),
            P("dp"),
            P("dp"),
            P("dp"),
            P("dp"),
            P(),
        ),
        out_specs=(
            P("dp", None),
            P("dp", None),
            P("dp"),
            P("dp"),
            P("dp"),
            P("dp"),
            P("dp"),
            P("dp"),
            P("dp"),
            P(),
        ),
        check_vma=False,
    )
```

```python
import functools

import jax
import jax.numpy as jnp
from jax import lax
from jax.experimental import pallas as pl
from jax.experimental.pallas import tpu as pltpu
from jax.sharding import PartitionSpec as P

HEADS = 9
KV_HEADS = 3
HEAD_DIM = 64
LENGTH = 1024


EPS = 1e-05
THETA = 100000.0
NEG_BIG = -1e30
LANES = 128
VMEM_LIMIT = 56 * 1024 * 1024
CORE_MASK = 1
LIGHT = pl.CostEstimate(flops=10**8, bytes_accessed=10**6, transcendentals=0)


def masks_of(devices):
    plane = tuple(2 * step for step in range(4))
    line = tuple(8 * step for step in range(devices // 8))
    return (plane, line)


def swap(field, mask, devices):
    return lax.ppermute(field, "dp", [(place, place ^ mask) for place in range(devices)])


def tree_sum(terms):
    while len(terms) > 1:
        odd = terms[len(terms) // 2 * 2 :]
        terms = [terms[at] + terms[at + 1] for at in range(0, len(terms) - 1, 2)] + odd
    return terms[0]


def widen(field):
    return field.astype(jnp.float32)


def slot_mask(core, slot, devices):
    line = devices // 8
    return core * CORE_MASK + 2 * (slot // line) + 8 * (slot % line)


def tiles_of(wide):
    return -(-wide // LANES)


def tile_widths(wide):
    return [min(LANES, wide - at) for at in range(0, wide, LANES)]


def flat_starts(shapes, devices):
    starts = [0]
    for rows, wide in shapes:
        starts.append(starts[-1] + rows * wide // (devices * LANES))
    return starts


def tiled_shapes(shapes):
    return [(tiles_of(wide), rows, LANES) for rows, wide in shapes if wide % LANES]


def unpack_kernel(place_ref, *refs, devices, shapes, joined, origins):
    count = len(origins)
    pieces, refs = refs[:count], refs[count:]
    out_count = 1 if joined else len(shapes)
    outs, flats, refs = refs[:out_count], refs[out_count : out_count + len(shapes)], refs[out_count + len(shapes) :]
    stage, landed, arrival, tiled_refs = refs[0], refs[1], refs[2], list(refs[3:])
    place = place_ref[0]
    starts = flat_starts(shapes, devices)
    block = pieces[0].shape[0]
    copies = [
        pltpu.make_async_copy(piece, landed.at[index], arrival.at[index])
        for index, piece in enumerate(pieces)
    ]
    for copy in copies:
        copy.start()
    for index, (core, plane, offset) in enumerate(origins):
        copies[index].wait()
        piece_ref = landed.at[index]
        cuts = []
        for flat, start, stop in zip(flats, starts, starts[1:]):
            low, high = max(start, offset), min(stop, offset + piece_ref.shape[1])
            if low < high:
                cuts.append((flat, stop - start, low - start, low - offset, high - offset))

        def load(slot, carry, core=core, plane=plane, piece_ref=piece_ref, cuts=cuts):
            owner = place ^ slot_mask(core, plane * block + slot, devices)
            piece = piece_ref[slot].astype(jnp.float32)
            if any(low % 8 for _, _, _, low, _ in cuts):
                stage[slot % 4] = piece
            for flat, each, inner, low, high in cuts:
                rows = stage[slot % 4, low:high, :] if low % 8 else piece[low:high]
                flat[pl.ds(owner * each + inner, high - low), :] = rows
            return carry

        lax.fori_loop(0, block, load, 0)
    column = 0
    for index, ((rows, wide), flat) in enumerate(zip(shapes, flats)):
        out = outs[0 if joined else index]
        whole = wide // LANES
        if wide % LANES == 0:
            for at in range(whole):
                tile = flat[pl.ds(at, rows, stride=whole), :]
                out[:, column + at * LANES : column + (at + 1) * LANES] = tile.astype(jnp.bfloat16)
        else:
            target = tiled_refs.pop(0)
            pairs, tiles_in = rows // 2, 2 * wide // LANES
            for at in range(whole + 1):
                target[at, pl.ds(0, pairs, stride=2), :] = flat[pl.ds(at, pairs, stride=tiles_in), :]
            rolled = None
            for at in range(whole, tiles_in):
                after = pltpu.roll(flat[pl.ds(at, pairs, stride=tiles_in), :], LANES // 2, 1)
                if rolled is not None:
                    lane = lax.broadcasted_iota(jnp.int32, after.shape, 1)
                    target[at - whole - 1, pl.ds(1, pairs, stride=2), :] = jnp.where(
                        lane < LANES // 2, rolled, after
                    )
                rolled = after
            target[whole, pl.ds(1, pairs, stride=2), :] = rolled
            for at, width in enumerate(tile_widths(wide)):
                tile = target[at]
                if joined and width < LANES:
                    lane = lax.broadcasted_iota(jnp.int32, tile.shape, 1)
                    tile = jnp.where(lane < width, tile, 0.0)
                    width = LANES
                start = column + at * LANES
                out[:, start : start + width] = tile[:, :width].astype(jnp.bfloat16)
        if joined:
            column += tiles_of(wide) * LANES


def unpack_pieces(place, pieces, origins, shapes, devices, joined):
    rows_in = pieces[0].shape[1]
    outs = shapes
    if joined:
        outs = [(shapes[0][0], sum(tiles_of(wide) for _, wide in shapes) * LANES)]
    return pl.pallas_call(
        functools.partial(
            unpack_kernel, devices=devices, shapes=shapes, joined=joined, origins=origins
        ),
        out_shape=[jax.ShapeDtypeStruct(shape, jnp.bfloat16) for shape in outs],
        in_specs=[pl.BlockSpec(memory_space=pltpu.SMEM)]
        + [pl.BlockSpec(memory_space=pl.ANY)] * len(pieces),
        out_specs=[pl.BlockSpec(memory_space=pltpu.VMEM)] * len(outs),
        scratch_shapes=[
            pltpu.VMEM((rows * wide // LANES, LANES), jnp.float32) for rows, wide in shapes
        ]
        + [
            pltpu.VMEM((4, rows_in, LANES), jnp.float32),
            pltpu.VMEM((len(pieces),) + pieces[0].shape, jnp.bfloat16),
            pltpu.SemaphoreType.DMA((len(pieces),)),
        ]
        + [pltpu.VMEM(shape, jnp.float32) for shape in tiled_shapes(shapes)],
        compiler_params=pltpu.CompilerParams(vmem_limit_bytes=VMEM_LIMIT),
        cost_estimate=LIGHT,
        name="unpack",
    )(place, *pieces)


def pack_kernel(place_ref, *refs, devices, shapes, tiled_in, extra):
    count = len(shapes) + (1 if extra else 0)
    sources, kept_ref, sent_ref, stage = refs[:count], refs[count], refs[count + 1], refs[count + 2]
    flats = refs[count + 3 : count + 3 + len(shapes)]
    tiled_refs = list(refs[count + 3 + len(shapes) :])
    place = place_ref[0]
    starts = flat_starts(shapes, devices)
    for index, ((rows, wide), flat) in enumerate(zip(shapes, flats)):
        source, whole = sources[index], wide // LANES
        if wide % LANES == 0:
            for at in range(whole):
                flat[pl.ds(at, rows, stride=whole), :] = (
                    source[at] if tiled_in[index] else source[:, at * LANES : (at + 1) * LANES]
                )
            continue
        if not tiled_in[index]:
            tiled = tiled_refs.pop(0)
            for at, width in enumerate(tile_widths(wide)):
                tiled[at, :, :width] = source[:, at * LANES : at * LANES + width]
            source = tiled
        pairs, tiles_in = rows // 2, 2 * wide // LANES
        for at in range(whole):
            flat[pl.ds(at, pairs, stride=tiles_in), :] = source[at, pl.ds(0, pairs, stride=2), :]
        before = source[whole, pl.ds(0, pairs, stride=2), :]
        lane = lax.broadcasted_iota(jnp.int32, before.shape, 1)
        for at in range(whole + 1):
            rolled = pltpu.roll(source[at, pl.ds(1, pairs, stride=2), :], LANES // 2, 1)
            flat[pl.ds(whole + at, pairs, stride=tiles_in), :] = jnp.where(
                lane < LANES // 2, before, rolled
            )
            before = rolled
    row_tiles = []
    if extra:
        row = jnp.concatenate([sources[-1][at : at + 1, :] for at in range(extra[0])], 1)
        row_tiles = [
            row[:, at * LANES : (at + 1) * LANES] for at in range(extra[0] * extra[1] // LANES)
        ]
    direct = not extra and all(start % 8 == 0 for start in starts)
    if not direct:
        for at in range(4):
            for index, tile in enumerate(row_tiles):
                stage[at, starts[-1] + index : starts[-1] + index + 1, :] = tile
            used = starts[-1] + len(row_tiles)
            if used < stage.shape[1]:
                stage[at, used:, :] = jnp.zeros((stage.shape[1] - used, LANES), jnp.float32)
    for core, pieces in enumerate((kept_ref, sent_ref)):

        def store(slot, carry, core=core, pieces=pieces):
            owner = place ^ slot_mask(core, slot, devices)
            parts = []
            for flat, start, stop in zip(flats, starts, starts[1:]):
                rows = flat[pl.ds(owner * (stop - start), stop - start), :]
                if direct:
                    parts.append(rows)
                else:
                    stage[slot % 4, start:stop, :] = rows
            spare = stage.shape[1] - starts[-1]
            if direct and spare:
                parts.append(jnp.zeros((spare, LANES), jnp.float32))
            piece = jnp.concatenate(parts, 0) if direct else stage[slot % 4]
            pieces[slot] = piece.astype(jnp.bfloat16)
            return carry

        lax.fori_loop(0, devices // 2, store, 0)


def pack_grads(place, grads, shapes, devices, extra):
    rows_out = sum(rows * wide for rows, wide in shapes) // (devices * LANES)
    sources = list(grads)
    if extra is not None:
        rows_out += extra.size // LANES
        sources.append(extra)
    rows_out = -(-rows_out // 16) * 16
    tiled_in = tuple(grad.ndim == 3 for grad in grads)
    half = jax.ShapeDtypeStruct((devices // 2, rows_out, LANES), jnp.bfloat16)
    untiled = [shape for shape, tiled in zip(shapes, tiled_in) if not tiled]
    return pl.pallas_call(
        functools.partial(
            pack_kernel, devices=devices, shapes=shapes, tiled_in=tiled_in,
            extra=None if extra is None else extra.shape,
        ),
        out_shape=[half, half],
        in_specs=[pl.BlockSpec(memory_space=pltpu.SMEM)]
        + [pl.BlockSpec(memory_space=pltpu.VMEM)] * len(sources),
        out_specs=[pl.BlockSpec(memory_space=pltpu.VMEM)] * 2,
        scratch_shapes=[pltpu.VMEM((4, rows_out, LANES), jnp.float32)]
        + [pltpu.VMEM((rows * wide // LANES, LANES), jnp.float32) for rows, wide in shapes]
        + [pltpu.VMEM(shape, jnp.float32) for shape in tiled_shapes(untiled)],
        compiler_params=pltpu.CompilerParams(vmem_limit_bytes=VMEM_LIMIT),
        cost_estimate=LIGHT,
        name="pack",
    )(place, *sources)


BLOCK = 256


def dot_nt(left, right):
    return lax.dot_general(
        left, right, (((1,), (1,)), ((), ())), preferred_element_type=jnp.float32
    )


def dot_tn(left, right):
    return lax.dot_general(
        left, right, (((0,), (0,)), ((), ())), preferred_element_type=jnp.float32
    )


def dot_nn(left, right):
    return jnp.dot(left, right, preferred_element_type=jnp.float32)


def key_columns(head):
    first = tiles_of(HEADS * HEAD_DIM) * LANES + head * HEAD_DIM
    return slice(first, first + HEAD_DIM)


def value_columns(head):
    first = (tiles_of(HEADS * HEAD_DIM) + tiles_of(KV_HEADS * HEAD_DIM)) * LANES + head * HEAD_DIM
    return slice(first, first + HEAD_DIM)


def attend_kernel(fields_ref, mixed_ref, total_ref, *, head, group):
    length = fields_ref.shape[0]
    keys = fields_ref[:, key_columns(head)]
    values = fields_ref[:, value_columns(head)]
    lower = lax.broadcasted_iota(jnp.int32, (BLOCK, BLOCK), 0) >= lax.broadcasted_iota(
        jnp.int32, (BLOCK, BLOCK), 1
    )
    lane = lax.broadcasted_iota(jnp.int32, (BLOCK, LANES), 1)
    for start in range(0, length, BLOCK):
        mixed, totals_row = [], jnp.zeros((BLOCK, LANES), jnp.float32)
        for member in range(group):
            at = (head * group + member) * HEAD_DIM
            query = fields_ref[start : start + BLOCK, at : at + HEAD_DIM]
            diagonal = jnp.where(lower, dot_nt(query, keys[start : start + BLOCK]), NEG_BIG)
            maxima = jnp.max(diagonal, 1, keepdims=True)
            if start:
                before = dot_nt(query, keys[:start])
                maxima = jnp.maximum(maxima, jnp.max(before, 1, keepdims=True))
            expo = jnp.exp(diagonal - maxima)
            totals = jnp.sum(expo, 1, keepdims=True)
            result = dot_nn(expo.astype(jnp.bfloat16), values[start : start + BLOCK])
            if start:
                expo = jnp.exp(before - maxima)
                totals = totals + jnp.sum(expo, 1, keepdims=True)
                result = result + dot_nn(expo.astype(jnp.bfloat16), values[:start])
            mixed.append(result / totals)
            totals_row = jnp.where(lane == member, maxima + jnp.log(totals), totals_row)
        mixed_ref[start : start + BLOCK, :] = jnp.concatenate(mixed, 1).astype(jnp.bfloat16)
        total_ref[start : start + BLOCK, :] = totals_row


def attend(fields, head, group):
    length = fields.shape[0]
    return pl.pallas_call(
        functools.partial(attend_kernel, head=head, group=group),
        out_shape=[
            jax.ShapeDtypeStruct((length, group * HEAD_DIM), jnp.bfloat16),
            jax.ShapeDtypeStruct((length, LANES), jnp.float32),
        ],
        in_specs=[pl.BlockSpec(memory_space=pltpu.VMEM)],
        out_specs=[pl.BlockSpec(memory_space=pltpu.VMEM)] * 2,
        compiler_params=pltpu.CompilerParams(vmem_limit_bytes=VMEM_LIMIT),
        cost_estimate=LIGHT,
        name="attend",
    )(fields)


def attend_back_kernel(
    fields_ref, back_ref, mixed_ref, total_ref,
    query_back_ref, key_back_ref, queries, backs, totals, deltas, query_sum, key_sum, value_sum,
    *, head, group,
):
    length = fields_ref.shape[0]
    ones = jnp.ones((8, HEAD_DIM), jnp.float32)
    totals[...] = total_ref[...].T[:8]
    for member in range(group):
        at = (head * group + member) * HEAD_DIM
        queries[member] = fields_ref[:, at : at + HEAD_DIM]
        back = back_ref[:, at : at + HEAD_DIM]
        backs[member] = back
        product = back.astype(jnp.float32) * mixed_ref[
            :, member * HEAD_DIM : (member + 1) * HEAD_DIM
        ].astype(jnp.float32)
        deltas[member] = lax.dot_general(
            ones, product, (((1,), (1,)), ((), ())),
            precision=lax.Precision.HIGHEST, preferred_element_type=jnp.float32,
        )
    keys_all = fields_ref[:, key_columns(head)]
    values_all = fields_ref[:, value_columns(head)]
    upper = lax.broadcasted_iota(jnp.int32, (BLOCK, BLOCK), 0) <= lax.broadcasted_iota(
        jnp.int32, (BLOCK, BLOCK), 1
    )
    for member in range(group):
        total_row = totals[member : member + 1, :]
        delta_row = deltas[member][0:1]
        for start in range(0, length, BLOCK):
            keys = keys_all[start : start + BLOCK]
            values = values_all[start : start + BLOCK]
            query = queries[member, start:, :]
            back = backs[member, start:, :]
            scores = dot_nt(keys, query)
            probs = jnp.exp(scores - total_row[:, start:])
            first = jnp.where(upper, probs[:, :BLOCK], 0.0)
            probs = first if start + BLOCK == length else jnp.concatenate(
                [first, probs[:, BLOCK:]], 1
            )
            prob_back = dot_nt(values, back)
            score_back = (probs * (prob_back - delta_row[:, start:])).astype(jnp.bfloat16)
            value_part = dot_nn(probs.astype(jnp.bfloat16), back)
            key_part = dot_nn(score_back, query)
            query_part = dot_tn(score_back, keys)
            if member:
                key_sum[start : start + BLOCK, :] += key_part
                value_sum[start : start + BLOCK, :] += value_part
            else:
                key_sum[start : start + BLOCK, :] = key_part
                value_sum[start : start + BLOCK, :] = value_part
            if start:
                query_sum[member, start:, :] += query_part
            else:
                query_sum[member] = query_part
    query_back_ref[...] = (
        jnp.concatenate([query_sum[member] for member in range(group)], 1) * HEAD_DIM ** (-0.5)
    )
    key_back_ref[...] = jnp.concatenate([key_sum[...], value_sum[...]], 1)


def attend_back(fields, back, mixed, total, head, group):
    length = fields.shape[0]
    return pl.pallas_call(
        functools.partial(attend_back_kernel, head=head, group=group),
        out_shape=[
            jax.ShapeDtypeStruct((length, group * HEAD_DIM), jnp.float32),
            jax.ShapeDtypeStruct((length, 2 * HEAD_DIM), jnp.float32),
        ],
        in_specs=[pl.BlockSpec(memory_space=pltpu.VMEM)] * 4,
        out_specs=[pl.BlockSpec(memory_space=pltpu.VMEM)] * 2,
        scratch_shapes=[
            pltpu.VMEM((group, length, HEAD_DIM), jnp.bfloat16),
            pltpu.VMEM((group, length, HEAD_DIM), jnp.bfloat16),
            pltpu.VMEM((8, length), jnp.float32),
            pltpu.VMEM((group, 8, length), jnp.float32),
            pltpu.VMEM((group, length, HEAD_DIM), jnp.float32),
            pltpu.VMEM((length, HEAD_DIM), jnp.float32),
            pltpu.VMEM((length, HEAD_DIM), jnp.float32),
        ],
        compiler_params=pltpu.CompilerParams(vmem_limit_bytes=VMEM_LIMIT),
        cost_estimate=LIGHT,
        name="attend_back",
    )(fields, back, mixed, total)


def partner_of(tile):
    lane = lax.broadcasted_iota(jnp.int32, tile.shape, 1)
    half = HEAD_DIM // 2
    return jnp.where(
        lane % HEAD_DIM < half, pltpu.roll(tile, LANES - half, 1), pltpu.roll(tile, half, 1)
    )


def first_gain(gains_ref):
    return gains_ref[...].astype(jnp.float32)[0:1]


def normed_rows(tokens_ref, gains_ref):
    resid = tokens_ref[...].astype(jnp.float32)
    inv_rms = lax.rsqrt(jnp.mean(resid * resid, 1, keepdims=True) + EPS)
    return resid, inv_rms, (resid * inv_rms * first_gain(gains_ref)).astype(jnp.bfloat16)


def project_kernel(
    tokens_in, cosine_in, sine_in, gains_ref, wide_ref, fields_ref,
    tokens_ref, cosine_ref, sine_ref, normed, arrival,
):
    copies = [
        pltpu.make_async_copy(source, target, arrival.at[at])
        for at, (source, target) in enumerate(
            ((tokens_in, tokens_ref), (cosine_in, cosine_ref), (sine_in, sine_ref))
        )
    ]
    for copy in copies:
        copy.start()
    for copy in copies:
        copy.wait()
    _, _, normed[...] = normed_rows(tokens_ref, gains_ref)
    first_key = tiles_of(HEADS * HEAD_DIM)
    first_value = first_key + tiles_of(KV_HEADS * HEAD_DIM)
    count = fields_ref.shape[1] // LANES
    for start in range(0, count, 2):
        stop = min(start + 2, count)
        pair = dot_nn(normed[...], wide_ref[:, start * LANES : stop * LANES])
        for at in range(start, stop):
            tile = pair[:, (at - start) * LANES : (at - start + 1) * LANES]
            if at < first_value:
                tile = tile * cosine_ref[...] - partner_of(tile) * sine_ref[...]
            tile = tile.astype(jnp.bfloat16)
            if at < first_key:
                tile = (tile.astype(jnp.float32) * HEAD_DIM ** (-0.5)).astype(jnp.bfloat16)
            fields_ref[:, at * LANES : (at + 1) * LANES] = tile


def vmem_call(kernel, out_shape, scratch_shapes, name, *args):
    single = not isinstance(out_shape, list)
    return pl.pallas_call(
        kernel,
        out_shape=out_shape,
        in_specs=[pl.BlockSpec(memory_space=pltpu.VMEM)] * len(args),
        out_specs=pl.BlockSpec(memory_space=pltpu.VMEM)
        if single
        else [pl.BlockSpec(memory_space=pltpu.VMEM)] * len(out_shape),
        scratch_shapes=scratch_shapes,
        compiler_params=pltpu.CompilerParams(vmem_limit_bytes=VMEM_LIMIT),
        cost_estimate=LIGHT,
        name=name,
    )(*args)


def project(tokens, gains, wide, cosine, sine):
    return pl.pallas_call(
        project_kernel,
        out_shape=jax.ShapeDtypeStruct((tokens.shape[0], wide.shape[1]), jnp.bfloat16),
        in_specs=[pl.BlockSpec(memory_space=pl.ANY)] * 3
        + [pl.BlockSpec(memory_space=pltpu.VMEM)] * 2,
        out_specs=pl.BlockSpec(memory_space=pltpu.VMEM),
        scratch_shapes=[
            pltpu.VMEM(tokens.shape, tokens.dtype),
            pltpu.VMEM(cosine.shape, cosine.dtype),
            pltpu.VMEM(sine.shape, sine.dtype),
            pltpu.VMEM(tokens.shape, jnp.bfloat16),
            pltpu.SemaphoreType.DMA((3,)),
        ],
        compiler_params=pltpu.CompilerParams(vmem_limit_bytes=VMEM_LIMIT),
        cost_estimate=LIGHT,
        name="project",
    )(tokens, cosine, sine, gains, wide)


def finish_kernel(
    tokens_ref, gains_ref, wide_ref, cosine_ref, sine_ref, mid_back_ref, *refs, heads
):
    backs = refs[: 2 * heads]
    input_grad_ref, tiled_ref, gain_ref, fields, normed_t = refs[2 * heads :]
    half = HEAD_DIM
    group = HEADS // heads
    wide_heads = [(backs[2 * (at // group)], at % group * half) for at in range(HEADS)]
    wide_heads += [None] * (HEADS % 2)
    for offset in (0, half):
        wide_heads += [(backs[2 * at + 1], offset) for at in range(heads)] + [None] * (heads % 2)
    turned = tiles_of(HEADS * HEAD_DIM) + tiles_of(heads * HEAD_DIM)
    for at in range(len(wide_heads) // 2):
        cols = []
        for item in wide_heads[2 * at : 2 * at + 2]:
            if item is None:
                cols.append(jnp.zeros((fields.shape[0], half), jnp.float32))
            else:
                cols.append(item[0][:, item[1] : item[1] + half])
        tile = jnp.concatenate(cols, 1)
        if at < turned:
            tile = tile * cosine_ref[...] + partner_of(tile) * sine_ref[...]
        fields[:, at * LANES : (at + 1) * LANES] = tile.astype(jnp.bfloat16)
    resid, inv_rms, normed = normed_rows(tokens_ref, gains_ref)
    normed_t[...] = normed.T
    count = fields.shape[1] // LANES
    for start in range(0, count, 2):
        stop = min(start + 2, count)
        pair = dot_nn(normed_t[...], fields[:, start * LANES : stop * LANES])
        for at in range(start, stop):
            tiled_ref[at] = pair[:, (at - start) * LANES : (at - start + 1) * LANES]
    one_back = dot_nt(fields[...], wide_ref[...])
    weighted = one_back * first_gain(gains_ref)
    cubed = inv_rms * inv_rms * inv_rms
    scaled = resid * inv_rms
    gain_ref[...] = jnp.sum(one_back * scaled, 0, keepdims=True)
    mean = jnp.mean(weighted * resid, 1, keepdims=True)
    grad = mid_back_ref[...] + inv_rms * weighted - resid * (cubed * mean)
    input_grad_ref[...] = grad.astype(jnp.bfloat16)


def finish(tokens, gains, wide, cosine, sine, mid_back, backs):
    heads = len(backs)
    rows, width = tokens.shape
    return vmem_call(
        functools.partial(finish_kernel, heads=heads),
        [
            jax.ShapeDtypeStruct(tokens.shape, jnp.bfloat16),
            jax.ShapeDtypeStruct((wide.shape[1] // LANES, width, LANES), jnp.float32),
            jax.ShapeDtypeStruct((1, width), jnp.float32),
        ],
        [
            pltpu.VMEM((rows, wide.shape[1]), jnp.bfloat16),
            pltpu.VMEM((width, rows), jnp.bfloat16),
        ],
        "finish",
        tokens, gains, wide, cosine, sine, mid_back, *[part for back in backs for part in back],
    )


def rotary_tables(length, head_dim):
    half_dim = head_dim // 2
    frequency = THETA ** (-(jnp.arange(half_dim, dtype=jnp.float32) * 2.0 / head_dim))
    angles = jnp.arange(length, dtype=jnp.float32)[:, None] * frequency[None, :]
    return (jnp.cos(angles), jnp.sin(angles))


def rotate_heads(field, cosine, sine):
    half_dim = field.shape[-1] // 2
    first_half = field[..., :half_dim]
    second_half = field[..., half_dim:]
    cosine = cosine[None, :, None, :]
    sine = sine[None, :, None, :]
    return jnp.concatenate(
        [first_half * cosine - second_half * sine, second_half * cosine + first_half * sine], -1
    )


def normalize(hidden, gain):
    inv_rms = lax.rsqrt(jnp.mean(hidden * hidden, -1, keepdims=True) + EPS)
    return (hidden * inv_rms * gain, inv_rms)


def normalize_back(grad, hidden, inv_rms, gain):
    weighted = grad * gain
    cubed = inv_rms * inv_rms * inv_rms
    hidden_grad = inv_rms * weighted - hidden * cubed * jnp.mean(
        weighted * hidden, -1, keepdims=True
    )
    gain_part = jnp.sum(grad * hidden * inv_rms, 0)
    return (hidden_grad, gain_part)


def outer_prod(left, right):
    return lax.dot_general(
        left, right, (((0,), (0,)), ((), ())), preferred_element_type=jnp.float32
    )


def times_transposed(left, matrix):
    return lax.dot_general(
        left, matrix, (((1,), (1,)), ((), ())), preferred_element_type=jnp.float32
    )


def whole_rows(shapes, devices):
    return (devices & (devices - 1)) == 0 and all(
        rows % (8 * devices // 4) == 0 and rows * wide % (devices * LANES) == 0
        for rows, wide in shapes
    )


def place_of():
    return lax.axis_index("dp").astype(jnp.int32).reshape(1)


class WeightGather:
    def __init__(self, shards, shapes, devices):
        self.shards, self.shapes, self.devices = shards, shapes, devices
        self.stages = whole_rows(shapes, devices)
        if self.stages:
            held = jnp.concatenate([shard.reshape(-1, LANES) for shard in shards])
            self.held = jnp.pad(held, ((0, -held.shape[0] % 16), (0, 0)))

    def line_stage(self, other):
        if not self.stages:
            return other
        _, line = masks_of(self.devices)
        self.held, other = tied(self.held, other)
        self.arrived = [self.held] + [swap(self.held, mask, self.devices) for mask in line[1:]]
        return other

    def plane_stage(self, other):
        if not self.stages:
            return other
        plane, _ = masks_of(self.devices)
        self.held, other = tied(jnp.stack(self.arrived), other)
        self.arrived = [self.held] + [swap(self.held, mask, self.devices) for mask in plane[1:]]
        self.origins = [(0, at, 0) for at in range(len(plane))]
        return other

    def first_half_stage(self, other):
        if not self.stages:
            return other
        plane, _ = masks_of(self.devices)
        cut = self.arrived[0].shape[0] // 2
        halves = [
            jnp.stack([field[at : at + cut] for field in self.arrived]) for at in (0, cut)
        ]
        halves, other = tied(halves, other)
        self.arrived = [
            [half, swap(half, mask, self.devices)] for half, mask in zip(halves, plane[1:3])
        ]
        return other

    def second_half_stage(self, other):
        if not self.stages:
            return other
        plane, _ = masks_of(self.devices)
        pairs, other = tied(self.arrived, other)
        cut = pairs[0][0].shape[1]
        self.arrived, self.origins = [], []
        for at, pair in enumerate(pairs):
            near, far = (1, 2) if at == 0 else (2, 1)
            self.arrived += pair + [swap(field, plane[far], self.devices) for field in pair]
            self.origins += [(0, where, at * cut) for where in (0, near, far, 3)]
        return other

    def core_stage(self, other, joined):
        if not self.stages:
            return other
        self.arrived, other = tied(self.arrived, other)
        if joined:
            self.arrived, self.origins = [jnp.concatenate(self.arrived)], [(0, 0, 0)]
        self.origins += [(1, where, offset) for _, where, offset in self.origins]
        self.got = [swap(field, CORE_MASK, self.devices) for field in self.arrived]
        return other

    def result(self, joined):
        if not self.stages:
            mats = [
                lax.all_gather(shard, "dp", axis=0, tiled=True).reshape(shape)
                for shard, shape in zip(self.shards, self.shapes)
            ]
            if not joined:
                return mats
            pads = [((0, 0), (0, tiles_of(mat.shape[1]) * LANES - mat.shape[1])) for mat in mats]
            return [jnp.concatenate([jnp.pad(mat, pad) for mat, pad in zip(mats, pads)], 1)]
        pieces = self.arrived + self.got
        return unpack_pieces(
            place_of(), pieces, tuple(self.origins), self.shapes, self.devices, joined
        )


def tied(first, second):
    return lax.optimization_barrier((first, second))


class GradSum:
    def __init__(self, grads, shapes, devices, extra=None):
        self.grads, self.shapes, self.devices, self.extra = grads, shapes, devices, extra
        self.stages = whole_rows(shapes, devices)
        if self.stages:
            self.kept, self.sent = pack_grads(place_of(), grads, shapes, devices, extra)

    def core_stage(self, other):
        if not self.stages:
            return other
        (self.kept, self.sent), other = tied((self.kept, self.sent), other)
        self.got = swap(self.sent, CORE_MASK, self.devices)
        return other

    def plane_stage(self, other):
        if not self.stages:
            return other
        plane, _ = masks_of(self.devices)
        block = self.kept.shape[0] // len(plane)
        cuts = [slice(at * block, (at + 1) * block) for at in range(len(plane))]
        parts = [(widen(self.kept[cut]) + widen(self.got[cut])).astype(jnp.bfloat16) for cut in cuts]
        self.parts, other = tied(parts, other)
        self.groups = [
            [self.parts[0]]
            + [swap(part, mask, self.devices) for part, mask in zip(self.parts[1:], plane[1:])]
        ]
        return other

    def first_half_stage(self, other):
        if not self.stages:
            return other
        plane, _ = masks_of(self.devices)
        block, cut = self.kept.shape[0] // len(plane), self.kept.shape[1] // 2
        parts = []
        for half in range(2):
            rows = slice(half * cut, (half + 1) * cut)
            cuts = [slice(at * block, (at + 1) * block) for at in range(len(plane))]
            parts.append(
                [
                    (widen(self.kept[at, rows]) + widen(self.got[at, rows])).astype(jnp.bfloat16)
                    for at in cuts
                ]
            )
        self.parts, other = tied(parts, other)
        self.arrived = [
            [swap(part[at], plane[near], self.devices) for at in (near, 3)]
            for part, near in zip(self.parts, (1, 2))
        ]
        return other

    def second_half_stage(self, other):
        if not self.stages:
            return other
        plane, _ = masks_of(self.devices)
        sends = [
            (widen(part[far]) + widen(arrived[1])).astype(jnp.bfloat16)
            for part, arrived, far in zip(self.parts, self.arrived, (2, 1))
        ]
        sends, other = tied(sends, other)
        self.groups = [
            [part[0], arrived[0], swap(send, plane[far], self.devices)]
            for part, arrived, send, far in zip(self.parts, self.arrived, sends, (2, 1))
        ]
        return other

    def line_stage(self, other):
        if not self.stages:
            return other
        _, line = masks_of(self.devices)
        parts = [
            jnp.concatenate(
                [
                    tree_sum([widen(term[at]) for term in terms]).astype(jnp.bfloat16)
                    for terms in self.groups
                ]
            )
            for at in range(len(line))
        ]
        self.parts, other = tied(parts, other)
        self.arrived = [
            swap(part, mask, self.devices) for part, mask in zip(self.parts[1:], line[1:])
        ]
        return other

    def result(self):
        if not self.stages:
            grads = [
                grad.swapaxes(0, 1).reshape(rows, -1)[:, :wide] if grad.ndim == 3 else grad
                for grad, (rows, wide) in zip(self.grads, self.shapes)
            ]
            sums = [
                lax.psum_scatter(grad.reshape(-1), "dp", scatter_dimension=0, tiled=True)
                for grad in grads
            ]
            return sums if self.extra is None else sums + [lax.psum(self.extra, "dp")]
        pieces = tree_sum([widen(term) for term in [self.parts[0]] + self.arrived])
        sums, start = [], 0
        for rows, wide in self.shapes:
            count = rows * wide // (self.devices * LANES)
            sums.append(pieces[start : start + count].reshape(-1))
            start += count
        if self.extra is not None:
            count = self.extra.size // LANES
            sums.append(pieces[start : start + count].reshape(self.extra.shape))
        return sums


def body(tokens, cotangent, w_query, w_key, w_value, w_out, w_gate, w_up, w_down, norm_gains):
    model_width = tokens.shape[1]
    seq_count = tokens.shape[0] // LENGTH
    group_size = HEADS // KV_HEADS
    scale_factor = HEAD_DIM ** (-0.5)
    gain_f = norm_gains.astype(jnp.float32)
    shards = (w_query, w_key, w_value, w_out, w_gate, w_up, w_down)
    devices = lax.axis_size("dp")
    widths = [shards[at].shape[0] * devices // model_width for at in range(6)]
    shapes = [(model_width, wide) for wide in widths] + [
        (shards[6].shape[0] * devices // model_width, model_width)
    ]
    first = WeightGather(shards[:3], shapes[:3], devices)
    rest = (4, 5, 6, 3)
    second = WeightGather(
        [shards[at] for at in rest], [shapes[at] for at in rest], devices
    )
    tokens = first.line_stage(tokens)
    if first.stages:
        first.arrived[1] = second.line_stage(first.arrived[1])
    tokens = first.plane_stage(tokens)
    tokens = first.core_stage(tokens, True)
    if first.stages:
        first.got = second.first_half_stage(first.got)
    (wide_mat,) = first.result(True)
    resid_in = tokens.astype(jnp.float32)
    cosine, sine = rotary_tables(LENGTH, HEAD_DIM)
    pairs = LANES // HEAD_DIM
    cosine = jnp.tile(cosine, (seq_count, 2 * pairs))
    sine = jnp.tile(jnp.concatenate([sine, -sine], 1), (seq_count, pairs))
    fields = project(tokens, norm_gains, wide_mat, cosine, sine)
    fields = second.second_half_stage(fields)
    attended = [attend(fields, head, group_size) for head in range(2)]
    fields, attended = second.core_stage((fields, attended), False)
    attended.append(attend(fields, 2, group_size))
    wg_mat, wu_mat, wd_mat, wo_mat = second.result(False)
    mixed = jnp.concatenate([part for part, _ in attended], 1)
    attn_out = jnp.dot(mixed, wo_mat, preferred_element_type=jnp.float32)
    middle = resid_in + attn_out
    normed_two, rms_two = normalize(middle, gain_f[1])
    normed_two = normed_two.astype(jnp.bfloat16)
    gate = jnp.dot(normed_two, wg_mat, preferred_element_type=jnp.float32)
    upward = jnp.dot(normed_two, wu_mat, preferred_element_type=jnp.float32)
    sigmoid_g = jax.nn.sigmoid(gate)
    activated = gate * sigmoid_g
    hidden = (activated * upward).astype(jnp.bfloat16)
    ffn_out = jnp.dot(hidden, wd_mat, preferred_element_type=jnp.float32)
    output = (middle + ffn_out).astype(jnp.bfloat16)
    grad_down = outer_prod(hidden, cotangent)
    hidden_back = times_transposed(cotangent, wd_mat)
    gate_back = (hidden_back * upward * sigmoid_g * (1.0 + gate * (1.0 - sigmoid_g))).astype(
        jnp.bfloat16
    )
    up_back = (hidden_back * activated).astype(jnp.bfloat16)
    grad_gate = outer_prod(normed_two, gate_back)
    grad_up = outer_prod(normed_two, up_back)
    two_back = times_transposed(gate_back, wg_mat) + times_transposed(up_back, wu_mat)
    norm_two_back, gain_two = normalize_back(two_back, middle, rms_two, gain_f[1])
    mid_back = cotangent.astype(jnp.float32) + norm_two_back
    mid_low = mid_back.astype(jnp.bfloat16)
    grad_out = outer_prod(mixed, mid_low)
    mixed_back = times_transposed(mid_low, wo_mat).astype(jnp.bfloat16)
    feed_sum = GradSum(
        (grad_gate, grad_up, grad_down, grad_out), [shapes[at] for at in rest], devices
    )

    def back_of(head, field):
        part, total = attended[head]
        return attend_back(fields, field, part, total, head, group_size)

    mixed_back = feed_sum.core_stage(mixed_back)
    backs = [back_of(0, mixed_back)]
    mixed_back, _ = tied(mixed_back, backs[0])
    mixed_back = feed_sum.first_half_stage(mixed_back)
    backs.append(back_of(1, mixed_back))
    mixed_back, backs = feed_sum.second_half_stage((mixed_back, backs))
    backs.append(back_of(2, mixed_back))
    backs = feed_sum.line_stage(backs)
    input_grad, tiled, gain_one = finish(tokens, norm_gains, wide_mat, cosine, sine, mid_back, backs)
    gains_back = jnp.concatenate([gain_one, gain_two[None]], 0)
    cuts = [0]
    for _, wide in shapes[:3]:
        cuts.append(cuts[-1] + tiles_of(wide))
    grads = tuple(tiled[start:stop] for start, stop in zip(cuts, cuts[1:]))
    mix_sum = GradSum(grads, shapes[:3], devices, gains_back)
    if feed_sum.stages:
        feed_sum.arrived = mix_sum.core_stage(feed_sum.arrived)
    input_grad = mix_sum.plane_stage(input_grad)
    input_grad = mix_sum.line_stage(input_grad)
    mix_parts = mix_sum.result()
    gate_part, up_part, down_part, out_part = feed_sum.result()
    all_parts = mix_parts[:3] + [out_part, gate_part, up_part, down_part]
    gain_grad = mix_parts[3]
    return (output, input_grad) + tuple(all_parts) + (gain_grad,)


def solution(mesh):
    return jax.shard_map(
        body,
        mesh=mesh,
        in_specs=(
            P("dp", None),
            P("dp", None),
            P("dp"),
            P("dp"),
            P("dp"),
            P("dp"),
            P("dp"),
            P("dp"),
            P("dp"),
            P(),
        ),
        out_specs=(
            P("dp", None),
            P("dp", None),
            P("dp"),
            P("dp"),
            P("dp"),
            P("dp"),
            P("dp"),
            P("dp"),
            P("dp"),
            P(),
        ),
        check_vma=False,
    )
```

```python
import functools

import jax
import jax.numpy as jnp
from jax import lax
from jax.experimental import pallas as pl
from jax.experimental.pallas import tpu as pltpu
from jax.sharding import PartitionSpec as P

HEADS = 9
KV_HEADS = 3
HEAD_DIM = 64
LENGTH = 1024


EPS = 1e-05
THETA = 100000.0
NEG_BIG = -1e30
LANES = 128
VMEM_LIMIT = 56 * 1024 * 1024
CORE_MASK = 1
LIGHT = pl.CostEstimate(flops=10**8, bytes_accessed=10**6, transcendentals=0)


def masks_of(devices):
    plane = tuple(2 * step for step in range(4))
    line = tuple(8 * step for step in range(devices // 8))
    return (plane, line)


def swap(field, mask, devices):
    return lax.ppermute(field, "dp", [(place, place ^ mask) for place in range(devices)])


def tree_sum(terms):
    while len(terms) > 1:
        odd = terms[len(terms) // 2 * 2 :]
        terms = [terms[at] + terms[at + 1] for at in range(0, len(terms) - 1, 2)] + odd
    return terms[0]


def widen(field):
    return field.astype(jnp.float32)


def slot_mask(core, slot, devices):
    line = devices // 8
    return core * CORE_MASK + 2 * (slot // line) + 8 * (slot % line)


def tiles_of(wide):
    return -(-wide // LANES)


def tile_widths(wide):
    return [min(LANES, wide - at) for at in range(0, wide, LANES)]


def flat_starts(shapes, devices):
    starts = [0]
    for rows, wide in shapes:
        starts.append(starts[-1] + rows * wide // (devices * LANES))
    return starts


def tiled_shapes(shapes):
    return [(tiles_of(wide), rows, LANES) for rows, wide in shapes if wide % LANES]


def unpack_kernel(place_ref, *refs, devices, shapes, joined, origins):
    count = len(origins)
    pieces, refs = refs[:count], refs[count:]
    out_count = 1 if joined else len(shapes)
    outs, flats, refs = refs[:out_count], refs[out_count : out_count + len(shapes)], refs[out_count + len(shapes) :]
    stage, landed, arrival, tiled_refs = refs[0], refs[1], refs[2], list(refs[3:])
    place = place_ref[0]
    starts = flat_starts(shapes, devices)
    block = pieces[0].shape[0]
    copies = [
        pltpu.make_async_copy(piece, landed.at[index], arrival.at[index])
        for index, piece in enumerate(pieces)
    ]
    for copy in copies:
        copy.start()
    for index, (core, plane, offset) in enumerate(origins):
        copies[index].wait()
        piece_ref = landed.at[index]
        cuts = []
        for flat, start, stop in zip(flats, starts, starts[1:]):
            low, high = max(start, offset), min(stop, offset + piece_ref.shape[1])
            if low < high:
                cuts.append((flat, stop - start, low - start, low - offset, high - offset))

        def load(slot, carry, core=core, plane=plane, piece_ref=piece_ref, cuts=cuts):
            owner = place ^ slot_mask(core, plane * block + slot, devices)
            piece = piece_ref[slot].astype(jnp.float32)
            if any(low % 8 for _, _, _, low, _ in cuts):
                stage[slot % 4] = piece
            for flat, each, inner, low, high in cuts:
                rows = stage[slot % 4, low:high, :] if low % 8 else piece[low:high]
                flat[pl.ds(owner * each + inner, high - low), :] = rows
            return carry

        lax.fori_loop(0, block, load, 0)
    column = 0
    for index, ((rows, wide), flat) in enumerate(zip(shapes, flats)):
        out = outs[0 if joined else index]
        whole = wide // LANES
        if wide % LANES == 0:
            for at in range(whole):
                tile = flat[pl.ds(at, rows, stride=whole), :]
                out[:, column + at * LANES : column + (at + 1) * LANES] = tile.astype(jnp.bfloat16)
        else:
            target = tiled_refs.pop(0)
            pairs, tiles_in = rows // 2, 2 * wide // LANES
            for at in range(whole + 1):
                target[at, pl.ds(0, pairs, stride=2), :] = flat[pl.ds(at, pairs, stride=tiles_in), :]
            rolled = None
            for at in range(whole, tiles_in):
                after = pltpu.roll(flat[pl.ds(at, pairs, stride=tiles_in), :], LANES // 2, 1)
                if rolled is not None:
                    lane = lax.broadcasted_iota(jnp.int32, after.shape, 1)
                    target[at - whole - 1, pl.ds(1, pairs, stride=2), :] = jnp.where(
                        lane < LANES // 2, rolled, after
                    )
                rolled = after
            target[whole, pl.ds(1, pairs, stride=2), :] = rolled
            for at, width in enumerate(tile_widths(wide)):
                tile = target[at]
                if joined and width < LANES:
                    lane = lax.broadcasted_iota(jnp.int32, tile.shape, 1)
                    tile = jnp.where(lane < width, tile, 0.0)
                    width = LANES
                start = column + at * LANES
                out[:, start : start + width] = tile[:, :width].astype(jnp.bfloat16)
        if joined:
            column += tiles_of(wide) * LANES


def unpack_pieces(place, pieces, origins, shapes, devices, joined):
    rows_in = pieces[0].shape[1]
    outs = shapes
    if joined:
        outs = [(shapes[0][0], sum(tiles_of(wide) for _, wide in shapes) * LANES)]
    return pl.pallas_call(
        functools.partial(
            unpack_kernel, devices=devices, shapes=shapes, joined=joined, origins=origins
        ),
        out_shape=[jax.ShapeDtypeStruct(shape, jnp.bfloat16) for shape in outs],
        in_specs=[pl.BlockSpec(memory_space=pltpu.SMEM)]
        + [pl.BlockSpec(memory_space=pl.ANY)] * len(pieces),
        out_specs=[pl.BlockSpec(memory_space=pltpu.VMEM)] * len(outs),
        scratch_shapes=[
            pltpu.VMEM((rows * wide // LANES, LANES), jnp.float32) for rows, wide in shapes
        ]
        + [
            pltpu.VMEM((4, rows_in, LANES), jnp.float32),
            pltpu.VMEM((len(pieces),) + pieces[0].shape, jnp.bfloat16),
            pltpu.SemaphoreType.DMA((len(pieces),)),
        ]
        + [pltpu.VMEM(shape, jnp.float32) for shape in tiled_shapes(shapes)],
        compiler_params=pltpu.CompilerParams(vmem_limit_bytes=VMEM_LIMIT),
        cost_estimate=LIGHT,
        name="unpack",
    )(place, *pieces)


def pack_kernel(place_ref, *refs, devices, shapes, tiled_in, extra):
    count = len(shapes) + (1 if extra else 0)
    sources, kept_ref, sent_ref, stage = refs[:count], refs[count], refs[count + 1], refs[count + 2]
    flats = refs[count + 3 : count + 3 + len(shapes)]
    tiled_refs = list(refs[count + 3 + len(shapes) :])
    place = place_ref[0]
    starts = flat_starts(shapes, devices)
    for index, ((rows, wide), flat) in enumerate(zip(shapes, flats)):
        source, whole = sources[index], wide // LANES
        if wide % LANES == 0:
            for at in range(whole):
                flat[pl.ds(at, rows, stride=whole), :] = (
                    source[at] if tiled_in[index] else source[:, at * LANES : (at + 1) * LANES]
                )
            continue
        if not tiled_in[index]:
            tiled = tiled_refs.pop(0)
            for at, width in enumerate(tile_widths(wide)):
                tiled[at, :, :width] = source[:, at * LANES : at * LANES + width]
            source = tiled
        pairs, tiles_in = rows // 2, 2 * wide // LANES
        for at in range(whole):
            flat[pl.ds(at, pairs, stride=tiles_in), :] = source[at, pl.ds(0, pairs, stride=2), :]
        before = source[whole, pl.ds(0, pairs, stride=2), :]
        lane = lax.broadcasted_iota(jnp.int32, before.shape, 1)
        for at in range(whole + 1):
            rolled = pltpu.roll(source[at, pl.ds(1, pairs, stride=2), :], LANES // 2, 1)
            flat[pl.ds(whole + at, pairs, stride=tiles_in), :] = jnp.where(
                lane < LANES // 2, before, rolled
            )
            before = rolled
    row_tiles = []
    if extra:
        row = jnp.concatenate([sources[-1][at : at + 1, :] for at in range(extra[0])], 1)
        row_tiles = [
            row[:, at * LANES : (at + 1) * LANES] for at in range(extra[0] * extra[1] // LANES)
        ]
    direct = not extra and all(start % 8 == 0 for start in starts)
    if not direct:
        for at in range(4):
            for index, tile in enumerate(row_tiles):
                stage[at, starts[-1] + index : starts[-1] + index + 1, :] = tile
            used = starts[-1] + len(row_tiles)
            if used < stage.shape[1]:
                stage[at, used:, :] = jnp.zeros((stage.shape[1] - used, LANES), jnp.float32)
    for core, pieces in enumerate((kept_ref, sent_ref)):

        def store(slot, carry, core=core, pieces=pieces):
            owner = place ^ slot_mask(core, slot, devices)
            parts = []
            for flat, start, stop in zip(flats, starts, starts[1:]):
                rows = flat[pl.ds(owner * (stop - start), stop - start), :]
                if direct:
                    parts.append(rows)
                else:
                    stage[slot % 4, start:stop, :] = rows
            spare = stage.shape[1] - starts[-1]
            if direct and spare:
                parts.append(jnp.zeros((spare, LANES), jnp.float32))
            piece = jnp.concatenate(parts, 0) if direct else stage[slot % 4]
            pieces[slot] = piece.astype(jnp.bfloat16)
            return carry

        lax.fori_loop(0, devices // 2, store, 0)


def pack_grads(place, grads, shapes, devices, extra):
    rows_out = sum(rows * wide for rows, wide in shapes) // (devices * LANES)
    sources = list(grads)
    if extra is not None:
        rows_out += extra.size // LANES
        sources.append(extra)
    rows_out = -(-rows_out // 16) * 16
    tiled_in = tuple(grad.ndim == 3 for grad in grads)
    half = jax.ShapeDtypeStruct((devices // 2, rows_out, LANES), jnp.bfloat16)
    untiled = [shape for shape, tiled in zip(shapes, tiled_in) if not tiled]
    return pl.pallas_call(
        functools.partial(
            pack_kernel, devices=devices, shapes=shapes, tiled_in=tiled_in,
            extra=None if extra is None else extra.shape,
        ),
        out_shape=[half, half],
        in_specs=[pl.BlockSpec(memory_space=pltpu.SMEM)]
        + [pl.BlockSpec(memory_space=pltpu.VMEM)] * len(sources),
        out_specs=[pl.BlockSpec(memory_space=pltpu.VMEM)] * 2,
        scratch_shapes=[pltpu.VMEM((4, rows_out, LANES), jnp.float32)]
        + [pltpu.VMEM((rows * wide // LANES, LANES), jnp.float32) for rows, wide in shapes]
        + [pltpu.VMEM(shape, jnp.float32) for shape in tiled_shapes(untiled)],
        compiler_params=pltpu.CompilerParams(vmem_limit_bytes=VMEM_LIMIT),
        cost_estimate=LIGHT,
        name="pack",
    )(place, *sources)


BLOCK = 256


def dot_nt(left, right):
    return lax.dot_general(
        left, right, (((1,), (1,)), ((), ())), preferred_element_type=jnp.float32
    )


def dot_tn(left, right):
    return lax.dot_general(
        left, right, (((0,), (0,)), ((), ())), preferred_element_type=jnp.float32
    )


def dot_nn(left, right):
    return jnp.dot(left, right, preferred_element_type=jnp.float32)


def key_columns(head):
    first = tiles_of(HEADS * HEAD_DIM) * LANES + head * HEAD_DIM
    return slice(first, first + HEAD_DIM)


def value_columns(head):
    first = (tiles_of(HEADS * HEAD_DIM) + tiles_of(KV_HEADS * HEAD_DIM)) * LANES + head * HEAD_DIM
    return slice(first, first + HEAD_DIM)


def attend_kernel(fields_ref, mixed_ref, total_ref, *, head, group):
    length = fields_ref.shape[0]
    keys = fields_ref[:, key_columns(head)]
    values = fields_ref[:, value_columns(head)]
    lower = lax.broadcasted_iota(jnp.int32, (BLOCK, BLOCK), 0) >= lax.broadcasted_iota(
        jnp.int32, (BLOCK, BLOCK), 1
    )
    lane = lax.broadcasted_iota(jnp.int32, (BLOCK, LANES), 1)
    for start in range(0, length, BLOCK):
        mixed, totals_row = [], jnp.zeros((BLOCK, LANES), jnp.float32)
        for member in range(group):
            at = (head * group + member) * HEAD_DIM
            query = fields_ref[start : start + BLOCK, at : at + HEAD_DIM]
            diagonal = jnp.where(lower, dot_nt(query, keys[start : start + BLOCK]), NEG_BIG)
            maxima = jnp.max(diagonal, 1, keepdims=True)
            if start:
                before = dot_nt(query, keys[:start])
                maxima = jnp.maximum(maxima, jnp.max(before, 1, keepdims=True))
            expo = jnp.exp(diagonal - maxima)
            totals = jnp.sum(expo, 1, keepdims=True)
            result = dot_nn(expo.astype(jnp.bfloat16), values[start : start + BLOCK])
            if start:
                expo = jnp.exp(before - maxima)
                totals = totals + jnp.sum(expo, 1, keepdims=True)
                result = result + dot_nn(expo.astype(jnp.bfloat16), values[:start])
            mixed.append(result / totals)
            totals_row = jnp.where(lane == member, maxima + jnp.log(totals), totals_row)
        mixed_ref[start : start + BLOCK, :] = jnp.concatenate(mixed, 1).astype(jnp.bfloat16)
        total_ref[start : start + BLOCK, :] = totals_row


def attend(fields, head, group):
    length = fields.shape[0]
    return pl.pallas_call(
        functools.partial(attend_kernel, head=head, group=group),
        out_shape=[
            jax.ShapeDtypeStruct((length, group * HEAD_DIM), jnp.bfloat16),
            jax.ShapeDtypeStruct((length, LANES), jnp.float32),
        ],
        in_specs=[pl.BlockSpec(memory_space=pltpu.VMEM)],
        out_specs=[pl.BlockSpec(memory_space=pltpu.VMEM)] * 2,
        compiler_params=pltpu.CompilerParams(vmem_limit_bytes=VMEM_LIMIT),
        cost_estimate=LIGHT,
        name="attend",
    )(fields)


def attend_back_kernel(
    fields_ref, back_ref, mixed_ref, total_ref,
    query_back_ref, key_back_ref, queries, backs, totals, deltas, query_sum, key_sum, value_sum,
    *, head, group,
):
    length = fields_ref.shape[0]
    ones = jnp.ones((8, HEAD_DIM), jnp.float32)
    totals[...] = total_ref[...].T[:8]
    for member in range(group):
        at = (head * group + member) * HEAD_DIM
        queries[member] = fields_ref[:, at : at + HEAD_DIM]
        back = back_ref[:, at : at + HEAD_DIM]
        backs[member] = back
        product = back.astype(jnp.float32) * mixed_ref[
            :, member * HEAD_DIM : (member + 1) * HEAD_DIM
        ].astype(jnp.float32)
        deltas[member] = lax.dot_general(
            ones, product, (((1,), (1,)), ((), ())),
            precision=lax.Precision.HIGHEST, preferred_element_type=jnp.float32,
        )
    keys_all = fields_ref[:, key_columns(head)]
    values_all = fields_ref[:, value_columns(head)]
    upper = lax.broadcasted_iota(jnp.int32, (BLOCK, BLOCK), 0) <= lax.broadcasted_iota(
        jnp.int32, (BLOCK, BLOCK), 1
    )
    for member in range(group):
        total_row = totals[member : member + 1, :]
        delta_row = deltas[member][0:1]
        for start in range(0, length, BLOCK):
            keys = keys_all[start : start + BLOCK]
            values = values_all[start : start + BLOCK]
            query = queries[member, start:, :]
            back = backs[member, start:, :]
            scores = dot_nt(keys, query)
            probs = jnp.exp(scores - total_row[:, start:])
            first = jnp.where(upper, probs[:, :BLOCK], 0.0)
            probs = first if start + BLOCK == length else jnp.concatenate(
                [first, probs[:, BLOCK:]], 1
            )
            prob_back = dot_nt(values, back)
            score_back = (probs * (prob_back - delta_row[:, start:])).astype(jnp.bfloat16)
            value_part = dot_nn(probs.astype(jnp.bfloat16), back)
            key_part = dot_nn(score_back, query)
            query_part = dot_tn(score_back, keys)
            if member:
                key_sum[start : start + BLOCK, :] += key_part
                value_sum[start : start + BLOCK, :] += value_part
            else:
                key_sum[start : start + BLOCK, :] = key_part
                value_sum[start : start + BLOCK, :] = value_part
            if start:
                query_sum[member, start:, :] += query_part
            else:
                query_sum[member] = query_part
    query_back_ref[...] = (
        jnp.concatenate([query_sum[member] for member in range(group)], 1) * HEAD_DIM ** (-0.5)
    )
    key_back_ref[...] = jnp.concatenate([key_sum[...], value_sum[...]], 1)


def attend_back(fields, back, mixed, total, head, group):
    length = fields.shape[0]
    return pl.pallas_call(
        functools.partial(attend_back_kernel, head=head, group=group),
        out_shape=[
            jax.ShapeDtypeStruct((length, group * HEAD_DIM), jnp.float32),
            jax.ShapeDtypeStruct((length, 2 * HEAD_DIM), jnp.float32),
        ],
        in_specs=[pl.BlockSpec(memory_space=pltpu.VMEM)] * 4,
        out_specs=[pl.BlockSpec(memory_space=pltpu.VMEM)] * 2,
        scratch_shapes=[
            pltpu.VMEM((group, length, HEAD_DIM), jnp.bfloat16),
            pltpu.VMEM((group, length, HEAD_DIM), jnp.bfloat16),
            pltpu.VMEM((8, length), jnp.float32),
            pltpu.VMEM((group, 8, length), jnp.float32),
            pltpu.VMEM((group, length, HEAD_DIM), jnp.float32),
            pltpu.VMEM((length, HEAD_DIM), jnp.float32),
            pltpu.VMEM((length, HEAD_DIM), jnp.float32),
        ],
        compiler_params=pltpu.CompilerParams(vmem_limit_bytes=VMEM_LIMIT),
        cost_estimate=LIGHT,
        name="attend_back",
    )(fields, back, mixed, total)


def partner_of(tile):
    lane = lax.broadcasted_iota(jnp.int32, tile.shape, 1)
    half = HEAD_DIM // 2
    return jnp.where(
        lane % HEAD_DIM < half, pltpu.roll(tile, LANES - half, 1), pltpu.roll(tile, half, 1)
    )


def first_gain(gains_ref):
    return gains_ref[...].astype(jnp.float32)[0:1]


def normed_rows(tokens_ref, gains_ref):
    resid = tokens_ref[...].astype(jnp.float32)
    inv_rms = lax.rsqrt(jnp.mean(resid * resid, 1, keepdims=True) + EPS)
    return resid, inv_rms, (resid * inv_rms * first_gain(gains_ref)).astype(jnp.bfloat16)


def project_kernel(
    tokens_in, cosine_in, sine_in, gains_ref, wide_ref, fields_ref,
    tokens_ref, cosine_ref, sine_ref, normed, arrival,
):
    copies = [
        pltpu.make_async_copy(source, target, arrival.at[at])
        for at, (source, target) in enumerate(
            ((tokens_in, tokens_ref), (cosine_in, cosine_ref), (sine_in, sine_ref))
        )
    ]
    for copy in copies:
        copy.start()
    for copy in copies:
        copy.wait()
    _, _, normed[...] = normed_rows(tokens_ref, gains_ref)
    first_key = tiles_of(HEADS * HEAD_DIM)
    first_value = first_key + tiles_of(KV_HEADS * HEAD_DIM)
    count = fields_ref.shape[1] // LANES
    for start in range(0, count, 2):
        stop = min(start + 2, count)
        pair = dot_nn(normed[...], wide_ref[:, start * LANES : stop * LANES])
        for at in range(start, stop):
            tile = pair[:, (at - start) * LANES : (at - start + 1) * LANES]
            if at < first_value:
                tile = tile * cosine_ref[...] - partner_of(tile) * sine_ref[...]
            tile = tile.astype(jnp.bfloat16)
            if at < first_key:
                tile = (tile.astype(jnp.float32) * HEAD_DIM ** (-0.5)).astype(jnp.bfloat16)
            fields_ref[:, at * LANES : (at + 1) * LANES] = tile


def vmem_call(kernel, out_shape, scratch_shapes, name, *args):
    single = not isinstance(out_shape, list)
    return pl.pallas_call(
        kernel,
        out_shape=out_shape,
        in_specs=[pl.BlockSpec(memory_space=pltpu.VMEM)] * len(args),
        out_specs=pl.BlockSpec(memory_space=pltpu.VMEM)
        if single
        else [pl.BlockSpec(memory_space=pltpu.VMEM)] * len(out_shape),
        scratch_shapes=scratch_shapes,
        compiler_params=pltpu.CompilerParams(vmem_limit_bytes=VMEM_LIMIT),
        cost_estimate=LIGHT,
        name=name,
    )(*args)


def project(tokens, gains, wide, cosine, sine):
    return pl.pallas_call(
        project_kernel,
        out_shape=jax.ShapeDtypeStruct((tokens.shape[0], wide.shape[1]), jnp.bfloat16),
        in_specs=[pl.BlockSpec(memory_space=pl.ANY)] * 3
        + [pl.BlockSpec(memory_space=pltpu.VMEM)] * 2,
        out_specs=pl.BlockSpec(memory_space=pltpu.VMEM),
        scratch_shapes=[
            pltpu.VMEM(tokens.shape, tokens.dtype),
            pltpu.VMEM(cosine.shape, cosine.dtype),
            pltpu.VMEM(sine.shape, sine.dtype),
            pltpu.VMEM(tokens.shape, jnp.bfloat16),
            pltpu.SemaphoreType.DMA((3,)),
        ],
        compiler_params=pltpu.CompilerParams(vmem_limit_bytes=VMEM_LIMIT),
        cost_estimate=LIGHT,
        name="project",
    )(tokens, cosine, sine, gains, wide)


def finish_kernel(
    tokens_ref, gains_ref, wide_ref, cosine_ref, sine_ref, mid_back_ref, *refs, heads
):
    backs = refs[: 2 * heads]
    input_grad_ref, gain_ref, *tiled_refs, fields, normed_t = refs[2 * heads :]
    places = [(ref, at) for ref in tiled_refs for at in range(ref.shape[0])]
    half = HEAD_DIM
    group = HEADS // heads
    wide_heads = [(backs[2 * (at // group)], at % group * half) for at in range(HEADS)]
    wide_heads += [None] * (HEADS % 2)
    for offset in (0, half):
        wide_heads += [(backs[2 * at + 1], offset) for at in range(heads)] + [None] * (heads % 2)
    turned = tiles_of(HEADS * HEAD_DIM) + tiles_of(heads * HEAD_DIM)
    for at in range(len(wide_heads) // 2):
        cols = []
        for item in wide_heads[2 * at : 2 * at + 2]:
            if item is None:
                cols.append(jnp.zeros((fields.shape[0], half), jnp.float32))
            else:
                cols.append(item[0][:, item[1] : item[1] + half])
        tile = jnp.concatenate(cols, 1)
        if at < turned:
            tile = tile * cosine_ref[...] + partner_of(tile) * sine_ref[...]
        fields[:, at * LANES : (at + 1) * LANES] = tile.astype(jnp.bfloat16)
    resid, inv_rms, normed = normed_rows(tokens_ref, gains_ref)
    normed_t[...] = normed.T
    count = fields.shape[1] // LANES
    for start in range(0, count, 2):
        stop = min(start + 2, count)
        pair = dot_nn(normed_t[...], fields[:, start * LANES : stop * LANES])
        for at in range(start, stop):
            ref, inner = places[at]
            ref[inner] = pair[:, (at - start) * LANES : (at - start + 1) * LANES]
    one_back = dot_nt(fields[...], wide_ref[...])
    weighted = one_back * first_gain(gains_ref)
    cubed = inv_rms * inv_rms * inv_rms
    scaled = resid * inv_rms
    gain_ref[...] = jnp.sum(one_back * scaled, 0, keepdims=True)
    mean = jnp.mean(weighted * resid, 1, keepdims=True)
    grad = mid_back_ref[...] + inv_rms * weighted - resid * (cubed * mean)
    input_grad_ref[...] = grad.astype(jnp.bfloat16)


def finish(tokens, gains, wide, cosine, sine, mid_back, backs):
    heads = len(backs)
    rows, width = tokens.shape
    return vmem_call(
        functools.partial(finish_kernel, heads=heads),
        [
            jax.ShapeDtypeStruct(tokens.shape, jnp.bfloat16),
            jax.ShapeDtypeStruct((1, width), jnp.float32),
        ]
        + [
            jax.ShapeDtypeStruct((tiles_of(count * HEAD_DIM), width, LANES), jnp.float32)
            for count in (HEADS, heads, heads)
        ],
        [
            pltpu.VMEM((rows, wide.shape[1]), jnp.bfloat16),
            pltpu.VMEM((width, rows), jnp.bfloat16),
        ],
        "finish",
        tokens, gains, wide, cosine, sine, mid_back, *[part for back in backs for part in back],
    )


def rotary_tables(length, head_dim):
    half_dim = head_dim // 2
    frequency = THETA ** (-(jnp.arange(half_dim, dtype=jnp.float32) * 2.0 / head_dim))
    angles = jnp.arange(length, dtype=jnp.float32)[:, None] * frequency[None, :]
    return (jnp.cos(angles), jnp.sin(angles))


def rotate_heads(field, cosine, sine):
    half_dim = field.shape[-1] // 2
    first_half = field[..., :half_dim]
    second_half = field[..., half_dim:]
    cosine = cosine[None, :, None, :]
    sine = sine[None, :, None, :]
    return jnp.concatenate(
        [first_half * cosine - second_half * sine, second_half * cosine + first_half * sine], -1
    )


def normalize(hidden, gain):
    inv_rms = lax.rsqrt(jnp.mean(hidden * hidden, -1, keepdims=True) + EPS)
    return (hidden * inv_rms * gain, inv_rms)


def normalize_back(grad, hidden, inv_rms, gain):
    weighted = grad * gain
    cubed = inv_rms * inv_rms * inv_rms
    hidden_grad = inv_rms * weighted - hidden * cubed * jnp.mean(
        weighted * hidden, -1, keepdims=True
    )
    gain_part = jnp.sum(grad * hidden * inv_rms, 0)
    return (hidden_grad, gain_part)


def outer_prod(left, right):
    return lax.dot_general(
        left, right, (((0,), (0,)), ((), ())), preferred_element_type=jnp.float32
    )


def times_transposed(left, matrix):
    return lax.dot_general(
        left, matrix, (((1,), (1,)), ((), ())), preferred_element_type=jnp.float32
    )


def whole_rows(shapes, devices):
    return (devices & (devices - 1)) == 0 and all(
        rows % (8 * devices // 4) == 0 and rows * wide % (devices * LANES) == 0
        for rows, wide in shapes
    )


def place_of():
    return lax.axis_index("dp").astype(jnp.int32).reshape(1)


class WeightGather:
    def __init__(self, shards, shapes, devices):
        self.shards, self.shapes, self.devices = shards, shapes, devices
        self.stages = whole_rows(shapes, devices)
        if self.stages:
            held = jnp.concatenate([shard.reshape(-1, LANES) for shard in shards])
            self.held = jnp.pad(held, ((0, -held.shape[0] % 16), (0, 0)))

    def line_stage(self, other):
        if not self.stages:
            return other
        _, line = masks_of(self.devices)
        self.held, other = tied(self.held, other)
        self.arrived = [self.held] + [swap(self.held, mask, self.devices) for mask in line[1:]]
        return other

    def plane_stage(self, other):
        if not self.stages:
            return other
        plane, _ = masks_of(self.devices)
        self.held, other = tied(jnp.stack(self.arrived), other)
        self.arrived = [self.held] + [swap(self.held, mask, self.devices) for mask in plane[1:]]
        self.origins = [(0, at, 0) for at in range(len(plane))]
        return other

    def first_half_stage(self, other):
        if not self.stages:
            return other
        plane, _ = masks_of(self.devices)
        cut = self.arrived[0].shape[0] // 2
        halves = [
            jnp.stack([field[at : at + cut] for field in self.arrived]) for at in (0, cut)
        ]
        halves, other = tied(halves, other)
        self.arrived = [
            [half, swap(half, mask, self.devices)] for half, mask in zip(halves, plane[1:3])
        ]
        return other

    def second_half_stage(self, other):
        if not self.stages:
            return other
        plane, _ = masks_of(self.devices)
        pairs, other = tied(self.arrived, other)
        cut = pairs[0][0].shape[1]
        self.arrived, self.origins = [], []
        for at, pair in enumerate(pairs):
            near, far = (1, 2) if at == 0 else (2, 1)
            self.arrived += pair + [swap(field, plane[far], self.devices) for field in pair]
            self.origins += [(0, where, at * cut) for where in (0, near, far, 3)]
        return other

    def core_stage(self, other, joined):
        if not self.stages:
            return other
        self.arrived, other = tied(self.arrived, other)
        if joined:
            self.arrived, self.origins = [jnp.concatenate(self.arrived)], [(0, 0, 0)]
        self.origins += [(1, where, offset) for _, where, offset in self.origins]
        self.got = [swap(field, CORE_MASK, self.devices) for field in self.arrived]
        return other

    def result(self, joined):
        if not self.stages:
            mats = [
                lax.all_gather(shard, "dp", axis=0, tiled=True).reshape(shape)
                for shard, shape in zip(self.shards, self.shapes)
            ]
            if not joined:
                return mats
            pads = [((0, 0), (0, tiles_of(mat.shape[1]) * LANES - mat.shape[1])) for mat in mats]
            return [jnp.concatenate([jnp.pad(mat, pad) for mat, pad in zip(mats, pads)], 1)]
        pieces = self.arrived + self.got
        return unpack_pieces(
            place_of(), pieces, tuple(self.origins), self.shapes, self.devices, joined
        )


def tied(first, second):
    return lax.optimization_barrier((first, second))


class GradSum:
    def __init__(self, grads, shapes, devices, extra=None):
        self.grads, self.shapes, self.devices, self.extra = grads, shapes, devices, extra
        self.stages = whole_rows(shapes, devices)
        if self.stages:
            self.kept, self.sent = pack_grads(place_of(), grads, shapes, devices, extra)

    def core_stage(self, other):
        if not self.stages:
            return other
        (self.kept, self.sent), other = tied((self.kept, self.sent), other)
        self.got = swap(self.sent, CORE_MASK, self.devices)
        return other

    def plane_stage(self, other):
        if not self.stages:
            return other
        plane, _ = masks_of(self.devices)
        block = self.kept.shape[0] // len(plane)
        cuts = [slice(at * block, (at + 1) * block) for at in range(len(plane))]
        parts = [(widen(self.kept[cut]) + widen(self.got[cut])).astype(jnp.bfloat16) for cut in cuts]
        self.parts, other = tied(parts, other)
        self.groups = [
            [self.parts[0]]
            + [swap(part, mask, self.devices) for part, mask in zip(self.parts[1:], plane[1:])]
        ]
        return other

    def first_half_stage(self, other):
        if not self.stages:
            return other
        plane, _ = masks_of(self.devices)
        block, cut = self.kept.shape[0] // len(plane), self.kept.shape[1] // 2
        parts = []
        for half in range(2):
            rows = slice(half * cut, (half + 1) * cut)
            cuts = [slice(at * block, (at + 1) * block) for at in range(len(plane))]
            parts.append(
                [
                    (widen(self.kept[at, rows]) + widen(self.got[at, rows])).astype(jnp.bfloat16)
                    for at in cuts
                ]
            )
        self.parts, other = tied(parts, other)
        self.arrived = [
            [swap(part[at], plane[near], self.devices) for at in (near, 3)]
            for part, near in zip(self.parts, (1, 2))
        ]
        return other

    def second_half_stage(self, other):
        if not self.stages:
            return other
        plane, _ = masks_of(self.devices)
        sends = [
            (widen(part[far]) + widen(arrived[1])).astype(jnp.bfloat16)
            for part, arrived, far in zip(self.parts, self.arrived, (2, 1))
        ]
        sends, other = tied(sends, other)
        self.groups = [
            [part[0], arrived[0], swap(send, plane[far], self.devices)]
            for part, arrived, send, far in zip(self.parts, self.arrived, sends, (2, 1))
        ]
        return other

    def line_stage(self, other):
        if not self.stages:
            return other
        _, line = masks_of(self.devices)
        parts = [
            jnp.concatenate(
                [
                    tree_sum([widen(term[at]) for term in terms]).astype(jnp.bfloat16)
                    for terms in self.groups
                ]
            )
            for at in range(len(line))
        ]
        self.parts, other = tied(parts, other)
        self.arrived = [
            swap(part, mask, self.devices) for part, mask in zip(self.parts[1:], line[1:])
        ]
        return other

    def result(self):
        if not self.stages:
            grads = [
                grad.swapaxes(0, 1).reshape(rows, -1)[:, :wide] if grad.ndim == 3 else grad
                for grad, (rows, wide) in zip(self.grads, self.shapes)
            ]
            sums = [
                lax.psum_scatter(grad.reshape(-1), "dp", scatter_dimension=0, tiled=True)
                for grad in grads
            ]
            return sums if self.extra is None else sums + [lax.psum(self.extra, "dp")]
        pieces = tree_sum([widen(term) for term in [self.parts[0]] + self.arrived])
        sums, start = [], 0
        for rows, wide in self.shapes:
            count = rows * wide // (self.devices * LANES)
            sums.append(pieces[start : start + count].reshape(-1))
            start += count
        if self.extra is not None:
            count = self.extra.size // LANES
            sums.append(pieces[start : start + count].reshape(self.extra.shape))
        return sums


def body(tokens, cotangent, w_query, w_key, w_value, w_out, w_gate, w_up, w_down, norm_gains):
    model_width = tokens.shape[1]
    seq_count = tokens.shape[0] // LENGTH
    group_size = HEADS // KV_HEADS
    scale_factor = HEAD_DIM ** (-0.5)
    gain_f = norm_gains.astype(jnp.float32)
    shards = (w_query, w_key, w_value, w_out, w_gate, w_up, w_down)
    devices = lax.axis_size("dp")
    widths = [shards[at].shape[0] * devices // model_width for at in range(6)]
    shapes = [(model_width, wide) for wide in widths] + [
        (shards[6].shape[0] * devices // model_width, model_width)
    ]
    first = WeightGather(shards[:3], shapes[:3], devices)
    rest = (4, 5, 6, 3)
    second = WeightGather(
        [shards[at] for at in rest], [shapes[at] for at in rest], devices
    )
    tokens = first.line_stage(tokens)
    if first.stages:
        first.arrived[1] = second.line_stage(first.arrived[1])
    tokens = first.plane_stage(tokens)
    tokens = first.core_stage(tokens, True)
    if first.stages:
        first.got = second.first_half_stage(first.got)
    (wide_mat,) = first.result(True)
    resid_in = tokens.astype(jnp.float32)
    cosine, sine = rotary_tables(LENGTH, HEAD_DIM)
    pairs = LANES // HEAD_DIM
    cosine = jnp.tile(cosine, (seq_count, 2 * pairs))
    sine = jnp.tile(jnp.concatenate([sine, -sine], 1), (seq_count, pairs))
    fields = project(tokens, norm_gains, wide_mat, cosine, sine)
    fields = second.second_half_stage(fields)
    attended = [attend(fields, head, group_size) for head in range(2)]
    fields, attended = second.core_stage((fields, attended), False)
    attended.append(attend(fields, 2, group_size))
    wg_mat, wu_mat, wd_mat, wo_mat = second.result(False)
    mixed = jnp.concatenate([part for part, _ in attended], 1)
    attn_out = jnp.dot(mixed, wo_mat, preferred_element_type=jnp.float32)
    middle = resid_in + attn_out
    normed_two, rms_two = normalize(middle, gain_f[1])
    normed_two = normed_two.astype(jnp.bfloat16)
    gate = jnp.dot(normed_two, wg_mat, preferred_element_type=jnp.float32)
    upward = jnp.dot(normed_two, wu_mat, preferred_element_type=jnp.float32)
    sigmoid_g = jax.nn.sigmoid(gate)
    activated = gate * sigmoid_g
    hidden = (activated * upward).astype(jnp.bfloat16)
    ffn_out = jnp.dot(hidden, wd_mat, preferred_element_type=jnp.float32)
    output = (middle + ffn_out).astype(jnp.bfloat16)
    grad_down = outer_prod(hidden, cotangent)
    hidden_back = times_transposed(cotangent, wd_mat)
    gate_back = (hidden_back * upward * sigmoid_g * (1.0 + gate * (1.0 - sigmoid_g))).astype(
        jnp.bfloat16
    )
    up_back = (hidden_back * activated).astype(jnp.bfloat16)
    grad_gate = outer_prod(normed_two, gate_back)
    grad_up = outer_prod(normed_two, up_back)
    two_back = times_transposed(gate_back, wg_mat) + times_transposed(up_back, wu_mat)
    norm_two_back, gain_two = normalize_back(two_back, middle, rms_two, gain_f[1])
    mid_back = cotangent.astype(jnp.float32) + norm_two_back
    mid_low = mid_back.astype(jnp.bfloat16)
    grad_out = outer_prod(mixed, mid_low)
    mixed_back = times_transposed(mid_low, wo_mat).astype(jnp.bfloat16)
    feed_sum = GradSum(
        (grad_gate, grad_up, grad_down, grad_out), [shapes[at] for at in rest], devices
    )

    def back_of(head, field):
        part, total = attended[head]
        return attend_back(fields, field, part, total, head, group_size)

    mixed_back = feed_sum.core_stage(mixed_back)
    backs = [back_of(0, mixed_back)]
    mixed_back, _ = tied(mixed_back, backs[0])
    mixed_back = feed_sum.first_half_stage(mixed_back)
    backs.append(back_of(1, mixed_back))
    mixed_back, backs = feed_sum.second_half_stage((mixed_back, backs))
    backs.append(back_of(2, mixed_back))
    backs, output = feed_sum.line_stage((backs, output))
    input_grad, gain_one, *tiled = finish(tokens, norm_gains, wide_mat, cosine, sine, mid_back, backs)
    gains_back = jnp.concatenate([gain_one, gain_two[None]], 0)
    mix_sum = GradSum(tuple(tiled), shapes[:3], devices, gains_back)
    if feed_sum.stages:
        feed_sum.arrived = mix_sum.core_stage(feed_sum.arrived)
    input_grad = mix_sum.plane_stage(input_grad)
    input_grad = mix_sum.line_stage(input_grad)
    mix_parts = mix_sum.result()
    gate_part, up_part, down_part, out_part = feed_sum.result()
    all_parts = mix_parts[:3] + [out_part, gate_part, up_part, down_part]
    gain_grad = mix_parts[3]
    return (output, input_grad) + tuple(all_parts) + (gain_grad,)


def solution(mesh):
    return jax.shard_map(
        body,
        mesh=mesh,
        in_specs=(
            P("dp", None),
            P("dp", None),
            P("dp"),
            P("dp"),
            P("dp"),
            P("dp"),
            P("dp"),
            P("dp"),
            P("dp"),
            P(),
        ),
        out_specs=(
            P("dp", None),
            P("dp", None),
            P("dp"),
            P("dp"),
            P("dp"),
            P("dp"),
            P("dp"),
            P("dp"),
            P("dp"),
            P(),
        ),
        check_vma=False,
    )
```

```python
import functools

import jax
import jax.numpy as jnp
from jax import lax
from jax.experimental import pallas as pl
from jax.experimental.pallas import tpu as pltpu
from jax.sharding import PartitionSpec as P

HEADS = 9
KV_HEADS = 3
HEAD_DIM = 64
LENGTH = 1024


EPS = 1e-05
THETA = 100000.0
NEG_BIG = -1e30
LANES = 128
VMEM_LIMIT = 56 * 1024 * 1024
CORE_MASK = 1
LIGHT = pl.CostEstimate(flops=10**8, bytes_accessed=10**6, transcendentals=0)


def masks_of(devices):
    plane = tuple(2 * step for step in range(4))
    line = tuple(8 * step for step in range(devices // 8))
    return (plane, line)


def swap(field, mask, devices):
    return lax.ppermute(field, "dp", [(place, place ^ mask) for place in range(devices)])


def tree_sum(terms):
    while len(terms) > 1:
        odd = terms[len(terms) // 2 * 2 :]
        terms = [terms[at] + terms[at + 1] for at in range(0, len(terms) - 1, 2)] + odd
    return terms[0]


def widen(field):
    return field.astype(jnp.float32)


def slot_mask(core, slot, devices):
    line = devices // 8
    return core * CORE_MASK + 2 * (slot // line) + 8 * (slot % line)


def tiles_of(wide):
    return -(-wide // LANES)


def tile_widths(wide):
    return [min(LANES, wide - at) for at in range(0, wide, LANES)]


def flat_starts(shapes, devices):
    starts = [0]
    for rows, wide in shapes:
        starts.append(starts[-1] + rows * wide // (devices * LANES))
    return starts


def tiled_shapes(shapes):
    return [(tiles_of(wide), rows, LANES) for rows, wide in shapes if wide % LANES]


def unpack_kernel(place_ref, *refs, devices, shapes, joined, origins):
    count = len(origins)
    pieces, refs = refs[:count], refs[count:]
    out_count = 1 if joined else len(shapes)
    outs, flats, refs = refs[:out_count], refs[out_count : out_count + len(shapes)], refs[out_count + len(shapes) :]
    stage, landed, arrival, tiled_refs = refs[0], refs[1], refs[2], list(refs[3:])
    place = place_ref[0]
    starts = flat_starts(shapes, devices)
    block = pieces[0].shape[0]
    copies = [
        pltpu.make_async_copy(piece, landed.at[index], arrival.at[index])
        for index, piece in enumerate(pieces)
    ]
    for copy in copies:
        copy.start()
    for index, (core, plane, offset) in enumerate(origins):
        copies[index].wait()
        piece_ref = landed.at[index]
        cuts = []
        for flat, start, stop in zip(flats, starts, starts[1:]):
            low, high = max(start, offset), min(stop, offset + piece_ref.shape[1])
            if low < high:
                cuts.append((flat, stop - start, low - start, low - offset, high - offset))

        def load(slot, carry, core=core, plane=plane, piece_ref=piece_ref, cuts=cuts):
            owner = place ^ slot_mask(core, plane * block + slot, devices)
            piece = piece_ref[slot].astype(jnp.float32)
            if any(low % 8 for _, _, _, low, _ in cuts):
                stage[slot % 4] = piece
            for flat, each, inner, low, high in cuts:
                rows = stage[slot % 4, low:high, :] if low % 8 else piece[low:high]
                flat[pl.ds(owner * each + inner, high - low), :] = rows
            return carry

        lax.fori_loop(0, block, load, 0)
    column = 0
    for index, ((rows, wide), flat) in enumerate(zip(shapes, flats)):
        out = outs[0 if joined else index]
        whole = wide // LANES
        if wide % LANES == 0:
            for at in range(whole):
                tile = flat[pl.ds(at, rows, stride=whole), :]
                out[:, column + at * LANES : column + (at + 1) * LANES] = tile.astype(jnp.bfloat16)
        else:
            target = tiled_refs.pop(0)
            pairs, tiles_in = rows // 2, 2 * wide // LANES
            for at in range(whole + 1):
                target[at, pl.ds(0, pairs, stride=2), :] = flat[pl.ds(at, pairs, stride=tiles_in), :]
            rolled = None
            for at in range(whole, tiles_in):
                after = pltpu.roll(flat[pl.ds(at, pairs, stride=tiles_in), :], LANES // 2, 1)
                if rolled is not None:
                    lane = lax.broadcasted_iota(jnp.int32, after.shape, 1)
                    target[at - whole - 1, pl.ds(1, pairs, stride=2), :] = jnp.where(
                        lane < LANES // 2, rolled, after
                    )
                rolled = after
            target[whole, pl.ds(1, pairs, stride=2), :] = rolled
            for at, width in enumerate(tile_widths(wide)):
                tile = target[at]
                if joined and width < LANES:
                    lane = lax.broadcasted_iota(jnp.int32, tile.shape, 1)
                    tile = jnp.where(lane < width, tile, 0.0)
                    width = LANES
                start = column + at * LANES
                out[:, start : start + width] = tile[:, :width].astype(jnp.bfloat16)
        if joined:
            column += tiles_of(wide) * LANES


def unpack_pieces(place, pieces, origins, shapes, devices, joined):
    rows_in = pieces[0].shape[1]
    outs = shapes
    if joined:
        outs = [(shapes[0][0], sum(tiles_of(wide) for _, wide in shapes) * LANES)]
    return pl.pallas_call(
        functools.partial(
            unpack_kernel, devices=devices, shapes=shapes, joined=joined, origins=origins
        ),
        out_shape=[jax.ShapeDtypeStruct(shape, jnp.bfloat16) for shape in outs],
        in_specs=[pl.BlockSpec(memory_space=pltpu.SMEM)]
        + [pl.BlockSpec(memory_space=pl.ANY)] * len(pieces),
        out_specs=[pl.BlockSpec(memory_space=pltpu.VMEM)] * len(outs),
        scratch_shapes=[
            pltpu.VMEM((rows * wide // LANES, LANES), jnp.float32) for rows, wide in shapes
        ]
        + [
            pltpu.VMEM((4, rows_in, LANES), jnp.float32),
            pltpu.VMEM((len(pieces),) + pieces[0].shape, jnp.bfloat16),
            pltpu.SemaphoreType.DMA((len(pieces),)),
        ]
        + [pltpu.VMEM(shape, jnp.float32) for shape in tiled_shapes(shapes)],
        compiler_params=pltpu.CompilerParams(vmem_limit_bytes=VMEM_LIMIT),
        cost_estimate=LIGHT,
        name="unpack",
    )(place, *pieces)


def pack_kernel(place_ref, *refs, devices, shapes, tiled_in, extra):
    count = len(shapes) + (1 if extra else 0)
    sources, kept_ref, sent_ref, stage = refs[:count], refs[count], refs[count + 1], refs[count + 2]
    flats = refs[count + 3 : count + 3 + len(shapes)]
    tiled_refs = list(refs[count + 3 + len(shapes) :])
    place = place_ref[0]
    starts = flat_starts(shapes, devices)
    for index, ((rows, wide), flat) in enumerate(zip(shapes, flats)):
        source, whole = sources[index], wide // LANES
        if wide % LANES == 0:
            for at in range(whole):
                flat[pl.ds(at, rows, stride=whole), :] = (
                    source[at] if tiled_in[index] else source[:, at * LANES : (at + 1) * LANES]
                )
            continue
        if not tiled_in[index]:
            tiled = tiled_refs.pop(0)
            for at, width in enumerate(tile_widths(wide)):
                tiled[at, :, :width] = source[:, at * LANES : at * LANES + width]
            source = tiled
        pairs, tiles_in = rows // 2, 2 * wide // LANES
        for at in range(whole):
            flat[pl.ds(at, pairs, stride=tiles_in), :] = source[at, pl.ds(0, pairs, stride=2), :]
        before = source[whole, pl.ds(0, pairs, stride=2), :]
        lane = lax.broadcasted_iota(jnp.int32, before.shape, 1)
        for at in range(whole + 1):
            rolled = pltpu.roll(source[at, pl.ds(1, pairs, stride=2), :], LANES // 2, 1)
            flat[pl.ds(whole + at, pairs, stride=tiles_in), :] = jnp.where(
                lane < LANES // 2, before, rolled
            )
            before = rolled
    row_tiles = []
    if extra:
        row = jnp.concatenate([sources[-1][at : at + 1, :] for at in range(extra[0])], 1)
        row_tiles = [
            row[:, at * LANES : (at + 1) * LANES] for at in range(extra[0] * extra[1] // LANES)
        ]
    direct = not extra and all(start % 8 == 0 for start in starts)
    if not direct:
        for at in range(4):
            for index, tile in enumerate(row_tiles):
                stage[at, starts[-1] + index : starts[-1] + index + 1, :] = tile
            used = starts[-1] + len(row_tiles)
            if used < stage.shape[1]:
                stage[at, used:, :] = jnp.zeros((stage.shape[1] - used, LANES), jnp.float32)
    for core, pieces in enumerate((kept_ref, sent_ref)):

        def store(slot, carry, core=core, pieces=pieces):
            owner = place ^ slot_mask(core, slot, devices)
            parts = []
            for flat, start, stop in zip(flats, starts, starts[1:]):
                rows = flat[pl.ds(owner * (stop - start), stop - start), :]
                if direct:
                    parts.append(rows)
                else:
                    stage[slot % 4, start:stop, :] = rows
            spare = stage.shape[1] - starts[-1]
            if direct and spare:
                parts.append(jnp.zeros((spare, LANES), jnp.float32))
            piece = jnp.concatenate(parts, 0) if direct else stage[slot % 4]
            pieces[slot] = piece.astype(jnp.bfloat16)
            return carry

        lax.fori_loop(0, devices // 2, store, 0)


def pack_grads(place, grads, shapes, devices, extra):
    rows_out = sum(rows * wide for rows, wide in shapes) // (devices * LANES)
    sources = list(grads)
    if extra is not None:
        rows_out += extra.size // LANES
        sources.append(extra)
    rows_out = -(-rows_out // 16) * 16
    tiled_in = tuple(grad.ndim == 3 for grad in grads)
    half = jax.ShapeDtypeStruct((devices // 2, rows_out, LANES), jnp.bfloat16)
    untiled = [shape for shape, tiled in zip(shapes, tiled_in) if not tiled]
    return pl.pallas_call(
        functools.partial(
            pack_kernel, devices=devices, shapes=shapes, tiled_in=tiled_in,
            extra=None if extra is None else extra.shape,
        ),
        out_shape=[half, half],
        in_specs=[pl.BlockSpec(memory_space=pltpu.SMEM)]
        + [pl.BlockSpec(memory_space=pltpu.VMEM)] * len(sources),
        out_specs=[pl.BlockSpec(memory_space=pltpu.VMEM)] * 2,
        scratch_shapes=[pltpu.VMEM((4, rows_out, LANES), jnp.float32)]
        + [pltpu.VMEM((rows * wide // LANES, LANES), jnp.float32) for rows, wide in shapes]
        + [pltpu.VMEM(shape, jnp.float32) for shape in tiled_shapes(untiled)],
        compiler_params=pltpu.CompilerParams(vmem_limit_bytes=VMEM_LIMIT),
        cost_estimate=LIGHT,
        name="pack",
    )(place, *sources)


BLOCK = 256


def dot_nt(left, right):
    return lax.dot_general(
        left, right, (((1,), (1,)), ((), ())), preferred_element_type=jnp.float32
    )


def dot_tn(left, right):
    return lax.dot_general(
        left, right, (((0,), (0,)), ((), ())), preferred_element_type=jnp.float32
    )


def dot_nn(left, right):
    return jnp.dot(left, right, preferred_element_type=jnp.float32)


def key_columns(head):
    first = tiles_of(HEADS * HEAD_DIM) * LANES + head * HEAD_DIM
    return slice(first, first + HEAD_DIM)


def value_columns(head):
    first = (tiles_of(HEADS * HEAD_DIM) + tiles_of(KV_HEADS * HEAD_DIM)) * LANES + head * HEAD_DIM
    return slice(first, first + HEAD_DIM)


def attend_kernel(fields_ref, mixed_ref, total_ref, *, head, group):
    length = fields_ref.shape[0]
    keys = fields_ref[:, key_columns(head)]
    values = fields_ref[:, value_columns(head)]
    lower = lax.broadcasted_iota(jnp.int32, (BLOCK, BLOCK), 0) >= lax.broadcasted_iota(
        jnp.int32, (BLOCK, BLOCK), 1
    )
    lane = lax.broadcasted_iota(jnp.int32, (BLOCK, LANES), 1)
    for start in range(0, length, BLOCK):
        mixed, totals_row = [], jnp.zeros((BLOCK, LANES), jnp.float32)
        for member in range(group):
            at = (head * group + member) * HEAD_DIM
            query = fields_ref[start : start + BLOCK, at : at + HEAD_DIM]
            diagonal = jnp.where(lower, dot_nt(query, keys[start : start + BLOCK]), NEG_BIG)
            maxima = jnp.max(diagonal, 1, keepdims=True)
            if start:
                before = dot_nt(query, keys[:start])
                maxima = jnp.maximum(maxima, jnp.max(before, 1, keepdims=True))
            expo = jnp.exp(diagonal - maxima)
            totals = jnp.sum(expo, 1, keepdims=True)
            result = dot_nn(expo.astype(jnp.bfloat16), values[start : start + BLOCK])
            if start:
                expo = jnp.exp(before - maxima)
                totals = totals + jnp.sum(expo, 1, keepdims=True)
                result = result + dot_nn(expo.astype(jnp.bfloat16), values[:start])
            mixed.append(result / totals)
            totals_row = jnp.where(lane == member, maxima + jnp.log(totals), totals_row)
        mixed_ref[start : start + BLOCK, :] = jnp.concatenate(mixed, 1).astype(jnp.bfloat16)
        total_ref[start : start + BLOCK, :] = totals_row


def attend(fields, head, group):
    length = fields.shape[0]
    return pl.pallas_call(
        functools.partial(attend_kernel, head=head, group=group),
        out_shape=[
            jax.ShapeDtypeStruct((length, group * HEAD_DIM), jnp.bfloat16),
            jax.ShapeDtypeStruct((length, LANES), jnp.float32),
        ],
        in_specs=[pl.BlockSpec(memory_space=pltpu.VMEM)],
        out_specs=[pl.BlockSpec(memory_space=pltpu.VMEM)] * 2,
        compiler_params=pltpu.CompilerParams(vmem_limit_bytes=VMEM_LIMIT),
        cost_estimate=LIGHT,
        name="attend",
    )(fields)


def attend_back_kernel(
    fields_ref, back_ref, mixed_ref, total_ref,
    query_back_ref, key_back_ref, queries, backs, totals, deltas, query_sum, key_sum, value_sum,
    *, head, group,
):
    length = fields_ref.shape[0]
    ones = jnp.ones((8, HEAD_DIM), jnp.float32)
    totals[...] = total_ref[...].T[:8]
    for member in range(group):
        at = (head * group + member) * HEAD_DIM
        queries[member] = fields_ref[:, at : at + HEAD_DIM]
        back = back_ref[:, at : at + HEAD_DIM]
        backs[member] = back
        product = back.astype(jnp.float32) * mixed_ref[
            :, member * HEAD_DIM : (member + 1) * HEAD_DIM
        ].astype(jnp.float32)
        deltas[member] = lax.dot_general(
            ones, product, (((1,), (1,)), ((), ())),
            precision=lax.Precision.HIGHEST, preferred_element_type=jnp.float32,
        )
    keys_all = fields_ref[:, key_columns(head)]
    values_all = fields_ref[:, value_columns(head)]
    upper = lax.broadcasted_iota(jnp.int32, (BLOCK, BLOCK), 0) <= lax.broadcasted_iota(
        jnp.int32, (BLOCK, BLOCK), 1
    )
    for member in range(group):
        total_row = totals[member : member + 1, :]
        delta_row = deltas[member][0:1]
        for start in range(0, length, BLOCK):
            keys = keys_all[start : start + BLOCK]
            values = values_all[start : start + BLOCK]
            query = queries[member, start:, :]
            back = backs[member, start:, :]
            scores = dot_nt(keys, query)
            probs = jnp.exp(scores - total_row[:, start:])
            first = jnp.where(upper, probs[:, :BLOCK], 0.0)
            probs = first if start + BLOCK == length else jnp.concatenate(
                [first, probs[:, BLOCK:]], 1
            )
            prob_back = dot_nt(values, back)
            score_back = (probs * (prob_back - delta_row[:, start:])).astype(jnp.bfloat16)
            value_part = dot_nn(probs.astype(jnp.bfloat16), back)
            key_part = dot_nn(score_back, query)
            query_part = dot_tn(score_back, keys)
            if member:
                key_sum[start : start + BLOCK, :] += key_part
                value_sum[start : start + BLOCK, :] += value_part
            else:
                key_sum[start : start + BLOCK, :] = key_part
                value_sum[start : start + BLOCK, :] = value_part
            if start:
                query_sum[member, start:, :] += query_part
            else:
                query_sum[member] = query_part
    query_back_ref[...] = (
        jnp.concatenate([query_sum[member] for member in range(group)], 1) * HEAD_DIM ** (-0.5)
    )
    key_back_ref[...] = jnp.concatenate([key_sum[...], value_sum[...]], 1)


def attend_back(fields, back, mixed, total, head, group):
    length = fields.shape[0]
    return pl.pallas_call(
        functools.partial(attend_back_kernel, head=head, group=group),
        out_shape=[
            jax.ShapeDtypeStruct((length, group * HEAD_DIM), jnp.float32),
            jax.ShapeDtypeStruct((length, 2 * HEAD_DIM), jnp.float32),
        ],
        in_specs=[pl.BlockSpec(memory_space=pltpu.VMEM)] * 4,
        out_specs=[pl.BlockSpec(memory_space=pltpu.VMEM)] * 2,
        scratch_shapes=[
            pltpu.VMEM((group, length, HEAD_DIM), jnp.bfloat16),
            pltpu.VMEM((group, length, HEAD_DIM), jnp.bfloat16),
            pltpu.VMEM((8, length), jnp.float32),
            pltpu.VMEM((group, 8, length), jnp.float32),
            pltpu.VMEM((group, length, HEAD_DIM), jnp.float32),
            pltpu.VMEM((length, HEAD_DIM), jnp.float32),
            pltpu.VMEM((length, HEAD_DIM), jnp.float32),
        ],
        compiler_params=pltpu.CompilerParams(vmem_limit_bytes=VMEM_LIMIT),
        cost_estimate=LIGHT,
        name="attend_back",
    )(fields, back, mixed, total)


def partner_of(tile):
    lane = lax.broadcasted_iota(jnp.int32, tile.shape, 1)
    half = HEAD_DIM // 2
    return jnp.where(
        lane % HEAD_DIM < half, pltpu.roll(tile, LANES - half, 1), pltpu.roll(tile, half, 1)
    )


def first_gain(gains_ref):
    return gains_ref[...].astype(jnp.float32)[0:1]


def normed_rows(tokens_ref, gains_ref):
    resid = tokens_ref[...].astype(jnp.float32)
    inv_rms = lax.rsqrt(jnp.mean(resid * resid, 1, keepdims=True) + EPS)
    return resid, inv_rms, (resid * inv_rms * first_gain(gains_ref)).astype(jnp.bfloat16)


def project_kernel(
    tokens_in, cosine_in, sine_in, gains_ref, wide_ref, fields_ref,
    tokens_ref, cosine_ref, sine_ref, normed, arrival,
):
    copies = [
        pltpu.make_async_copy(source, target, arrival.at[at])
        for at, (source, target) in enumerate(
            ((tokens_in, tokens_ref), (cosine_in, cosine_ref), (sine_in, sine_ref))
        )
    ]
    for copy in copies:
        copy.start()
    for copy in copies:
        copy.wait()
    _, _, normed[...] = normed_rows(tokens_ref, gains_ref)
    first_key = tiles_of(HEADS * HEAD_DIM)
    first_value = first_key + tiles_of(KV_HEADS * HEAD_DIM)
    count = fields_ref.shape[1] // LANES
    for start in range(0, count, 2):
        stop = min(start + 2, count)
        pair = dot_nn(normed[...], wide_ref[:, start * LANES : stop * LANES])
        for at in range(start, stop):
            tile = pair[:, (at - start) * LANES : (at - start + 1) * LANES]
            if at < first_value:
                tile = tile * cosine_ref[...] - partner_of(tile) * sine_ref[...]
            tile = tile.astype(jnp.bfloat16)
            if at < first_key:
                tile = (tile.astype(jnp.float32) * HEAD_DIM ** (-0.5)).astype(jnp.bfloat16)
            fields_ref[:, at * LANES : (at + 1) * LANES] = tile


def vmem_call(kernel, out_shape, scratch_shapes, name, *args):
    single = not isinstance(out_shape, list)
    return pl.pallas_call(
        kernel,
        out_shape=out_shape,
        in_specs=[pl.BlockSpec(memory_space=pltpu.VMEM)] * len(args),
        out_specs=pl.BlockSpec(memory_space=pltpu.VMEM)
        if single
        else [pl.BlockSpec(memory_space=pltpu.VMEM)] * len(out_shape),
        scratch_shapes=scratch_shapes,
        compiler_params=pltpu.CompilerParams(vmem_limit_bytes=VMEM_LIMIT),
        cost_estimate=LIGHT,
        name=name,
    )(*args)


def project(tokens, gains, wide, cosine, sine):
    return pl.pallas_call(
        project_kernel,
        out_shape=jax.ShapeDtypeStruct((tokens.shape[0], wide.shape[1]), jnp.bfloat16),
        in_specs=[pl.BlockSpec(memory_space=pl.ANY)] * 3
        + [pl.BlockSpec(memory_space=pltpu.VMEM)] * 2,
        out_specs=pl.BlockSpec(memory_space=pltpu.VMEM),
        scratch_shapes=[
            pltpu.VMEM(tokens.shape, tokens.dtype),
            pltpu.VMEM(cosine.shape, cosine.dtype),
            pltpu.VMEM(sine.shape, sine.dtype),
            pltpu.VMEM(tokens.shape, jnp.bfloat16),
            pltpu.SemaphoreType.DMA((3,)),
        ],
        compiler_params=pltpu.CompilerParams(vmem_limit_bytes=VMEM_LIMIT),
        cost_estimate=LIGHT,
        name="project",
    )(tokens, cosine, sine, gains, wide)


def finish_kernel(
    tokens_ref, gains_ref, wide_ref, cosine_ref, sine_ref, mid_back_ref, *refs, heads
):
    backs = refs[: 2 * heads]
    input_grad_ref, gain_ref, *tiled_refs, fields, normed_t = refs[2 * heads :]
    places = [(ref, at) for ref in tiled_refs for at in range(ref.shape[0])]
    half = HEAD_DIM
    group = HEADS // heads
    wide_heads = [(backs[2 * (at // group)], at % group * half) for at in range(HEADS)]
    wide_heads += [None] * (HEADS % 2)
    for offset in (0, half):
        wide_heads += [(backs[2 * at + 1], offset) for at in range(heads)] + [None] * (heads % 2)
    turned = tiles_of(HEADS * HEAD_DIM) + tiles_of(heads * HEAD_DIM)
    for at in range(len(wide_heads) // 2):
        cols = []
        for item in wide_heads[2 * at : 2 * at + 2]:
            if item is None:
                cols.append(jnp.zeros((fields.shape[0], half), jnp.float32))
            else:
                cols.append(item[0][:, item[1] : item[1] + half])
        tile = jnp.concatenate(cols, 1)
        if at < turned:
            tile = tile * cosine_ref[...] + partner_of(tile) * sine_ref[...]
        fields[:, at * LANES : (at + 1) * LANES] = tile.astype(jnp.bfloat16)
    resid, inv_rms, normed = normed_rows(tokens_ref, gains_ref)
    normed_t[...] = normed.T
    count = fields.shape[1] // LANES
    for start in range(0, count, 2):
        stop = min(start + 2, count)
        pair = dot_nn(normed_t[...], fields[:, start * LANES : stop * LANES])
        for at in range(start, stop):
            ref, inner = places[at]
            ref[inner] = pair[:, (at - start) * LANES : (at - start + 1) * LANES]
    one_back = dot_nt(fields[...], wide_ref[...])
    weighted = one_back * first_gain(gains_ref)
    cubed = inv_rms * inv_rms * inv_rms
    scaled = resid * inv_rms
    gain_ref[...] = jnp.sum(one_back * scaled, 0, keepdims=True)
    mean = jnp.mean(weighted * resid, 1, keepdims=True)
    grad = mid_back_ref[...] + inv_rms * weighted - resid * (cubed * mean)
    input_grad_ref[...] = grad.astype(jnp.bfloat16)


def finish(tokens, gains, wide, cosine, sine, mid_back, backs):
    heads = len(backs)
    rows, width = tokens.shape
    return vmem_call(
        functools.partial(finish_kernel, heads=heads),
        [
            jax.ShapeDtypeStruct(tokens.shape, jnp.bfloat16),
            jax.ShapeDtypeStruct((1, width), jnp.float32),
        ]
        + [
            jax.ShapeDtypeStruct((tiles_of(count * HEAD_DIM), width, LANES), jnp.float32)
            for count in (HEADS, heads, heads)
        ],
        [
            pltpu.VMEM((rows, wide.shape[1]), jnp.bfloat16),
            pltpu.VMEM((width, rows), jnp.bfloat16),
        ],
        "finish",
        tokens, gains, wide, cosine, sine, mid_back, *[part for back in backs for part in back],
    )


def rotary_tables(length, head_dim):
    half_dim = head_dim // 2
    frequency = THETA ** (-(jnp.arange(half_dim, dtype=jnp.float32) * 2.0 / head_dim))
    angles = jnp.arange(length, dtype=jnp.float32)[:, None] * frequency[None, :]
    return (jnp.cos(angles), jnp.sin(angles))


def rotate_heads(field, cosine, sine):
    half_dim = field.shape[-1] // 2
    first_half = field[..., :half_dim]
    second_half = field[..., half_dim:]
    cosine = cosine[None, :, None, :]
    sine = sine[None, :, None, :]
    return jnp.concatenate(
        [first_half * cosine - second_half * sine, second_half * cosine + first_half * sine], -1
    )


def normalize(hidden, gain):
    inv_rms = lax.rsqrt(jnp.mean(hidden * hidden, -1, keepdims=True) + EPS)
    return (hidden * inv_rms * gain, inv_rms)


def normalize_back(grad, hidden, inv_rms, gain):
    weighted = grad * gain
    cubed = inv_rms * inv_rms * inv_rms
    hidden_grad = inv_rms * weighted - hidden * cubed * jnp.mean(
        weighted * hidden, -1, keepdims=True
    )
    gain_part = jnp.sum(grad * hidden * inv_rms, 0)
    return (hidden_grad, gain_part)


def outer_prod(left, right):
    return lax.dot_general(
        left, right, (((0,), (0,)), ((), ())), preferred_element_type=jnp.float32
    )


def times_transposed(left, matrix):
    return lax.dot_general(
        left, matrix, (((1,), (1,)), ((), ())), preferred_element_type=jnp.float32
    )


def whole_rows(shapes, devices):
    return (devices & (devices - 1)) == 0 and all(
        rows % (8 * devices // 4) == 0 and rows * wide % (devices * LANES) == 0
        for rows, wide in shapes
    )


def place_of():
    return lax.axis_index("dp").astype(jnp.int32).reshape(1)


class WeightGather:
    def __init__(self, shards, shapes, devices):
        self.shards, self.shapes, self.devices = shards, shapes, devices
        self.stages = whole_rows(shapes, devices)
        if self.stages:
            held = jnp.concatenate([shard.reshape(-1, LANES) for shard in shards])
            self.held = jnp.pad(held, ((0, -held.shape[0] % 16), (0, 0)))

    def line_stage(self, other):
        if not self.stages:
            return other
        _, line = masks_of(self.devices)
        self.held, other = tied(self.held, other)
        self.arrived = [self.held] + [swap(self.held, mask, self.devices) for mask in line[1:]]
        return other

    def plane_stage(self, other):
        if not self.stages:
            return other
        plane, _ = masks_of(self.devices)
        self.held, other = tied(jnp.stack(self.arrived), other)
        self.arrived = [self.held] + [swap(self.held, mask, self.devices) for mask in plane[1:]]
        self.origins = [(0, at, 0) for at in range(len(plane))]
        return other

    def first_half_stage(self, other):
        if not self.stages:
            return other
        plane, _ = masks_of(self.devices)
        cut = self.arrived[0].shape[0] // 2
        halves = [
            jnp.stack([field[at : at + cut] for field in self.arrived]) for at in (0, cut)
        ]
        halves, other = tied(halves, other)
        self.arrived = [
            [half, swap(half, mask, self.devices)] for half, mask in zip(halves, plane[1:3])
        ]
        return other

    def second_half_stage(self, other):
        if not self.stages:
            return other
        plane, _ = masks_of(self.devices)
        pairs, other = tied(self.arrived, other)
        cut = pairs[0][0].shape[1]
        self.arrived, self.origins = [], []
        for at, pair in enumerate(pairs):
            near, far = (1, 2) if at == 0 else (2, 1)
            self.arrived += pair + [swap(field, plane[far], self.devices) for field in pair]
            self.origins += [(0, where, at * cut) for where in (0, near, far, 3)]
        return other

    def core_stage(self, other, joined):
        if not self.stages:
            return other
        self.arrived, other = tied(self.arrived, other)
        if joined:
            self.arrived, self.origins = [jnp.concatenate(self.arrived)], [(0, 0, 0)]
        self.origins += [(1, where, offset) for _, where, offset in self.origins]
        self.got = [swap(field, CORE_MASK, self.devices) for field in self.arrived]
        return other

    def result(self, joined):
        if not self.stages:
            mats = [
                lax.all_gather(shard, "dp", axis=0, tiled=True).reshape(shape)
                for shard, shape in zip(self.shards, self.shapes)
            ]
            if not joined:
                return mats
            pads = [((0, 0), (0, tiles_of(mat.shape[1]) * LANES - mat.shape[1])) for mat in mats]
            return [jnp.concatenate([jnp.pad(mat, pad) for mat, pad in zip(mats, pads)], 1)]
        pieces = self.arrived + self.got
        return unpack_pieces(
            place_of(), pieces, tuple(self.origins), self.shapes, self.devices, joined
        )


def tied(first, second):
    return lax.optimization_barrier((first, second))


class GradSum:
    def __init__(self, grads, shapes, devices, extra=None):
        self.grads, self.shapes, self.devices, self.extra = grads, shapes, devices, extra
        self.stages = whole_rows(shapes, devices)
        if self.stages:
            self.kept, self.sent = pack_grads(place_of(), grads, shapes, devices, extra)

    def core_stage(self, other):
        if not self.stages:
            return other
        (self.kept, self.sent), other = tied((self.kept, self.sent), other)
        self.got = swap(self.sent, CORE_MASK, self.devices)
        return other

    def plane_stage(self, other):
        if not self.stages:
            return other
        plane, _ = masks_of(self.devices)
        block = self.kept.shape[0] // len(plane)
        cuts = [slice(at * block, (at + 1) * block) for at in range(len(plane))]
        parts = [(widen(self.kept[cut]) + widen(self.got[cut])).astype(jnp.bfloat16) for cut in cuts]
        self.parts, other = tied(parts, other)
        self.groups = [
            [self.parts[0]]
            + [swap(part, mask, self.devices) for part, mask in zip(self.parts[1:], plane[1:])]
        ]
        return other

    def first_half_stage(self, other):
        if not self.stages:
            return other
        plane, _ = masks_of(self.devices)
        block, cut = self.kept.shape[0] // len(plane), self.kept.shape[1] // 2
        parts = []
        for half in range(2):
            rows = slice(half * cut, (half + 1) * cut)
            cuts = [slice(at * block, (at + 1) * block) for at in range(len(plane))]
            parts.append(
                [
                    (widen(self.kept[at, rows]) + widen(self.got[at, rows])).astype(jnp.bfloat16)
                    for at in cuts
                ]
            )
        self.parts, other = tied(parts, other)
        self.arrived = [
            [swap(part[at], plane[near], self.devices) for at in (near, 3)]
            for part, near in zip(self.parts, (1, 2))
        ]
        return other

    def second_half_stage(self, other):
        if not self.stages:
            return other
        plane, _ = masks_of(self.devices)
        sends = [
            (widen(part[far]) + widen(arrived[1])).astype(jnp.bfloat16)
            for part, arrived, far in zip(self.parts, self.arrived, (2, 1))
        ]
        sends, other = tied(sends, other)
        self.groups = [
            [part[0], arrived[0], swap(send, plane[far], self.devices)]
            for part, arrived, send, far in zip(self.parts, self.arrived, sends, (2, 1))
        ]
        return other

    def line_stage(self, other):
        if not self.stages:
            return other
        _, line = masks_of(self.devices)
        parts = [
            jnp.concatenate(
                [
                    tree_sum([widen(term[at]) for term in terms]).astype(jnp.bfloat16)
                    for terms in self.groups
                ]
            )
            for at in range(len(line))
        ]
        self.parts, other = tied(parts, other)
        self.arrived = [
            swap(part, mask, self.devices) for part, mask in zip(self.parts[1:], line[1:])
        ]
        return other

    def result(self):
        if not self.stages:
            grads = [
                grad.swapaxes(0, 1).reshape(rows, -1)[:, :wide] if grad.ndim == 3 else grad
                for grad, (rows, wide) in zip(self.grads, self.shapes)
            ]
            sums = [
                lax.psum_scatter(grad.reshape(-1), "dp", scatter_dimension=0, tiled=True)
                for grad in grads
            ]
            return sums if self.extra is None else sums + [lax.psum(self.extra, "dp")]
        pieces = tree_sum([widen(term) for term in [self.parts[0]] + self.arrived])
        sums, start = [], 0
        for rows, wide in self.shapes:
            count = rows * wide // (self.devices * LANES)
            sums.append(pieces[start : start + count].reshape(-1))
            start += count
        if self.extra is not None:
            count = self.extra.size // LANES
            sums.append(pieces[start : start + count].reshape(self.extra.shape))
        return sums


def body(tokens, cotangent, w_query, w_key, w_value, w_out, w_gate, w_up, w_down, norm_gains):
    model_width = tokens.shape[1]
    seq_count = tokens.shape[0] // LENGTH
    group_size = HEADS // KV_HEADS
    scale_factor = HEAD_DIM ** (-0.5)
    gain_f = norm_gains.astype(jnp.float32)
    shards = (w_query, w_key, w_value, w_out, w_gate, w_up, w_down)
    devices = lax.axis_size("dp")
    widths = [shards[at].shape[0] * devices // model_width for at in range(6)]
    shapes = [(model_width, wide) for wide in widths] + [
        (shards[6].shape[0] * devices // model_width, model_width)
    ]
    first = WeightGather(shards[:3], shapes[:3], devices)
    rest = (4, 5, 6, 3)
    second = WeightGather(
        [shards[at] for at in rest], [shapes[at] for at in rest], devices
    )
    tokens = first.line_stage(tokens)
    if first.stages:
        first.arrived[1] = second.line_stage(first.arrived[1])
    tokens = first.plane_stage(tokens)
    tokens = first.core_stage(tokens, True)
    if first.stages:
        tokens = second.first_half_stage(tokens)
    (wide_mat,) = first.result(True)
    resid_in = tokens.astype(jnp.float32)
    cosine, sine = rotary_tables(LENGTH, HEAD_DIM)
    pairs = LANES // HEAD_DIM
    cosine = jnp.tile(cosine, (seq_count, 2 * pairs))
    sine = jnp.tile(jnp.concatenate([sine, -sine], 1), (seq_count, pairs))
    fields = project(tokens, norm_gains, wide_mat, cosine, sine)
    fields = second.second_half_stage(fields)
    attended = [attend(fields, head, group_size) for head in range(2)]
    fields, attended = second.core_stage((fields, attended), False)
    attended.append(attend(fields, 2, group_size))
    wg_mat, wu_mat, wd_mat, wo_mat = second.result(False)
    mixed = jnp.concatenate([part for part, _ in attended], 1)
    attn_out = jnp.dot(mixed, wo_mat, preferred_element_type=jnp.float32)
    middle = resid_in + attn_out
    normed_two, rms_two = normalize(middle, gain_f[1])
    normed_two = normed_two.astype(jnp.bfloat16)
    gate = jnp.dot(normed_two, wg_mat, preferred_element_type=jnp.float32)
    upward = jnp.dot(normed_two, wu_mat, preferred_element_type=jnp.float32)
    sigmoid_g = jax.nn.sigmoid(gate)
    activated = gate * sigmoid_g
    hidden = (activated * upward).astype(jnp.bfloat16)
    ffn_out = jnp.dot(hidden, wd_mat, preferred_element_type=jnp.float32)
    output = (middle + ffn_out).astype(jnp.bfloat16)
    grad_down = outer_prod(hidden, cotangent)
    hidden_back = times_transposed(cotangent, wd_mat)
    gate_back = (hidden_back * upward * sigmoid_g * (1.0 + gate * (1.0 - sigmoid_g))).astype(
        jnp.bfloat16
    )
    up_back = (hidden_back * activated).astype(jnp.bfloat16)
    grad_gate = outer_prod(normed_two, gate_back)
    grad_up = outer_prod(normed_two, up_back)
    two_back = times_transposed(gate_back, wg_mat) + times_transposed(up_back, wu_mat)
    norm_two_back, gain_two = normalize_back(two_back, middle, rms_two, gain_f[1])
    mid_back = cotangent.astype(jnp.float32) + norm_two_back
    mid_low = mid_back.astype(jnp.bfloat16)
    grad_out = outer_prod(mixed, mid_low)
    mixed_back = times_transposed(mid_low, wo_mat).astype(jnp.bfloat16)
    feed_sum = GradSum(
        (grad_gate, grad_up, grad_down, grad_out), [shapes[at] for at in rest], devices
    )

    def back_of(head, field):
        part, total = attended[head]
        return attend_back(fields, field, part, total, head, group_size)

    mixed_back = feed_sum.core_stage(mixed_back)
    backs = [back_of(0, mixed_back)]
    mixed_back, _ = tied(mixed_back, backs[0])
    mixed_back = feed_sum.first_half_stage(mixed_back)
    backs.append(back_of(1, mixed_back))
    mixed_back, backs = feed_sum.second_half_stage((mixed_back, backs))
    backs.append(back_of(2, mixed_back))
    backs, output = feed_sum.line_stage((backs, output))
    input_grad, gain_one, *tiled = finish(tokens, norm_gains, wide_mat, cosine, sine, mid_back, backs)
    gains_back = jnp.concatenate([gain_one, gain_two[None]], 0)
    mix_sum = GradSum(tuple(tiled), shapes[:3], devices, gains_back)
    if feed_sum.stages:
        feed_sum.arrived = mix_sum.core_stage(feed_sum.arrived)
    input_grad = mix_sum.plane_stage(input_grad)
    input_grad = mix_sum.line_stage(input_grad)
    mix_parts = mix_sum.result()
    gate_part, up_part, down_part, out_part = feed_sum.result()
    all_parts = mix_parts[:3] + [out_part, gate_part, up_part, down_part]
    gain_grad = mix_parts[3]
    return (output, input_grad) + tuple(all_parts) + (gain_grad,)


def solution(mesh):
    return jax.shard_map(
        body,
        mesh=mesh,
        in_specs=(
            P("dp", None),
            P("dp", None),
            P("dp"),
            P("dp"),
            P("dp"),
            P("dp"),
            P("dp"),
            P("dp"),
            P("dp"),
            P(),
        ),
        out_specs=(
            P("dp", None),
            P("dp", None),
            P("dp"),
            P("dp"),
            P("dp"),
            P("dp"),
            P("dp"),
            P("dp"),
            P("dp"),
            P(),
        ),
        check_vma=False,
    )
```
